32 devices in a mesh: depth: 2 (over y), lat: 16 (over z, x, core).
Axes of the slice: x: 2, y: 2, z: 4, core: 2. Of those that a mesh axis runs over, the one named last changes fastest.
Arguments:
- source_field: bfloat16 [2, 2, 128, 2048], P(None, None, 'lat'), may hold values from -6 to 6
- receiver_field: bfloat16 [2, 2, 128, 2048], P(None, None, 'lat'), may hold values from -6 to 6
- freq_index: int32 [2], replicated, may hold values from 0 to 63
- slowness: float32 [2, 128, 2048], P('depth', 'lat'), may hold values from 0.5 to 2
- ffd_coef: float32 [2, 128, 2048], P('depth', 'lat'), may hold values from 0.04 to 0.12
- band: bfloat16 [16, 3, 128, 128], P('depth'), may hold values from -0.3125 to 0.3125
- image_mask: int32 [2, 128, 2048], P('depth', 'lat'), may hold values 0 or 1
Outputs:
- image: float32 [2, 128, 2048], P('depth', 'lat')
- gradient: float32 [2, 128, 2048], P('depth', 'lat')
The draws below stay inside these ranges and needn't reach their ends.
All inputs are finite; a program needn't handle non-finite values. No bound on the sum of `image_mask` on one device may be relied on, other than what follows from the above.
Results may differ from the reference program's by a relative error of at most 0.0035.
The reference program's roundings to bfloat16 on the way count: a program that leaves them out, or rounds other values in their place, can miss the bound.
Values may be sent and summed in bfloat16 or wider, within the bound.
A program may use at most 64 MiB of HBM per device.

```python
import math
import jax
import jax.numpy as jnp
from jax import lax

LD = 1
NY = 2048
BLOCK = 128
HALO = 8
NFREQ = 64
NX = 128
NF = 2
L = 2
NBLK = 16


def touch_ends(values, stream_key, low, top_value):
    longest = values.shape.index(max(values.shape))
    spots = []
    for shift in (0, 1):
        where = [jax.random.randint(jax.random.fold_in(stream_key, axis), (), 0, length) for axis, length in enumerate(values.shape)]
        where[longest] = (where[longest] + shift) % values.shape[longest]
        spots.append(tuple(where))
    return values.at[spots[0]].set(low).at[spots[1]].set(top_value)


def steps_of(rng, dims, shards, low, largest):
    def one(position, parts):
        heights = jax.random.uniform(jax.random.fold_in(jax.random.fold_in(rng, 6), position), (parts,), jnp.float32, low / len(shards), largest / len(shards))
        return jnp.repeat(jnp.exp(heights), dims[position] // parts).reshape((-1,) + (1,) * (len(dims) - position - 1))

    gain = one(*shards[0])
    for cut in shards[1:]:
        gain = gain * one(*cut)
    return gain


def bell_draw(stream_key, shape, scale, limit, cuts=(), kind=jnp.bfloat16):
    entries = jax.random.normal(stream_key, shape, jnp.float32) * scale
    if len(cuts) > 0:
        entries = steps_of(stream_key, shape, cuts, -0.22, 0.18) * entries
    return jnp.clip(entries, min=-limit, max=limit).astype(kind)


def setup_inputs(seed: int = 0) -> dict:
    arg_keys = jax.random.split(jax.random.key(seed), 8)
    return {
        "source_field": bell_draw(arg_keys[0], (NF, 2, NX, NY), 1.0, 6.0, ((2, 16),)),
        "receiver_field": bell_draw(arg_keys[1], (NF, 2, NX, NY), 1.0, 6.0, ((2, 16),)),
        "freq_index": jax.random.randint(arg_keys[2], (NF,), 0, NFREQ).astype(jnp.int32),
        "slowness": jnp.clip(jnp.exp(math.log(2.0) - 1.3862944 * jax.random.uniform(arg_keys[3], (L, NX, NY), jnp.float32) ** steps_of(arg_keys[3], (L, NX, NY), ((0, 2), (1, 16)), -0.2, 0.2)), 0.5, 2.0),
        "ffd_coef": jnp.clip(jnp.exp(math.log(0.12) - 1.0986123 * jax.random.uniform(arg_keys[4], (L, NX, NY), jnp.float32) ** steps_of(arg_keys[4], (L, NX, NY), ((0, 2), (1, 16)), -0.2, 0.2)), 0.04, 0.12),
        "band": bell_draw(arg_keys[5], (NBLK, 3, BLOCK, BLOCK), (3 * BLOCK) ** -0.5, 0.3125, ((0, 2),)),
        "image_mask": touch_ends((jax.random.randint(arg_keys[6], (L, NX, NY), 0, 4) < 3).astype(jnp.int32), jax.random.fold_in(arg_keys[6], 1), 0, 1),
    }


def roundtrip(values):
    return lax.optimization_barrier(values.astype(jnp.bfloat16)).astype(jnp.float32)


def stencil_full(field):
    rows = field.shape[-2]
    axis = field.ndim - 2
    widths = [(0, 0)] * field.ndim
    widths[axis] = (HALO, HALO)
    padded = jnp.pad(field, widths)
    total = jnp.zeros_like(field)
    for offset in range(1, HALO + 1):
        upper = lax.slice_in_dim(padded, HALO + offset, HALO + offset + rows, axis=axis)
        lower = lax.slice_in_dim(padded, HALO - offset, HALO - offset + rows, axis=axis)
        total = total + (0.25 / offset) * (upper + lower - 2.0 * field)
    return total


def band_full(field, band32):
    comps, rows, width = field.shape
    nblocks = band32.shape[0]
    block = band32.shape[2]
    tiles = field.reshape(comps, rows, nblocks, block)
    padded = jnp.pad(tiles, ((0, 0), (0, 0), (1, 1), (0, 0)))
    total = jnp.zeros(tiles.shape, jnp.float32)
    for offset in range(3):
        window = lax.slice_in_dim(padded, offset, offset + nblocks, axis=2)
        total = total + jnp.einsum("acjb,jbd->acjd", window, band32[:, offset], precision=lax.Precision.HIGHEST)
    return total.reshape(comps, rows, width)


def band_full_t(field, band32):
    comps, rows, width = field.shape
    nblocks = band32.shape[0]
    block = band32.shape[2]
    tiles = field.reshape(comps, rows, nblocks, block)
    total = jnp.zeros(tiles.shape, jnp.float32)
    for offset in range(3):
        moved = jnp.einsum("acjd,jbd->acjb", tiles, band32[:, offset], precision=lax.Precision.HIGHEST)
        padded = jnp.pad(moved, ((0, 0), (0, 0), (1, 1), (0, 0)))
        total = total + lax.slice_in_dim(padded, 2 - offset, 2 - offset + nblocks, axis=2)
    return total.reshape(comps, rows, width)


def level_step(field, omega, slow, coef, band32):
    theta = omega * slow
    cosine = jnp.cos(theta)
    sine_part = jnp.sin(theta)
    phased = jnp.stack([field[0] * cosine - field[1] * sine_part, field[0] * sine_part + field[1] * cosine])
    rounded = roundtrip(phased)
    lateral = band_full(rounded, band32) + stencil_full(rounded)
    return phased, jnp.stack([phased[0] - coef * lateral[1], phased[1] + coef * lateral[0]])


def adjoint_step(adjoint, phased, omega, slow, coef, band32):
    scaled = roundtrip(coef * adjoint)
    lateral = band_full_t(scaled, band32) + stencil_full(scaled)
    back_re = adjoint[0] + lateral[1]
    back_im = adjoint[1] - lateral[0]
    term = omega * (back_im * phased[0] - back_re * phased[1])
    theta = omega * slow
    cosine = jnp.cos(theta)
    sine_part = jnp.sin(theta)
    upward = jnp.stack([back_re * cosine + back_im * sine_part, back_im * cosine - back_re * sine_part])
    return term, upward


def reference(source_field, receiver_field, freq_index, slowness, ffd_coef, band, image_mask):
    levels = slowness.shape[0]
    count = freq_index.shape[0]
    omegas = 0.1 * (freq_index.astype(jnp.float32) + 1.0)
    level_ids = jnp.arange(levels, dtype=jnp.int32)
    band32 = band.astype(jnp.float32)

    def march(source, receiver, omega):
        def down(carry, inputs):
            field_s, field_q = carry
            slow, coef, level = inputs
            unused, new_s = level_step(field_s, omega, slow, coef, band32)
            phased_q, new_q = level_step(field_q, omega, slow, coef, band32)
            product = jnp.sum(new_s * new_q, axis=0)
            boundary = (level + 1) % LD == 0
            next_s = jnp.where(boundary, roundtrip(new_s), new_s)
            next_q = jnp.where(boundary, roundtrip(new_q), new_q)
            return (next_s, next_q), (product, new_s, phased_q)

        start = (source.astype(jnp.float32), receiver.astype(jnp.float32))
        final, outputs = lax.scan(down, start, (slowness, ffd_coef, level_ids))
        return outputs

    def image_part(total, inputs):
        products, states, phases = march(inputs[0], inputs[1], inputs[2])
        return total + products, None

    zero_levels = jnp.zeros(slowness.shape, jnp.float32)
    summed, unused = lax.scan(image_part, zero_levels, (source_field, receiver_field, omegas))
    image = summed / count
    masked = image_mask.astype(jnp.float32) * image

    def gradient_part(total, inputs):
        omega = inputs[2]
        products, states, phases = march(inputs[0], inputs[1], omega)

        def up(adjoint, items):
            slow, coef, weight, state, phased, level = items
            adjoint = adjoint + weight * state
            term, upward = adjoint_step(adjoint, phased, omega, slow, coef, band32)
            upward = jnp.where(level % LD == 0, roundtrip(upward), upward)
            return upward, term

        start = jnp.zeros(source_field.shape[1:], jnp.float32)
        final, terms = lax.scan(up, start, (slowness, ffd_coef, masked, states, phases, level_ids), reverse=True)
        return total + terms, None

    summed_grad, unused = lax.scan(gradient_part, zero_levels, (source_field, receiver_field, omegas))
    return image, summed_grad / count
```

```python
import functools

import jax
import jax.numpy as jnp
from jax import lax
from jax.experimental import pallas as pl
from jax.experimental.pallas import tpu as pltpu
from jax.sharding import PartitionSpec as P

HALO = 8
F32 = jnp.float32
BF16 = jnp.bfloat16
WEIGHTS = [0.0] + [0.25 / k for k in range(1, HALO + 1)]
UP, DOWN, LEFT, RIGHT = range(4)


def sincos(theta):
    turns = jnp.floor(theta * 0.6366197723675814 + 0.5)
    rest = theta - turns * 1.5703125
    rest = rest - turns * 4.837512969970703125e-4
    rest = rest - turns * 7.54978995489188216e-8
    square = rest * rest
    sine = rest + rest * square * (
        -1.6666654611e-1 + square * (8.3321608736e-3 + square * -1.9515295891e-4)
    )
    cosine = (
        1.0
        - 0.5 * square
        + square
        * square
        * (
            4.166664568298827e-2
            + square * (-1.388731625493765e-3 + square * 2.443315711809948e-5)
        )
    )
    quadrant = turns.astype(jnp.int32)
    odd = (quadrant & 1) == 1
    sin_out = jnp.where(odd, cosine, sine)
    cos_out = jnp.where(odd, sine, cosine)
    sin_out = jnp.where((quadrant & 2) == 2, -sin_out, sin_out)
    cos_out = jnp.where(((quadrant + 1) & 2) == 2, -cos_out, cos_out)
    return sin_out, cos_out


def stencil(cur, prev, nxt):
    row = lax.broadcasted_iota(jnp.int32, cur.shape, 0)
    total = WEIGHTS[HALO] * (prev + nxt) - 2.0 * sum(WEIGHTS) * cur
    for k in range(1, HALO):
        inside = row >= k
        near = jnp.where(inside, WEIGHTS[k], WEIGHTS[HALO - k])
        far = jnp.where(inside, WEIGHTS[HALO - k], WEIGHTS[k])
        mixed = near * cur + far * jnp.where(inside, prev, nxt)
        total = total + pltpu.roll(mixed, HALO - k, 0)
    return total


def loop(count, body):
    if count <= 2:
        for i in range(count):
            body(i)
    else:
        lax.fori_loop(0, count, lambda i, c: (body(i), c)[1], 0)


def kernel(
    dims,
    freq_ref,
    src_ref,
    rcv_ref,
    slow_ref,
    coef_ref,
    mask_ref,
    band_ref,
    image_ref,
    grad_ref,
    fields,
    slow,
    coef,
    mask,
    band,
    band_t,
    band_edge,
    sines,
    cosines,
    phased,
    state,
    adj,
    hbuf,
    hlat,
    gbuf,
    glat,
    qbuf,
    img,
    grad,
    fsend,
    frecv,
    bsend,
    brecv,
    rsend,
    rrecv,
    esend,
    erecv,
    osend,
    orecv,
    own_sem,
    loc_sem,
):
    D, LATS, L, layers, NF, C, nb, B, W = dims
    NFC = NF // C
    me = lax.axis_index("depth")
    lat = lax.axis_index("lat")
    first = pl.multiple_of(me * W, B)
    mine = pl.ds(first, W)
    exists = {UP: lat > 0, DOWN: lat < LATS - 1, LEFT: me > 0, RIGHT: me < D - 1}
    target = {
        UP: {"lat": lat - 1},
        DOWN: {"lat": lat + 1},
        LEFT: {"depth": me - 1},
        RIGHT: {"depth": me + 1},
    }
    opposite = {UP: DOWN, DOWN: UP, LEFT: RIGHT, RIGHT: LEFT}
    DIRS = (UP, DOWN, LEFT, RIGHT)
    MESH = pl.DeviceIdType.MESH

    own_levels = pl.ds(me * layers, layers)
    local = [
        pltpu.make_async_copy(slow_ref.at[:, :, mine], slow.at[own_levels], loc_sem.at[0]),
        pltpu.make_async_copy(src_ref.at[:, :, :, mine], fields.at[0], loc_sem.at[1]),
        pltpu.make_async_copy(rcv_ref.at[:, :, :, mine], fields.at[1], loc_sem.at[2]),
        pltpu.make_async_copy(band_ref, band, loc_sem.at[3]),
        pltpu.make_async_copy(coef_ref.at[:, :, mine], coef.at[own_levels], loc_sem.at[4]),
        pltpu.make_async_copy(mask_ref.at[:, :, mine], mask.at[own_levels], loc_sem.at[5]),
    ]
    for copy in local:
        copy.start()

    barrier = pltpu.get_barrier_semaphore()
    for way in (UP, DOWN):

        @pl.when(exists[way])
        def _():
            pl.semaphore_signal(barrier, inc=1, device_id=target[way], device_id_type=MESH)

    for s in range(1, D):
        pl.semaphore_signal(
            barrier, inc=1, device_id={"depth": lax.rem(me + s, D)}, device_id_type=MESH
        )
    pl.semaphore_wait(
        barrier, (D - 1) + exists[UP].astype(jnp.int32) + exists[DOWN].astype(jnp.int32)
    )

    tables = ((slow_ref, slow), (coef_ref, coef), (mask_ref, mask))

    def table_copy(a, s):
        peer = lax.rem(me + s, D)
        return pltpu.make_async_remote_copy(
            src_ref=tables[a][0].at[:, :, pl.ds(pl.multiple_of(peer * W, B), W)],
            dst_ref=tables[a][1].at[own_levels],
            send_sem=rsend.at[a, s],
            recv_sem=rrecv.at[a, s],
            device_id={"depth": peer},
            device_id_type=MESH,
        )

    def table_wait(a, s):
        source = lax.rem(me - s + D, D)
        pltpu.make_async_remote_copy(
            src_ref=tables[a][1].at[pl.ds(source * layers, layers)],
            dst_ref=tables[a][1].at[pl.ds(source * layers, layers)],
            send_sem=rsend.at[a, s],
            recv_sem=rrecv.at[a, s],
            device_id={"depth": source},
            device_id_type=MESH,
        ).wait_recv()

    def edge_copy(way):
        j, k, slot = (0, 0, 1) if way == LEFT else (nb - 1, 2, 0)
        return pltpu.make_async_remote_copy(
            src_ref=band_ref.at[j, k],
            dst_ref=band_edge.at[slot],
            send_sem=esend.at[slot],
            recv_sem=erecv.at[slot],
            device_id=target[way],
            device_id_type=MESH,
        )

    for a in (0, 1):
        for s in range(1, D):
            table_copy(a, s).start()

    def late_sends():
        for s in range(1, D):
            table_copy(2, s).start()
        for way in (LEFT, RIGHT):

            @pl.when(exists[way])
            def _():
                edge_copy(way).start()

    def halo_copy(buf, lats, ssem, rsem, l, c, way):
        if way in (UP, DOWN):
            src = buf.at[l, c, :, pl.ds(B, W)]
            dst = lats.at[l, c, opposite[way]]
        else:
            src = buf.at[l, c, :, pl.ds(B if way == LEFT else W, B)]
            dst = buf.at[l, c, :, pl.ds(W + B if way == LEFT else 0, B)]
        return pltpu.make_async_remote_copy(
            src_ref=src,
            dst_ref=dst,
            send_sem=ssem.at[l, c, way],
            recv_sem=rsem.at[l, c, opposite[way]],
            device_id=target[way],
            device_id_type=MESH,
        )

    def send_halo(args, l, c):
        for way in DIRS:

            @pl.when(exists[way])
            def _():
                halo_copy(*args, l, c, way).start()

    def wait_halo(args, l, c, ways):
        for way in ways:

            @pl.when(exists[way])
            def _():
                halo_copy(*args, l, c, opposite[way]).wait_recv()

    forward = (hbuf, hlat, fsend, frecv)
    backward = (gbuf, glat, bsend, brecv)

    for way in (UP, DOWN):

        @pl.when(jnp.logical_not(exists[way]))
        def _():
            hlat[:, :, way] = jnp.zeros(hlat.shape[:2] + hlat.shape[3:], BF16)
            glat[:, :, way] = jnp.zeros(glat.shape[:2] + glat.shape[3:], BF16)

    for way, start, slot in ((LEFT, 0, 0), (RIGHT, W + B, 1)):

        @pl.when(jnp.logical_not(exists[way]))
        def _():
            hbuf[:, :, :, start : start + B] = jnp.zeros(hbuf.shape[:3] + (B,), BF16)
            gbuf[:, :, :, start : start + B] = jnp.zeros(gbuf.shape[:3] + (B,), BF16)
            band_edge[slot] = jnp.zeros((B, B), BF16)

    CW = min(W, 512)
    pieces = [slice(x, x + CW) for x in range(0, W, CW)]

    def omega_of(f):
        return 0.1 * (freq_ref[f].astype(F32) + 1.0)

    def angles(l):
        def one(f):
            omega = omega_of(f)
            for cols in pieces:
                sines[l, f, :, cols], cosines[l, f, :, cols] = sincos(omega * slow[l, :, cols])

        loop(NF, one)

    def store_phase(l, c, fi, s, cols, re, im):
        f = c * NFC + fi
        cosine, sine = cosines[l, f, :, cols], sines[l, f, :, cols]
        phase_re = re * cosine - im * sine
        phase_im = re * sine + im * cosine
        phased[l, f, s, 0, :, cols] = phase_re
        phased[l, f, s, 1, :, cols] = phase_im
        rows = pl.ds(pl.multiple_of((fi * 2 + s) * 16, 16), 16)
        inner = slice(cols.start + B, cols.stop + B)
        hbuf[l, c, rows, inner] = jnp.concatenate([phase_re, phase_im], axis=0).astype(BF16)

    def first_phase(c):
        def one(fi):
            f = c * NFC + fi
            for s in range(2):
                for cols in pieces:
                    re = fields[s, f, 0, :, cols].astype(F32)
                    im = fields[s, f, 1, :, cols].astype(F32)
                    store_phase(0, c, fi, s, cols, re, im)

        loop(NFC, one)

    def band_blocks(buf, matrix, l, c, blocks, rows):
        for j in blocks:
            qbuf[c, :rows, j * B : (j + 1) * B] = jnp.dot(
                buf[l, c, :, j * B : (j + 3) * B],
                matrix[j].reshape(3 * B, B),
                preferred_element_type=F32,
            )

    inner_blocks = range(1, nb - 1)
    outer_blocks = sorted({0, nb - 1})

    def lateral(buf, lats, l, c, row, cols):
        rows = pl.ds(pl.multiple_of(row, 16), 16)
        cur = buf[l, c, rows, cols.start + B : cols.stop + B].astype(F32)
        prev = lats[l, c, UP, rows, cols].astype(F32)
        nxt = lats[l, c, DOWN, rows, cols].astype(F32)
        product = qbuf[c, rows, cols]
        return [
            product[h] + stencil(cur[h], prev[h], nxt[h]) for h in (slice(0, 8), slice(8, 16))
        ]

    R, RB = NFC * 32, NFC * 16

    def forward_finish(l, c):
        wait_halo(forward, l, c, (LEFT, RIGHT))
        band_blocks(hbuf, band, l, c, outer_blocks, R)
        wait_halo(forward, l, c, (UP, DOWN))

        def one(fi):
            f = c * NFC + fi
            for cols in pieces:
                coefs = coef[l, :, cols]
                new = []
                for s in range(2):
                    q_re, q_im = lateral(hbuf, hlat, l, c, (fi * 2 + s) * 16, cols)
                    re = phased[l, f, s, 0, :, cols] - coefs * q_im
                    im = phased[l, f, s, 1, :, cols] + coefs * q_re
                    new.append((re, im))
                    if l + 1 < L:
                        store_phase(
                            l + 1,
                            c,
                            fi,
                            s,
                            cols,
                            re.astype(BF16).astype(F32),
                            im.astype(BF16).astype(F32),
                        )
                state[l, f, 0, :, cols] = new[0][0]
                state[l, f, 1, :, cols] = new[0][1]
                product = new[0][0] * new[1][0] + new[0][1] * new[1][1]
                if c == 0 and isinstance(fi, int) and fi == 0:
                    img[l, :, cols] = product
                else:
                    img[l, :, cols] += product

        if NFC > 2 and c == 0:
            img[l] = jnp.zeros(img.shape[1:], F32)
        loop(NFC, one)
        if c == C - 1:
            img[l] = img[l] * (1.0 / NF)

    results = ((img, image_ref), (grad, grad_ref))

    def own_copy(a, l):
        return pltpu.make_async_copy(
            results[a][0].at[l], results[a][1].at[l % layers, :, mine], own_sem.at[a, l % layers]
        )

    def out_copy(a, l):
        owner = l // layers
        return pltpu.make_async_remote_copy(
            src_ref=results[a][0].at[l],
            dst_ref=results[a][1].at[l % layers, :, mine],
            send_sem=osend.at[a, l],
            recv_sem=orecv.at[a, l % layers, lax.rem(owner - me + D, D)],
            device_id={"depth": owner},
            device_id_type=MESH,
        )

    def deliver(a, l):
        @pl.when(me == l // layers)
        def _():
            own_copy(a, l).start()

        @pl.when(me != l // layers)
        def _():
            out_copy(a, l).start()

    def begin_adjoint(l, c, fi, cols, mu):
        f = c * NFC + fi
        weight = mask[l, :, cols].astype(F32) * img[l, :, cols]
        coefs = coef[l, :, cols]
        scaled = []
        for part in range(2):
            value = weight * state[l, f, part, :, cols]
            if mu is not None:
                value = value + mu[part]
            adj[f, part, :, cols] = value
            scaled.append(coefs * value)
        rows = pl.ds(pl.multiple_of(fi * 16, 16), 16)
        gbuf[l, c, rows, cols.start + B : cols.stop + B] = jnp.concatenate(
            scaled, axis=0
        ).astype(BF16)

    def first_adjoint(c):
        def one(fi):
            for cols in pieces:
                begin_adjoint(L - 1, c, fi, cols, None)

        loop(NFC, one)

    def backward_finish(l, c):
        wait_halo(backward, l, c, (LEFT, RIGHT))
        band_blocks(gbuf, band_t, l, c, outer_blocks, RB)
        wait_halo(backward, l, c, (UP, DOWN))

        def one(fi):
            f = c * NFC + fi
            omega = omega_of(f)
            for cols in pieces:
                t_re, t_im = lateral(gbuf, glat, l, c, fi * 16, cols)
                back_re = adj[f, 0, :, cols] + t_im
                back_im = adj[f, 1, :, cols] - t_re
                term = omega * (
                    back_im * phased[l, f, 1, 0, :, cols] - back_re * phased[l, f, 1, 1, :, cols]
                )
                if c == 0 and isinstance(fi, int) and fi == 0:
                    grad[l, :, cols] = term
                else:
                    grad[l, :, cols] += term
                if l > 0:
                    cosine, sine = cosines[l, f, :, cols], sines[l, f, :, cols]
                    mu_re = back_re * cosine + back_im * sine
                    mu_im = back_im * cosine - back_re * sine
                    mu = [mu_re.astype(BF16).astype(F32), mu_im.astype(BF16).astype(F32)]
                    begin_adjoint(l - 1, c, fi, cols, mu)

        if NFC > 2 and c == 0:
            grad[l] = jnp.zeros(grad.shape[1:], F32)
        loop(NFC, one)
        if c == C - 1:
            grad[l] = grad[l] * (1.0 / NF)

    def arrive(a, l):
        if l % layers == 0:
            s = lax.rem(me - l // layers + D, D)

            @pl.when(s != 0)
            def _():
                table_wait(a, s)

    local[0].wait()
    arrive(0, 0)
    angles(0)
    local[1].wait()
    local[2].wait()
    for c in range(C):
        first_phase(c)
        send_halo(forward, 0, c)
    late_sends()
    local[3].wait()
    for c in range(C):
        band_blocks(hbuf, band, 0, c, inner_blocks, R)
    for l in range(1, L):
        arrive(0, l)
        angles(l)
    local[4].wait()
    arrive(1, 0)
    for l in range(L):
        if l > 0:
            arrive(1, l)
            for c in range(C):
                band_blocks(hbuf, band, l, c, inner_blocks, R)
        if l == L - 1:
            for way in (LEFT, RIGHT):

                @pl.when(exists[way])
                def _():
                    edge_copy(opposite[way]).wait_recv()

            for j in range(nb):
                parts = (
                    band_edge[0] if j == 0 else band[j - 1, 2],
                    band[j, 1],
                    band_edge[1] if j == nb - 1 else band[j + 1, 0],
                )
                for k in range(3):
                    band_t[j, k] = parts[k].astype(F32).T.astype(BF16)
        for c in range(C):
            forward_finish(l, c)
            if l + 1 < L:
                send_halo(forward, l + 1, c)
        if l + 1 < L:
            deliver(0, l)
    local[5].wait()
    for l in range(L):
        arrive(2, l)
    for c in range(C):
        first_adjoint(c)
        send_halo(backward, L - 1, c)
    deliver(0, L - 1)
    for l in reversed(range(L)):
        for c in range(C):
            band_blocks(gbuf, band_t, l, c, inner_blocks, RB)
        for c in range(C):
            backward_finish(l, c)
            if l > 0:
                send_halo(backward, l - 1, c)
        deliver(1, l)

    for l in range(L):
        for c in range(C):
            for way in DIRS:

                @pl.when(exists[way])
                def _():
                    halo_copy(*forward, l, c, way).wait_send()
                    halo_copy(*backward, l, c, way).wait_send()

    for s in range(1, D):
        for a in range(3):
            table_copy(a, s).wait_send()
    for way in (LEFT, RIGHT):

        @pl.when(exists[way])
        def _():
            edge_copy(way).wait_send()

    for a in range(2):
        for l in range(L):

            @pl.when(me == l // layers)
            def _():
                own_copy(a, l).wait()

            @pl.when(me != l // layers)
            def _():
                out_copy(a, l).wait_send()

        for i in range(layers):
            for s in range(1, D):
                source = lax.rem(me - s + D, D)
                theirs = pl.ds(pl.multiple_of(source * W, B), W)
                pltpu.make_async_remote_copy(
                    src_ref=results[a][0].at[i],
                    dst_ref=results[a][1].at[i, :, theirs],
                    send_sem=osend.at[a, i],
                    recv_sem=orecv.at[a, i, s],
                    device_id={"depth": source},
                    device_id_type=MESH,
                ).wait_recv()


def per_device(source_field, receiver_field, freq_index, slowness, ffd_coef, band, image_mask):
    D, LATS = lax.axis_size("depth"), lax.axis_size("lat")
    NF, _, height, width = source_field.shape
    layers = slowness.shape[0]
    L = layers * D
    nb, _, B, _ = band.shape
    W = width // D
    assert height == HALO and W == nb * B
    C = 2 if NF % 2 == 0 else 1
    NFC = NF // C
    dims = (D, LATS, L, layers, NF, C, nb, B, W)
    R, RB = NFC * 32, NFC * 16
    dma = pltpu.SemaphoreType.DMA
    anywhere = pl.BlockSpec(memory_space=pl.ANY)
    tile = (height, W)
    scratch = [
        pltpu.VMEM((2, NF, 2) + tile, BF16),
        pltpu.VMEM((L,) + tile, F32),
        pltpu.VMEM((L,) + tile, F32),
        pltpu.VMEM((L,) + tile, jnp.int32),
        pltpu.VMEM((nb, 3, B, B), BF16),
        pltpu.VMEM((nb, 3, B, B), BF16),
        pltpu.VMEM((2, B, B), BF16),
        pltpu.VMEM((L, NF) + tile, F32),
        pltpu.VMEM((L, NF) + tile, F32),
        pltpu.VMEM((L, NF, 2, 2) + tile, F32),
        pltpu.VMEM((L, NF, 2) + tile, F32),
        pltpu.VMEM((NF, 2) + tile, F32),
        pltpu.VMEM((L, C, R, W + 2 * B), BF16),
        pltpu.VMEM((L, C, 2, R, W), BF16),
        pltpu.VMEM((L, C, RB, W + 2 * B), BF16),
        pltpu.VMEM((L, C, 2, RB, W), BF16),
        pltpu.VMEM((C, R, W), F32),
        pltpu.VMEM((L,) + tile, F32),
        pltpu.VMEM((L,) + tile, F32),
        dma((L, C, 4)),
        dma((L, C, 4)),
        dma((L, C, 4)),
        dma((L, C, 4)),
        dma((3, D)),
        dma((3, D)),
        dma((2,)),
        dma((2,)),
        dma((2, L)),
        dma((2, layers, D)),
        dma((2, layers)),
        dma((6,)),
    ]
    return pl.pallas_call(
        functools.partial(kernel, dims),
        out_shape=[jax.ShapeDtypeStruct(slowness.shape, F32)] * 2,
        in_specs=[pl.BlockSpec(memory_space=pltpu.SMEM)] + [anywhere] * 6,
        out_specs=[anywhere] * 2,
        scratch_shapes=scratch,
        compiler_params=pltpu.CompilerParams(
            collective_id=0, has_side_effects=True, vmem_limit_bytes=48 * 1024 * 1024
        ),
    )(freq_index, source_field, receiver_field, slowness, ffd_coef, image_mask, band)


def solution(mesh):
    return jax.shard_map(
        per_device,
        mesh=mesh,
        in_specs=(
            P(None, None, "lat", None),
            P(None, None, "lat", None),
            P(),
            P("depth", "lat", None),
            P("depth", "lat", None),
            P("depth", None, None, None),
            P("depth", "lat", None),
        ),
        out_specs=(P("depth", "lat", None), P("depth", "lat", None)),
        check_vma=False,
    )
```

```python
import functools

import jax
import jax.numpy as jnp
from jax import lax
from jax.experimental import pallas as pl
from jax.experimental.pallas import tpu as pltpu
from jax.sharding import PartitionSpec as P

HALO = 8
F32 = jnp.float32
BF16 = jnp.bfloat16
WEIGHTS = [0.0] + [0.25 / k for k in range(1, HALO + 1)]
UP, DOWN, LEFT, RIGHT = range(4)


def sincos(theta):
    turns = jnp.floor(theta * 0.6366197723675814 + 0.5)
    rest = theta - turns * 1.5703125
    rest = rest - turns * 4.837512969970703125e-4
    rest = rest - turns * 7.54978995489188216e-8
    square = rest * rest
    sine = rest + rest * square * (
        -1.6666654611e-1 + square * (8.3321608736e-3 + square * -1.9515295891e-4)
    )
    cosine = (
        1.0
        - 0.5 * square
        + square
        * square
        * (
            4.166664568298827e-2
            + square * (-1.388731625493765e-3 + square * 2.443315711809948e-5)
        )
    )
    quadrant = turns.astype(jnp.int32)
    odd = (quadrant & 1) == 1
    sin_out = jnp.where(odd, cosine, sine)
    cos_out = jnp.where(odd, sine, cosine)
    sin_out = jnp.where((quadrant & 2) == 2, -sin_out, sin_out)
    cos_out = jnp.where(((quadrant + 1) & 2) == 2, -cos_out, cos_out)
    return sin_out, cos_out


def stencil(cur, prev, nxt):
    row = lax.broadcasted_iota(jnp.int32, cur.shape, 0)
    total = WEIGHTS[HALO] * (prev + nxt) - 2.0 * sum(WEIGHTS) * cur
    for k in range(1, HALO):
        inside = row >= k
        near = jnp.where(inside, WEIGHTS[k], WEIGHTS[HALO - k])
        far = jnp.where(inside, WEIGHTS[HALO - k], WEIGHTS[k])
        mixed = near * cur + far * jnp.where(inside, prev, nxt)
        total = total + pltpu.roll(mixed, HALO - k, 0)
    return total


def loop(count, body):
    if count <= 2:
        for i in range(count):
            body(i)
    else:
        lax.fori_loop(0, count, lambda i, c: (body(i), c)[1], 0)


def kernel(
    dims,
    freq_hbm,
    src_ref,
    rcv_ref,
    slow_ref,
    coef_ref,
    mask_ref,
    band_ref,
    image_ref,
    grad_ref,
    freq_ref,
    fields,
    slow,
    coef,
    mask,
    band,
    band_t,
    band_edge,
    sines,
    cosines,
    phased,
    state,
    adj,
    hbuf,
    hlat,
    gbuf,
    glat,
    qbuf,
    img,
    grad,
    fsend,
    frecv,
    bsend,
    brecv,
    rsend,
    rrecv,
    esend,
    erecv,
    osend,
    orecv,
    own_sem,
    loc_sem,
    band_sem,
):
    D, LATS, L, layers, NF, C, nb, G, B, W = dims
    NFC = NF // C
    me = lax.axis_index("depth")
    lat = lax.axis_index("lat")
    first = pl.multiple_of(me * W, B)
    mine = pl.ds(first, W)
    exists = {UP: lat > 0, DOWN: lat < LATS - 1, LEFT: me > 0, RIGHT: me < D - 1}
    target = {
        UP: {"lat": lat - 1},
        DOWN: {"lat": lat + 1},
        LEFT: {"depth": me - 1},
        RIGHT: {"depth": me + 1},
    }
    opposite = {UP: DOWN, DOWN: UP, LEFT: RIGHT, RIGHT: LEFT}
    DIRS = (LEFT, RIGHT, UP, DOWN)
    MESH = pl.DeviceIdType.MESH

    own_levels = pl.ds(me * layers, layers)
    local = [
        pltpu.make_async_copy(slow_ref.at[:, :, mine], slow.at[own_levels], loc_sem.at[0]),
        pltpu.make_async_copy(src_ref.at[:, :, :, mine], fields.at[0], loc_sem.at[1]),
        pltpu.make_async_copy(rcv_ref.at[:, :, :, mine], fields.at[1], loc_sem.at[2]),
        pltpu.make_async_copy(coef_ref.at[:, :, mine], coef.at[own_levels], loc_sem.at[3]),
        pltpu.make_async_copy(mask_ref.at[:, :, mine], mask.at[own_levels], loc_sem.at[4]),
        pltpu.make_async_copy(freq_hbm, freq_ref, loc_sem.at[5]),
    ] + [
        pltpu.make_async_copy(
            band_ref.at[:, e], band.at[:, e : e + 3, :, e * B : (e + 1) * B], band_sem.at[e]
        )
        for e in range(G)
    ]
    for copy in local:
        copy.start()

    barrier = pltpu.get_barrier_semaphore()
    for way in (UP, DOWN):

        @pl.when(exists[way])
        def _():
            pl.semaphore_signal(barrier, inc=1, device_id=target[way], device_id_type=MESH)

    for s in range(1, D):
        pl.semaphore_signal(
            barrier, inc=1, device_id={"depth": lax.rem(me + s, D)}, device_id_type=MESH
        )
    for way in (UP, DOWN):

        @pl.when(jnp.logical_not(exists[way]))
        def _():
            hlat[:, :, way] = jnp.zeros(hlat.shape[:2] + hlat.shape[3:], BF16)
            glat[:, :, way] = jnp.zeros(glat.shape[:2] + glat.shape[3:], BF16)

    for way, start, slot in ((LEFT, 0, 0), (RIGHT, W + B, 1)):

        @pl.when(jnp.logical_not(exists[way]))
        def _():
            hbuf[:, :, :, start : start + B] = jnp.zeros(hbuf.shape[:3] + (B,), BF16)
            gbuf[:, :, :, start : start + B] = jnp.zeros(gbuf.shape[:3] + (B,), BF16)
            band_edge[slot] = jnp.zeros((B, B), BF16)

    for matrix in (band, band_t):
        for e in range(G):
            for r in range(G + 2):
                if not e <= r < e + 3:
                    matrix[:, r, :, e * B : (e + 1) * B] = jnp.zeros((nb // G, B, B), BF16)

    pl.semaphore_wait(
        barrier, (D - 1) + exists[UP].astype(jnp.int32) + exists[DOWN].astype(jnp.int32)
    )

    tables = ((slow_ref, slow), (coef_ref, coef), (mask_ref, mask))

    def table_copy(a, s):
        peer = lax.rem(me + s, D)
        return pltpu.make_async_remote_copy(
            src_ref=tables[a][0].at[:, :, pl.ds(pl.multiple_of(peer * W, B), W)],
            dst_ref=tables[a][1].at[own_levels],
            send_sem=rsend.at[a, s],
            recv_sem=rrecv.at[a, s],
            device_id={"depth": peer},
            device_id_type=MESH,
        )

    def table_wait(a, s):
        source = lax.rem(me - s + D, D)
        pltpu.make_async_remote_copy(
            src_ref=tables[a][1].at[pl.ds(source * layers, layers)],
            dst_ref=tables[a][1].at[pl.ds(source * layers, layers)],
            send_sem=rsend.at[a, s],
            recv_sem=rrecv.at[a, s],
            device_id={"depth": source},
            device_id_type=MESH,
        ).wait_recv()

    def edge_copy(way):
        j, k, slot = (0, 0, 1) if way == LEFT else (nb - 1, 2, 0)
        return pltpu.make_async_remote_copy(
            src_ref=band_ref.at[j // G, j % G, k],
            dst_ref=band_edge.at[slot],
            send_sem=esend.at[slot],
            recv_sem=erecv.at[slot],
            device_id=target[way],
            device_id_type=MESH,
        )

    for a in (0, 1):
        for s in range(1, D):
            table_copy(a, s).start()

    def late_sends():
        for s in range(1, D):
            table_copy(2, s).start()
        for way in (LEFT, RIGHT):

            @pl.when(exists[way])
            def _():
                edge_copy(way).start()

    def halo_copy(buf, lats, ssem, rsem, l, c, way):
        if way in (UP, DOWN):
            src = buf.at[l, c, :, pl.ds(B, W)]
            dst = lats.at[l, c, opposite[way]]
        else:
            src = buf.at[l, c, :, pl.ds(B if way == LEFT else W, B)]
            dst = buf.at[l, c, :, pl.ds(W + B if way == LEFT else 0, B)]
        return pltpu.make_async_remote_copy(
            src_ref=src,
            dst_ref=dst,
            send_sem=ssem.at[l, c, way],
            recv_sem=rsem.at[l, c, opposite[way]],
            device_id=target[way],
            device_id_type=MESH,
        )

    def send_halo(args, l, c):
        for way in DIRS:

            @pl.when(exists[way])
            def _():
                halo_copy(*args, l, c, way).start()

    def wait_halo(args, l, c, ways):
        for way in ways:

            @pl.when(exists[way])
            def _():
                halo_copy(*args, l, c, opposite[way]).wait_recv()

    forward = (hbuf, hlat, fsend, frecv)
    backward = (gbuf, glat, bsend, brecv)

    CW = min(W, 512)
    pieces = [slice(x, x + CW) for x in range(0, W, CW)]

    def omega_of(f):
        return 0.1 * (freq_ref[f].astype(F32) + 1.0)

    def angles(l):
        def one(f):
            omega = omega_of(f)
            for cols in pieces:
                sines[l, f, :, cols], cosines[l, f, :, cols] = sincos(omega * slow[l, :, cols])

        loop(NF, one)

    def store_phase(l, c, fi, s, cols, re, im):
        f = c * NFC + fi
        cosine, sine = cosines[l, f, :, cols], sines[l, f, :, cols]
        phase_re = re * cosine - im * sine
        phase_im = re * sine + im * cosine
        phased[l, f, s, 0, :, cols] = phase_re
        phased[l, f, s, 1, :, cols] = phase_im
        rows = pl.ds(pl.multiple_of((fi * 2 + s) * 16, 16), 16)
        inner = slice(cols.start + B, cols.stop + B)
        hbuf[l, c, rows, inner] = jnp.concatenate([phase_re, phase_im], axis=0).astype(BF16)

    def first_phase(c):
        def one(fi):
            f = c * NFC + fi
            for s in range(2):
                for cols in pieces:
                    re = fields[s, f, 0, :, cols].astype(F32)
                    im = fields[s, f, 1, :, cols].astype(F32)
                    store_phase(0, c, fi, s, cols, re, im)

        loop(NFC, one)

    R, RB = NFC * 32, NFC * 16

    def band_groups(buf, matrix, l, groups, rows):
        for p in groups:
            left = p * G * B
            qbuf[: C * rows, left : left + G * B] = jnp.dot(
                buf[l, :, :, left : left + (G + 2) * B].reshape(C * rows, (G + 2) * B),
                matrix[p].reshape((G + 2) * B, G * B),
                preferred_element_type=F32,
            )

    inner_groups = range(1, nb // G - 1)
    outer_groups = sorted({0, nb // G - 1})

    def band_products(args, matrix, l, rows):
        band_groups(args[0], matrix, l, inner_groups, rows)
        for c in range(C):
            wait_halo(args, l, c, (LEFT, RIGHT))
        band_groups(args[0], matrix, l, outer_groups, rows)

    def lateral(buf, lats, l, c, row, cols):
        rows = pl.ds(pl.multiple_of(row, 16), 16)
        cur = buf[l, c, rows, cols.start + B : cols.stop + B].astype(F32)
        prev = lats[l, c, UP, rows, cols].astype(F32)
        nxt = lats[l, c, DOWN, rows, cols].astype(F32)
        product = qbuf[pl.ds(pl.multiple_of(c * buf.shape[2] + row, 16), 16), cols]
        return [
            product[h] + stencil(cur[h], prev[h], nxt[h]) for h in (slice(0, 8), slice(8, 16))
        ]

    def forward_finish(l, c):
        wait_halo(forward, l, c, (UP, DOWN))

        def one(fi):
            f = c * NFC + fi
            for cols in pieces:
                coefs = coef[l, :, cols]
                new = []
                for s in range(2):
                    q_re, q_im = lateral(hbuf, hlat, l, c, (fi * 2 + s) * 16, cols)
                    re = phased[l, f, s, 0, :, cols] - coefs * q_im
                    im = phased[l, f, s, 1, :, cols] + coefs * q_re
                    new.append((re, im))
                    if l + 1 < L:
                        store_phase(
                            l + 1,
                            c,
                            fi,
                            s,
                            cols,
                            re.astype(BF16).astype(F32),
                            im.astype(BF16).astype(F32),
                        )
                state[l, f, 0, :, cols] = new[0][0]
                state[l, f, 1, :, cols] = new[0][1]
                product = new[0][0] * new[1][0] + new[0][1] * new[1][1]
                if c == 0 and isinstance(fi, int) and fi == 0:
                    img[l, :, cols] = product
                else:
                    img[l, :, cols] += product

        if NFC > 2 and c == 0:
            img[l] = jnp.zeros(img.shape[1:], F32)
        loop(NFC, one)
        if c == C - 1:
            img[l] = img[l] * (1.0 / NF)

    results = ((img, image_ref), (grad, grad_ref))

    def own_copy(a, l):
        return pltpu.make_async_copy(
            results[a][0].at[l], results[a][1].at[l % layers, :, mine], own_sem.at[a, l % layers]
        )

    def out_copy(a, l):
        owner = l // layers
        return pltpu.make_async_remote_copy(
            src_ref=results[a][0].at[l],
            dst_ref=results[a][1].at[l % layers, :, mine],
            send_sem=osend.at[a, l],
            recv_sem=orecv.at[a, l % layers, lax.rem(owner - me + D, D)],
            device_id={"depth": owner},
            device_id_type=MESH,
        )

    def deliver(a, l):
        @pl.when(me == l // layers)
        def _():
            own_copy(a, l).start()

        @pl.when(me != l // layers)
        def _():
            out_copy(a, l).start()

    def begin_adjoint(l, c, fi, cols, mu):
        f = c * NFC + fi
        weight = mask[l, :, cols].astype(F32) * img[l, :, cols]
        coefs = coef[l, :, cols]
        scaled = []
        for part in range(2):
            value = weight * state[l, f, part, :, cols]
            if mu is not None:
                value = value + mu[part]
            adj[f, part, :, cols] = value
            scaled.append(coefs * value)
        rows = pl.ds(pl.multiple_of(fi * 16, 16), 16)
        gbuf[l, c, rows, cols.start + B : cols.stop + B] = jnp.concatenate(
            scaled, axis=0
        ).astype(BF16)

    def first_adjoint(c):
        def one(fi):
            for cols in pieces:
                begin_adjoint(L - 1, c, fi, cols, None)

        loop(NFC, one)

    def backward_finish(l, c):
        wait_halo(backward, l, c, (UP, DOWN))

        def one(fi):
            f = c * NFC + fi
            omega = omega_of(f)
            for cols in pieces:
                t_re, t_im = lateral(gbuf, glat, l, c, fi * 16, cols)
                back_re = adj[f, 0, :, cols] + t_im
                back_im = adj[f, 1, :, cols] - t_re
                term = omega * (
                    back_im * phased[l, f, 1, 0, :, cols] - back_re * phased[l, f, 1, 1, :, cols]
                )
                if c == 0 and isinstance(fi, int) and fi == 0:
                    grad[l, :, cols] = term
                else:
                    grad[l, :, cols] += term
                if l > 0:
                    cosine, sine = cosines[l, f, :, cols], sines[l, f, :, cols]
                    mu_re = back_re * cosine + back_im * sine
                    mu_im = back_im * cosine - back_re * sine
                    mu = [mu_re.astype(BF16).astype(F32), mu_im.astype(BF16).astype(F32)]
                    begin_adjoint(l - 1, c, fi, cols, mu)

        if NFC > 2 and c == 0:
            grad[l] = jnp.zeros(grad.shape[1:], F32)
        loop(NFC, one)
        if c == C - 1:
            grad[l] = grad[l] * (1.0 / NF)

    def arrive(a, l):
        if l % layers == 0:
            s = lax.rem(me - l // layers + D, D)

            @pl.when(s != 0)
            def _():
                table_wait(a, s)

    def transpose(j, k):
        i = j + k - 1
        if k != 1 and not 0 <= j < nb:
            value = band_edge[0 if j < 0 else 1]
        else:
            value = band[j // G, j % G + k, :, (j % G) * B : (j % G + 1) * B]
        band_t[i // G, i % G + 2 - k, :, (i % G) * B : (i % G + 1) * B] = (
            value.astype(F32).T.astype(BF16)
        )

    for copy in local[6:]:
        copy.wait()
    for j in range(nb):
        for k in range(3):
            if 0 <= j + k - 1 < nb:
                transpose(j, k)
    local[0].wait()
    local[5].wait()
    arrive(0, 0)
    angles(0)
    local[1].wait()
    local[2].wait()
    for c in range(C):
        first_phase(c)
        send_halo(forward, 0, c)
    late_sends()
    for l in range(1, L):
        arrive(0, l)
        angles(l)
    local[3].wait()
    arrive(1, 0)
    for l in range(L):
        if l > 0:
            arrive(1, l)
        band_products(forward, band, l, R)
        if l == L - 1:
            for way in (LEFT, RIGHT):

                @pl.when(exists[way])
                def _():
                    edge_copy(opposite[way]).wait_recv()

            transpose(-1, 2)
            transpose(nb, 0)
        for c in range(C):
            forward_finish(l, c)
            if l + 1 < L:
                send_halo(forward, l + 1, c)
        if l + 1 < L:
            deliver(0, l)
    local[4].wait()
    for l in range(L):
        arrive(2, l)
    for c in range(C):
        first_adjoint(c)
        send_halo(backward, L - 1, c)
    deliver(0, L - 1)
    for l in reversed(range(L)):
        band_products(backward, band_t, l, RB)
        for c in range(C):
            backward_finish(l, c)
            if l > 0:
                send_halo(backward, l - 1, c)
        deliver(1, l)

    for l in range(L):
        for c in range(C):
            for way in DIRS:

                @pl.when(exists[way])
                def _():
                    halo_copy(*forward, l, c, way).wait_send()
                    halo_copy(*backward, l, c, way).wait_send()

    for s in range(1, D):
        for a in range(3):
            table_copy(a, s).wait_send()
    for way in (LEFT, RIGHT):

        @pl.when(exists[way])
        def _():
            edge_copy(way).wait_send()

    for a in range(2):
        for l in range(L):

            @pl.when(me == l // layers)
            def _():
                own_copy(a, l).wait()

            @pl.when(me != l // layers)
            def _():
                out_copy(a, l).wait_send()

        for i in range(layers):
            for s in range(1, D):
                source = lax.rem(me - s + D, D)
                theirs = pl.ds(pl.multiple_of(source * W, B), W)
                pltpu.make_async_remote_copy(
                    src_ref=results[a][0].at[i],
                    dst_ref=results[a][1].at[i, :, theirs],
                    send_sem=osend.at[a, i],
                    recv_sem=orecv.at[a, i, s],
                    device_id={"depth": source},
                    device_id_type=MESH,
                ).wait_recv()


def per_device(source_field, receiver_field, freq_index, slowness, ffd_coef, band, image_mask):
    D, LATS = lax.axis_size("depth"), lax.axis_size("lat")
    NF, _, height, width = source_field.shape
    layers = slowness.shape[0]
    L = layers * D
    nb, _, B, _ = band.shape
    W = width // D
    assert height == HALO and W == nb * B
    C = 2 if NF % 2 == 0 else 1
    NFC = NF // C
    G = 2 if nb % 2 == 0 else 1
    dims = (D, LATS, L, layers, NF, C, nb, G, B, W)
    R, RB = NFC * 32, NFC * 16
    dma = pltpu.SemaphoreType.DMA
    anywhere = pl.BlockSpec(memory_space=pl.ANY)
    in_hbm = pl.BlockSpec(memory_space=pltpu.HBM)
    tile = (height, W)
    scratch = [
        pltpu.SMEM((NF,), jnp.int32),
        pltpu.VMEM((2, NF, 2) + tile, BF16),
        pltpu.VMEM((L,) + tile, F32),
        pltpu.VMEM((L,) + tile, F32),
        pltpu.VMEM((L,) + tile, jnp.int32),
        pltpu.VMEM((nb // G, G + 2, B, G * B), BF16),
        pltpu.VMEM((nb // G, G + 2, B, G * B), BF16),
        pltpu.VMEM((2, B, B), BF16),
        pltpu.VMEM((L, NF) + tile, F32),
        pltpu.VMEM((L, NF) + tile, F32),
        pltpu.VMEM((L, NF, 2, 2) + tile, F32),
        pltpu.VMEM((L, NF, 2) + tile, F32),
        pltpu.VMEM((NF, 2) + tile, F32),
        pltpu.VMEM((L, C, R, W + 2 * B), BF16),
        pltpu.VMEM((L, C, 2, R, W), BF16),
        pltpu.VMEM((L, C, RB, W + 2 * B), BF16),
        pltpu.VMEM((L, C, 2, RB, W), BF16),
        pltpu.VMEM((C * R, W), F32),
        pltpu.VMEM((L,) + tile, F32),
        pltpu.VMEM((L,) + tile, F32),
        dma((L, C, 4)),
        dma((L, C, 4)),
        dma((L, C, 4)),
        dma((L, C, 4)),
        dma((3, D)),
        dma((3, D)),
        dma((2,)),
        dma((2,)),
        dma((2, L)),
        dma((2, layers, D)),
        dma((2, layers)),
        dma((6,)),
        dma((G,)),
    ]
    return pl.pallas_call(
        functools.partial(kernel, dims),
        out_shape=[jax.ShapeDtypeStruct(slowness.shape, F32)] * 2,
        in_specs=[in_hbm] * 7,
        out_specs=[anywhere] * 2,
        scratch_shapes=scratch,
        compiler_params=pltpu.CompilerParams(
            collective_id=0, has_side_effects=True, vmem_limit_bytes=48 * 1024 * 1024
        ),
    )(freq_index, source_field, receiver_field, slowness, ffd_coef, image_mask, band.reshape(nb // G, G, 3, B, B))


def solution(mesh):
    return jax.shard_map(
        per_device,
        mesh=mesh,
        in_specs=(
            P(None, None, "lat", None),
            P(None, None, "lat", None),
            P(),
            P("depth", "lat", None),
            P("depth", "lat", None),
            P("depth", None, None, None),
            P("depth", "lat", None),
        ),
        out_specs=(P("depth", "lat", None), P("depth", "lat", None)),
        check_vma=False,
    )
```

```python
import functools

import jax
import jax.numpy as jnp
from jax import lax
from jax.experimental import pallas as pl
from jax.experimental.pallas import tpu as pltpu
from jax.sharding import PartitionSpec as P

HALO = 8
VMEM_BYTES = 64 * 1024 * 1024
F32 = jnp.float32
BF16 = jnp.bfloat16
WEIGHTS = [0.0] + [0.25 / k for k in range(1, HALO + 1)]
UP, DOWN, LEFT, RIGHT = range(4)


def sincos(theta):
    turns = jnp.floor(theta * 0.6366197723675814 + 0.5)
    rest = theta - turns * 1.5703125
    rest = rest - turns * 4.837512969970703125e-4
    rest = rest - turns * 7.54978995489188216e-8
    square = rest * rest
    sine = rest + rest * square * (
        -1.6666654611e-1 + square * (8.3321608736e-3 + square * -1.9515295891e-4)
    )
    cosine = (
        1.0
        - 0.5 * square
        + square
        * square
        * (
            4.166664568298827e-2
            + square * (-1.388731625493765e-3 + square * 2.443315711809948e-5)
        )
    )
    quadrant = turns.astype(jnp.int32)
    odd = (quadrant & 1) == 1
    sin_out = jnp.where(odd, cosine, sine)
    cos_out = jnp.where(odd, sine, cosine)
    sin_out = jnp.where((quadrant & 2) == 2, -sin_out, sin_out)
    cos_out = jnp.where(((quadrant + 1) & 2) == 2, -cos_out, cos_out)
    return sin_out, cos_out


def stencil(cur, prev, nxt):
    row = lax.broadcasted_iota(jnp.int32, cur.shape, 0)
    total = WEIGHTS[HALO] * (prev + nxt) - 2.0 * sum(WEIGHTS) * cur
    for k in range(1, HALO):
        inside = row >= k
        near = jnp.where(inside, WEIGHTS[k], WEIGHTS[HALO - k])
        far = jnp.where(inside, WEIGHTS[HALO - k], WEIGHTS[k])
        mixed = near * cur + far * jnp.where(inside, prev, nxt)
        total = total + pltpu.roll(mixed, HALO - k, 0)
    return total


def loop(count, body):
    if count <= 2:
        for i in range(count):
            body(i)
    else:
        lax.fori_loop(0, count, lambda i, c: (body(i), c)[1], 0)


def kernel(
    dims,
    freq_hbm,
    src_ref,
    rcv_ref,
    slow_ref,
    coef_ref,
    mask_ref,
    band_ref,
    image_ref,
    grad_ref,
    freq_ref,
    fields,
    slow,
    coef,
    mask,
    band,
    band_t,
    band_edge,
    sines,
    cosines,
    phased,
    state,
    adj,
    hbuf,
    hlat,
    gbuf,
    glat,
    qbuf,
    img,
    grad,
    fsend,
    frecv,
    bsend,
    brecv,
    rsend,
    rrecv,
    esend,
    erecv,
    osend,
    orecv,
    own_sem,
    loc_sem,
    band_sem,
):
    D, LATS, L, layers, NF, C, nb, G, B, W = dims
    NFC = NF // C
    me = lax.axis_index("depth")
    lat = lax.axis_index("lat")
    first = pl.multiple_of(me * W, B)
    mine = pl.ds(first, W)
    exists = {UP: lat > 0, DOWN: lat < LATS - 1, LEFT: me > 0, RIGHT: me < D - 1}
    target = {
        UP: {"lat": lat - 1},
        DOWN: {"lat": lat + 1},
        LEFT: {"depth": me - 1},
        RIGHT: {"depth": me + 1},
    }
    opposite = {UP: DOWN, DOWN: UP, LEFT: RIGHT, RIGHT: LEFT}
    DIRS = (LEFT, RIGHT, UP, DOWN)
    MESH = pl.DeviceIdType.MESH

    own_levels = pl.ds(me * layers, layers)
    local = [
        pltpu.make_async_copy(slow_ref.at[:, :, mine], slow.at[own_levels], loc_sem.at[0]),
        pltpu.make_async_copy(src_ref.at[:, :, :, mine], fields.at[0], loc_sem.at[1]),
        pltpu.make_async_copy(rcv_ref.at[:, :, :, mine], fields.at[1], loc_sem.at[2]),
        pltpu.make_async_copy(coef_ref.at[:, :, mine], coef.at[own_levels], loc_sem.at[3]),
        pltpu.make_async_copy(mask_ref.at[:, :, mine], mask.at[own_levels], loc_sem.at[4]),
        pltpu.make_async_copy(freq_hbm, freq_ref, loc_sem.at[5]),
    ] + [
        pltpu.make_async_copy(
            band_ref.at[:, e], band.at[:, e : e + 3, :, e * B : (e + 1) * B], band_sem.at[e]
        )
        for e in range(G)
    ]
    for copy in local:
        copy.start()

    barrier = pltpu.get_barrier_semaphore()
    for way in (UP, DOWN):

        @pl.when(exists[way])
        def _():
            pl.semaphore_signal(barrier, inc=1, device_id=target[way], device_id_type=MESH)

    for s in range(1, D):
        pl.semaphore_signal(
            barrier, inc=1, device_id={"depth": lax.rem(me + s, D)}, device_id_type=MESH
        )
    for way in (UP, DOWN):

        @pl.when(jnp.logical_not(exists[way]))
        def _():
            hlat[:, :, way] = jnp.zeros(hlat.shape[:2] + hlat.shape[3:], BF16)
            glat[:, :, way] = jnp.zeros(glat.shape[:2] + glat.shape[3:], BF16)

    for way, start, slot in ((LEFT, 0, 0), (RIGHT, W + B, 1)):

        @pl.when(jnp.logical_not(exists[way]))
        def _():
            hbuf[:, :, :, start : start + B] = jnp.zeros(hbuf.shape[:3] + (B,), BF16)
            gbuf[:, :, :, start : start + B] = jnp.zeros(gbuf.shape[:3] + (B,), BF16)
            band_edge[slot] = jnp.zeros((B, B), BF16)

    for matrix in (band, band_t):
        for e in range(G):
            for r in range(G + 2):
                if not e <= r < e + 3:
                    matrix[:, r, :, e * B : (e + 1) * B] = jnp.zeros((nb // G, B, B), BF16)

    pl.semaphore_wait(
        barrier, (D - 1) + exists[UP].astype(jnp.int32) + exists[DOWN].astype(jnp.int32)
    )

    tables = ((slow_ref, slow), (coef_ref, coef), (mask_ref, mask))

    def table_copy(a, s):
        peer = lax.rem(me + s, D)
        return pltpu.make_async_remote_copy(
            src_ref=tables[a][0].at[:, :, pl.ds(pl.multiple_of(peer * W, B), W)],
            dst_ref=tables[a][1].at[own_levels],
            send_sem=rsend.at[a, s],
            recv_sem=rrecv.at[a, s],
            device_id={"depth": peer},
            device_id_type=MESH,
        )

    def table_wait(a, s):
        source = lax.rem(me - s + D, D)
        pltpu.make_async_remote_copy(
            src_ref=tables[a][1].at[pl.ds(source * layers, layers)],
            dst_ref=tables[a][1].at[pl.ds(source * layers, layers)],
            send_sem=rsend.at[a, s],
            recv_sem=rrecv.at[a, s],
            device_id={"depth": source},
            device_id_type=MESH,
        ).wait_recv()

    def edge_copy(way):
        j, k, slot = (0, 0, 1) if way == LEFT else (nb - 1, 2, 0)
        return pltpu.make_async_remote_copy(
            src_ref=band_ref.at[j // G, j % G, k],
            dst_ref=band_edge.at[slot],
            send_sem=esend.at[slot],
            recv_sem=erecv.at[slot],
            device_id=target[way],
            device_id_type=MESH,
        )

    for a in (0, 1):
        for s in range(1, D):
            table_copy(a, s).start()

    def late_sends():
        for s in range(1, D):
            table_copy(2, s).start()
        for way in (LEFT, RIGHT):

            @pl.when(exists[way])
            def _():
                edge_copy(way).start()

    def halo_copy(buf, lats, ssem, rsem, l, c, way):
        if way in (UP, DOWN):
            src = buf.at[l, c, :, pl.ds(B, W)]
            dst = lats.at[l, c, opposite[way]]
        else:
            src = buf.at[l, c, :, pl.ds(B if way == LEFT else W, B)]
            dst = buf.at[l, c, :, pl.ds(W + B if way == LEFT else 0, B)]
        return pltpu.make_async_remote_copy(
            src_ref=src,
            dst_ref=dst,
            send_sem=ssem.at[l, c, way],
            recv_sem=rsem.at[l, c, opposite[way]],
            device_id=target[way],
            device_id_type=MESH,
        )

    def send_halo(args, l, c):
        for way in DIRS:

            @pl.when(exists[way])
            def _():
                halo_copy(*args, l, c, way).start()

    def wait_halo(args, l, c, ways):
        for way in ways:

            @pl.when(exists[way])
            def _():
                halo_copy(*args, l, c, opposite[way]).wait_recv()

    forward = (hbuf, hlat, fsend, frecv)
    backward = (gbuf, glat, bsend, brecv)

    CW = min(W, 512)
    pieces = [slice(x, x + CW) for x in range(0, W, CW)]

    def omega_of(f):
        return 0.1 * (freq_ref[f].astype(F32) + 1.0)

    def angles(l):
        def one(f):
            omega = omega_of(f)
            for cols in pieces:
                sines[l, f, :, cols], cosines[l, f, :, cols] = sincos(omega * slow[l, :, cols])

        loop(NF, one)

    def store_phase(l, c, fi, s, cols, re, im):
        f = c * NFC + fi
        cosine, sine = cosines[l, f, :, cols], sines[l, f, :, cols]
        phase_re = re * cosine - im * sine
        phase_im = re * sine + im * cosine
        phased[l, f, s, 0, :, cols] = phase_re
        phased[l, f, s, 1, :, cols] = phase_im
        rows = pl.ds(pl.multiple_of((fi * 2 + s) * 16, 16), 16)
        inner = slice(cols.start + B, cols.stop + B)
        hbuf[l, c, rows, inner] = jnp.concatenate([phase_re, phase_im], axis=0).astype(BF16)

    def first_phase(c):
        def one(fi):
            f = c * NFC + fi
            for s in range(2):
                for cols in pieces:
                    re = fields[s, f, 0, :, cols].astype(F32)
                    im = fields[s, f, 1, :, cols].astype(F32)
                    store_phase(0, c, fi, s, cols, re, im)

        loop(NFC, one)

    R, RB = NFC * 32, NFC * 16

    def band_groups(buf, matrix, l, groups, rows):
        for p in groups:
            left = p * G * B
            qbuf[: C * rows, left : left + G * B] = jnp.dot(
                buf[l, :, :, left : left + (G + 2) * B].reshape(C * rows, (G + 2) * B),
                matrix[p].reshape((G + 2) * B, G * B),
                preferred_element_type=F32,
            )

    inner_groups = range(1, nb // G - 1)
    outer_groups = sorted({0, nb // G - 1})

    def band_products(args, matrix, l, rows):
        band_groups(args[0], matrix, l, inner_groups, rows)
        for c in range(C):
            wait_halo(args, l, c, (LEFT, RIGHT))
        band_groups(args[0], matrix, l, outer_groups, rows)

    def lateral(buf, lats, l, c, row, cols):
        rows = pl.ds(pl.multiple_of(row, 16), 16)
        cur = buf[l, c, rows, cols.start + B : cols.stop + B].astype(F32)
        prev = lats[l, c, UP, rows, cols].astype(F32)
        nxt = lats[l, c, DOWN, rows, cols].astype(F32)
        product = qbuf[pl.ds(pl.multiple_of(c * buf.shape[2] + row, 16), 16), cols]
        return [
            product[h] + stencil(cur[h], prev[h], nxt[h]) for h in (slice(0, 8), slice(8, 16))
        ]

    def forward_finish(l, c):
        wait_halo(forward, l, c, (UP, DOWN))

        def one(fi):
            f = c * NFC + fi
            for cols in pieces:
                coefs = coef[l, :, cols]
                new = []
                for s in range(2):
                    q_re, q_im = lateral(hbuf, hlat, l, c, (fi * 2 + s) * 16, cols)
                    re = phased[l, f, s, 0, :, cols] - coefs * q_im
                    im = phased[l, f, s, 1, :, cols] + coefs * q_re
                    new.append((re, im))
                    if l + 1 < L:
                        store_phase(
                            l + 1,
                            c,
                            fi,
                            s,
                            cols,
                            re.astype(BF16).astype(F32),
                            im.astype(BF16).astype(F32),
                        )
                state[l, f, 0, :, cols] = new[0][0]
                state[l, f, 1, :, cols] = new[0][1]
                product = new[0][0] * new[1][0] + new[0][1] * new[1][1]
                if c == 0 and isinstance(fi, int) and fi == 0:
                    img[l, :, cols] = product
                else:
                    img[l, :, cols] += product

        if NFC > 2 and c == 0:
            img[l] = jnp.zeros(img.shape[1:], F32)
        loop(NFC, one)
        if c == C - 1:
            img[l] = img[l] * (1.0 / NF)

    results = ((img, image_ref), (grad, grad_ref))

    def own_copy(a, l):
        return pltpu.make_async_copy(
            results[a][0].at[l], results[a][1].at[l % layers, :, mine], own_sem.at[a, l % layers]
        )

    def out_copy(a, l):
        owner = l // layers
        return pltpu.make_async_remote_copy(
            src_ref=results[a][0].at[l],
            dst_ref=results[a][1].at[l % layers, :, mine],
            send_sem=osend.at[a, l],
            recv_sem=orecv.at[a, l % layers, lax.rem(owner - me + D, D)],
            device_id={"depth": owner},
            device_id_type=MESH,
        )

    def deliver(a, l):
        @pl.when(me == l // layers)
        def _():
            own_copy(a, l).start()

        @pl.when(me != l // layers)
        def _():
            out_copy(a, l).start()

    def begin_adjoint(l, c, fi, cols, mu):
        f = c * NFC + fi
        weight = mask[l, :, cols].astype(F32) * img[l, :, cols]
        coefs = coef[l, :, cols]
        scaled = []
        for part in range(2):
            value = weight * state[l, f, part, :, cols]
            if mu is not None:
                value = value + mu[part]
            adj[f, part, :, cols] = value
            scaled.append(coefs * value)
        rows = pl.ds(pl.multiple_of(fi * 16, 16), 16)
        gbuf[l, c, rows, cols.start + B : cols.stop + B] = jnp.concatenate(
            scaled, axis=0
        ).astype(BF16)

    def first_adjoint(c):
        def one(fi):
            for cols in pieces:
                begin_adjoint(L - 1, c, fi, cols, None)

        loop(NFC, one)

    def backward_finish(l, c):
        wait_halo(backward, l, c, (UP, DOWN))

        def one(fi):
            f = c * NFC + fi
            omega = omega_of(f)
            for cols in pieces:
                t_re, t_im = lateral(gbuf, glat, l, c, fi * 16, cols)
                back_re = adj[f, 0, :, cols] + t_im
                back_im = adj[f, 1, :, cols] - t_re
                term = omega * (
                    back_im * phased[l, f, 1, 0, :, cols] - back_re * phased[l, f, 1, 1, :, cols]
                )
                if c == 0 and isinstance(fi, int) and fi == 0:
                    grad[l, :, cols] = term
                else:
                    grad[l, :, cols] += term
                if l > 0:
                    cosine, sine = cosines[l, f, :, cols], sines[l, f, :, cols]
                    mu_re = back_re * cosine + back_im * sine
                    mu_im = back_im * cosine - back_re * sine
                    mu = [mu_re.astype(BF16).astype(F32), mu_im.astype(BF16).astype(F32)]
                    begin_adjoint(l - 1, c, fi, cols, mu)

        if NFC > 2 and c == 0:
            grad[l] = jnp.zeros(grad.shape[1:], F32)
        loop(NFC, one)
        if c == C - 1:
            grad[l] = grad[l] * (1.0 / NF)

    def arrive(a, l):
        if l % layers == 0:
            s = lax.rem(me - l // layers + D, D)

            @pl.when(s != 0)
            def _():
                table_wait(a, s)

    def transpose(j, k):
        i = j + k - 1
        if k != 1 and not 0 <= j < nb:
            value = band_edge[0 if j < 0 else 1]
        else:
            value = band[j // G, j % G + k, :, (j % G) * B : (j % G + 1) * B]
        band_t[i // G, i % G + 2 - k, :, (i % G) * B : (i % G + 1) * B] = (
            value.astype(F32).T.astype(BF16)
        )

    for copy in local[6:]:
        copy.wait()
    for j in range(nb):
        for k in range(3):
            if 0 <= j + k - 1 < nb:
                transpose(j, k)
    local[0].wait()
    local[5].wait()
    arrive(0, 0)
    angles(0)
    local[1].wait()
    local[2].wait()
    for c in range(C):
        first_phase(c)
        send_halo(forward, 0, c)
    late_sends()
    for l in range(1, L):
        arrive(0, l)
        angles(l)
    local[3].wait()
    arrive(1, 0)
    for l in range(L):
        if l > 0:
            arrive(1, l)
        band_products(forward, band, l, R)
        if l == L - 1:
            for way in (LEFT, RIGHT):

                @pl.when(exists[way])
                def _():
                    edge_copy(opposite[way]).wait_recv()

            transpose(-1, 2)
            transpose(nb, 0)
        for c in range(C):
            forward_finish(l, c)
            if l + 1 < L:
                send_halo(forward, l + 1, c)
        if l + 1 < L:
            deliver(0, l)
    local[4].wait()
    for l in range(L):
        arrive(2, l)
    for c in range(C):
        first_adjoint(c)
        send_halo(backward, L - 1, c)
    deliver(0, L - 1)
    for l in reversed(range(L)):
        band_products(backward, band_t, l, RB)
        for c in range(C):
            backward_finish(l, c)
            if l > 0:
                send_halo(backward, l - 1, c)
        deliver(1, l)

    for l in range(L):
        for c in range(C):
            for way in DIRS:

                @pl.when(exists[way])
                def _():
                    halo_copy(*forward, l, c, way).wait_send()
                    halo_copy(*backward, l, c, way).wait_send()

    for s in range(1, D):
        for a in range(3):
            table_copy(a, s).wait_send()
    for way in (LEFT, RIGHT):

        @pl.when(exists[way])
        def _():
            edge_copy(way).wait_send()

    for a in range(2):
        for l in range(L):

            @pl.when(me == l // layers)
            def _():
                own_copy(a, l).wait()

            @pl.when(me != l // layers)
            def _():
                out_copy(a, l).wait_send()

        for i in range(layers):
            for s in range(1, D):
                source = lax.rem(me - s + D, D)
                theirs = pl.ds(pl.multiple_of(source * W, B), W)
                pltpu.make_async_remote_copy(
                    src_ref=results[a][0].at[i],
                    dst_ref=results[a][1].at[i, :, theirs],
                    send_sem=osend.at[a, i],
                    recv_sem=orecv.at[a, i, s],
                    device_id={"depth": source},
                    device_id_type=MESH,
                ).wait_recv()


def publish(image_in, grad_in, image_out, grad_out, sems):
    copies = [
        pltpu.make_async_copy(image_in, image_out, sems.at[0]),
        pltpu.make_async_copy(grad_in, grad_out, sems.at[1]),
    ]
    for copy in copies:
        copy.start()
    for copy in copies:
        copy.wait()


def per_device(source_field, receiver_field, freq_index, slowness, ffd_coef, band, image_mask):
    D, LATS = lax.axis_size("depth"), lax.axis_size("lat")
    NF, _, height, width = source_field.shape
    layers = slowness.shape[0]
    L = layers * D
    nb, _, B, _ = band.shape
    W = width // D
    assert height == HALO and W == nb * B
    C = 2 if NF % 2 == 0 else 1
    NFC = NF // C
    G = 2 if nb % 2 == 0 else 1
    dims = (D, LATS, L, layers, NF, C, nb, G, B, W)
    R, RB = NFC * 32, NFC * 16
    dma = pltpu.SemaphoreType.DMA
    in_hbm = pl.BlockSpec(memory_space=pltpu.HBM)
    tile = (height, W)
    scratch = [
        pltpu.SMEM((NF,), jnp.int32),
        pltpu.VMEM((2, NF, 2) + tile, BF16),
        pltpu.VMEM((L,) + tile, F32),
        pltpu.VMEM((L,) + tile, F32),
        pltpu.VMEM((L,) + tile, jnp.int32),
        pltpu.VMEM((nb // G, G + 2, B, G * B), BF16),
        pltpu.VMEM((nb // G, G + 2, B, G * B), BF16),
        pltpu.VMEM((2, B, B), BF16),
        pltpu.VMEM((L, NF) + tile, F32),
        pltpu.VMEM((L, NF) + tile, F32),
        pltpu.VMEM((L, NF, 2, 2) + tile, F32),
        pltpu.VMEM((L, NF, 2) + tile, F32),
        pltpu.VMEM((NF, 2) + tile, F32),
        pltpu.VMEM((L, C, R, W + 2 * B), BF16),
        pltpu.VMEM((L, C, 2, R, W), BF16),
        pltpu.VMEM((L, C, RB, W + 2 * B), BF16),
        pltpu.VMEM((L, C, 2, RB, W), BF16),
        pltpu.VMEM((C * R, W), F32),
        pltpu.VMEM((L,) + tile, F32),
        pltpu.VMEM((L,) + tile, F32),
        dma((L, C, 4)),
        dma((L, C, 4)),
        dma((L, C, 4)),
        dma((L, C, 4)),
        dma((3, D)),
        dma((3, D)),
        dma((2,)),
        dma((2,)),
        dma((2, L)),
        dma((2, layers, D)),
        dma((2, layers)),
        dma((6,)),
        dma((G,)),
    ]
    image, grad = pl.pallas_call(
        functools.partial(kernel, dims),
        out_shape=[jax.ShapeDtypeStruct(slowness.shape, F32)] * 2,
        in_specs=[in_hbm] * 7,
        out_specs=[in_hbm] * 2,
        scratch_shapes=scratch,
        compiler_params=pltpu.CompilerParams(
            collective_id=0, has_side_effects=True, vmem_limit_bytes=VMEM_BYTES
        ),
    )(freq_index, source_field, receiver_field, slowness, ffd_coef, image_mask, band.reshape(nb // G, G, 3, B, B))
    return pl.pallas_call(
        publish,
        out_shape=[jax.ShapeDtypeStruct(slowness.shape, F32)] * 2,
        in_specs=[in_hbm] * 2,
        out_specs=[in_hbm] * 2,
        scratch_shapes=[dma((2,))],
        compiler_params=pltpu.CompilerParams(vmem_limit_bytes=VMEM_BYTES),
    )(image, grad)


def solution(mesh):
    return jax.shard_map(
        per_device,
        mesh=mesh,
        in_specs=(
            P(None, None, "lat", None),
            P(None, None, "lat", None),
            P(),
            P("depth", "lat", None),
            P("depth", "lat", None),
            P("depth", None, None, None),
            P("depth", "lat", None),
        ),
        out_specs=(P("depth", "lat", None), P("depth", "lat", None)),
        check_vma=False,
    )
```

```python
import functools

import jax
import jax.numpy as jnp
from jax import lax
from jax.experimental import pallas as pl
from jax.experimental.pallas import tpu as pltpu
from jax.sharding import PartitionSpec as P

HALO = 8
VMEM_BYTES = 64 * 1024 * 1024 - 208 * 1024
F32 = jnp.float32
BF16 = jnp.bfloat16
WEIGHTS = [0.0] + [0.25 / k for k in range(1, HALO + 1)]
UP, DOWN, LEFT, RIGHT = range(4)


def sincos(theta):
    turns = jnp.floor(theta * 0.6366197723675814 + 0.5)
    rest = theta - turns * 1.5703125
    rest = rest - turns * 4.837512969970703125e-4
    rest = rest - turns * 7.54978995489188216e-8
    square = rest * rest
    sine = rest + rest * square * (
        -1.6666654611e-1 + square * (8.3321608736e-3 + square * -1.9515295891e-4)
    )
    cosine = (
        1.0
        - 0.5 * square
        + square
        * square
        * (
            4.166664568298827e-2
            + square * (-1.388731625493765e-3 + square * 2.443315711809948e-5)
        )
    )
    quadrant = turns.astype(jnp.int32)
    odd = (quadrant & 1) == 1
    sin_out = jnp.where(odd, cosine, sine)
    cos_out = jnp.where(odd, sine, cosine)
    sin_out = jnp.where((quadrant & 2) == 2, -sin_out, sin_out)
    cos_out = jnp.where(((quadrant + 1) & 2) == 2, -cos_out, cos_out)
    return sin_out, cos_out


def stencil(cur, prev, nxt):
    row = lax.broadcasted_iota(jnp.int32, cur.shape, 0)
    total = WEIGHTS[HALO] * (prev + nxt) - 2.0 * sum(WEIGHTS) * cur
    for k in range(1, HALO):
        inside = row >= k
        near = jnp.where(inside, WEIGHTS[k], WEIGHTS[HALO - k])
        far = jnp.where(inside, WEIGHTS[HALO - k], WEIGHTS[k])
        mixed = near * cur + far * jnp.where(inside, prev, nxt)
        total = total + pltpu.roll(mixed, HALO - k, 0)
    return total


def loop(count, body):
    if count <= 2:
        for i in range(count):
            body(i)
    else:
        lax.fori_loop(0, count, lambda i, c: (body(i), c)[1], 0)


def kernel(
    dims,
    freq_hbm,
    src_ref,
    rcv_ref,
    slow_ref,
    coef_ref,
    mask_ref,
    band_ref,
    image_ref,
    grad_ref,
    freq_ref,
    fields,
    slow,
    coef,
    mask,
    band,
    band_t,
    band_edge,
    sines,
    cosines,
    phased,
    state,
    adj,
    hbuf,
    hlat,
    gbuf,
    glat,
    qbuf,
    img,
    grad,
    fsend,
    frecv,
    bsend,
    brecv,
    rsend,
    rrecv,
    esend,
    erecv,
    osend,
    orecv,
    own_sem,
    loc_sem,
    band_sem,
):
    D, LATS, L, layers, NF, C, nb, G, B, W = dims
    NFC = NF // C
    me = lax.axis_index("depth")
    lat = lax.axis_index("lat")
    first = pl.multiple_of(me * W, B)
    mine = pl.ds(first, W)
    exists = {UP: lat > 0, DOWN: lat < LATS - 1, LEFT: me > 0, RIGHT: me < D - 1}
    target = {
        UP: {"lat": lat - 1},
        DOWN: {"lat": lat + 1},
        LEFT: {"depth": me - 1},
        RIGHT: {"depth": me + 1},
    }
    opposite = {UP: DOWN, DOWN: UP, LEFT: RIGHT, RIGHT: LEFT}
    DIRS = (LEFT, RIGHT, UP, DOWN)
    MESH = pl.DeviceIdType.MESH

    own_levels = pl.ds(me * layers, layers)
    local = [
        pltpu.make_async_copy(slow_ref.at[:, :, mine], slow.at[own_levels], loc_sem.at[0]),
        pltpu.make_async_copy(src_ref.at[:, :, :, mine], fields.at[0], loc_sem.at[1]),
        pltpu.make_async_copy(rcv_ref.at[:, :, :, mine], fields.at[1], loc_sem.at[2]),
        pltpu.make_async_copy(coef_ref.at[:, :, mine], coef.at[own_levels], loc_sem.at[3]),
        pltpu.make_async_copy(mask_ref.at[:, :, mine], mask.at[own_levels], loc_sem.at[4]),
        pltpu.make_async_copy(freq_hbm, freq_ref, loc_sem.at[5]),
    ] + [
        pltpu.make_async_copy(
            band_ref.at[:, e], band.at[:, e : e + 3, :, e * B : (e + 1) * B], band_sem.at[e]
        )
        for e in range(G)
    ]
    for copy in local:
        copy.start()

    barrier = pltpu.get_barrier_semaphore()
    for way in (UP, DOWN):

        @pl.when(exists[way])
        def _():
            pl.semaphore_signal(barrier, inc=1, device_id=target[way], device_id_type=MESH)

    for s in range(1, D):
        pl.semaphore_signal(
            barrier, inc=1, device_id={"depth": lax.rem(me + s, D)}, device_id_type=MESH
        )
    for way in (UP, DOWN):

        @pl.when(jnp.logical_not(exists[way]))
        def _():
            hlat[:, :, way] = jnp.zeros(hlat.shape[:2] + hlat.shape[3:], BF16)
            glat[:, :, way] = jnp.zeros(glat.shape[:2] + glat.shape[3:], BF16)

    for way, start, slot in ((LEFT, 0, 0), (RIGHT, W + B, 1)):

        @pl.when(jnp.logical_not(exists[way]))
        def _():
            hbuf[:, :, :, start : start + B] = jnp.zeros(hbuf.shape[:3] + (B,), BF16)
            gbuf[:, :, :, start : start + B] = jnp.zeros(gbuf.shape[:3] + (B,), BF16)
            band_edge[slot] = jnp.zeros((B, B), BF16)

    for matrix in (band, band_t):
        for e in range(G):
            for r in range(G + 2):
                if not e <= r < e + 3:
                    matrix[:, r, :, e * B : (e + 1) * B] = jnp.zeros((nb // G, B, B), BF16)

    pl.semaphore_wait(
        barrier, (D - 1) + exists[UP].astype(jnp.int32) + exists[DOWN].astype(jnp.int32)
    )

    tables = ((slow_ref, slow), (coef_ref, coef), (mask_ref, mask))

    def table_copy(a, s):
        peer = lax.rem(me + s, D)
        return pltpu.make_async_remote_copy(
            src_ref=tables[a][0].at[:, :, pl.ds(pl.multiple_of(peer * W, B), W)],
            dst_ref=tables[a][1].at[own_levels],
            send_sem=rsend.at[a, s],
            recv_sem=rrecv.at[a, s],
            device_id={"depth": peer},
            device_id_type=MESH,
        )

    def table_wait(a, s):
        source = lax.rem(me - s + D, D)
        pltpu.make_async_remote_copy(
            src_ref=tables[a][1].at[pl.ds(source * layers, layers)],
            dst_ref=tables[a][1].at[pl.ds(source * layers, layers)],
            send_sem=rsend.at[a, s],
            recv_sem=rrecv.at[a, s],
            device_id={"depth": source},
            device_id_type=MESH,
        ).wait_recv()

    def edge_copy(way):
        j, k, slot = (0, 0, 1) if way == LEFT else (nb - 1, 2, 0)
        return pltpu.make_async_remote_copy(
            src_ref=band_ref.at[j // G, j % G, k],
            dst_ref=band_edge.at[slot],
            send_sem=esend.at[slot],
            recv_sem=erecv.at[slot],
            device_id=target[way],
            device_id_type=MESH,
        )

    for a in (0, 1):
        for s in range(1, D):
            table_copy(a, s).start()

    def late_sends():
        for s in range(1, D):
            table_copy(2, s).start()
        for way in (LEFT, RIGHT):

            @pl.when(exists[way])
            def _():
                edge_copy(way).start()

    def halo_copy(buf, lats, ssem, rsem, l, c, way):
        if way in (UP, DOWN):
            src = buf.at[l, c, :, pl.ds(B, W)]
            dst = lats.at[l, c, opposite[way]]
        else:
            src = buf.at[l, c, :, pl.ds(B if way == LEFT else W, B)]
            dst = buf.at[l, c, :, pl.ds(W + B if way == LEFT else 0, B)]
        return pltpu.make_async_remote_copy(
            src_ref=src,
            dst_ref=dst,
            send_sem=ssem.at[l, c, way],
            recv_sem=rsem.at[l, c, opposite[way]],
            device_id=target[way],
            device_id_type=MESH,
        )

    def send_halo(args, l, c):
        for way in DIRS:

            @pl.when(exists[way])
            def _():
                halo_copy(*args, l, c, way).start()

    def wait_halo(args, l, c, ways):
        for way in ways:

            @pl.when(exists[way])
            def _():
                halo_copy(*args, l, c, opposite[way]).wait_recv()

    forward = (hbuf, hlat, fsend, frecv)
    backward = (gbuf, glat, bsend, brecv)

    CW = min(W, 512)
    pieces = [slice(x, x + CW) for x in range(0, W, CW)]

    def omega_of(f):
        return 0.1 * (freq_ref[f].astype(F32) + 1.0)

    def angles(l):
        def one(f):
            omega = omega_of(f)
            for cols in pieces:
                sines[l, f, :, cols], cosines[l, f, :, cols] = sincos(omega * slow[l, :, cols])

        loop(NF, one)

    def store_phase(l, c, fi, s, cols, re, im):
        f = c * NFC + fi
        cosine, sine = cosines[l, f, :, cols], sines[l, f, :, cols]
        phase_re = re * cosine - im * sine
        phase_im = re * sine + im * cosine
        phased[l, f, s, 0, :, cols] = phase_re
        phased[l, f, s, 1, :, cols] = phase_im
        rows = pl.ds(pl.multiple_of((fi * 2 + s) * 16, 16), 16)
        inner = slice(cols.start + B, cols.stop + B)
        hbuf[l, c, rows, inner] = jnp.concatenate([phase_re, phase_im], axis=0).astype(BF16)

    def first_phase(c):
        def one(fi):
            f = c * NFC + fi
            for s in range(2):
                for cols in pieces:
                    re = fields[s, f, 0, :, cols].astype(F32)
                    im = fields[s, f, 1, :, cols].astype(F32)
                    store_phase(0, c, fi, s, cols, re, im)

        loop(NFC, one)

    R, RB = NFC * 32, NFC * 16

    def band_groups(buf, matrix, l, groups, rows):
        for p in groups:
            left = p * G * B
            qbuf[: C * rows, left : left + G * B] = jnp.dot(
                buf[l, :, :, left : left + (G + 2) * B].reshape(C * rows, (G + 2) * B),
                matrix[p].reshape((G + 2) * B, G * B),
                preferred_element_type=F32,
            )

    inner_groups = range(1, nb // G - 1)
    outer_groups = sorted({0, nb // G - 1})

    def band_products(args, matrix, l, rows):
        band_groups(args[0], matrix, l, inner_groups, rows)
        for c in range(C):
            wait_halo(args, l, c, (LEFT, RIGHT))
        band_groups(args[0], matrix, l, outer_groups, rows)

    def lateral(buf, lats, l, c, row, cols):
        rows = pl.ds(pl.multiple_of(row, 16), 16)
        cur = buf[l, c, rows, cols.start + B : cols.stop + B].astype(F32)
        prev = lats[l, c, UP, rows, cols].astype(F32)
        nxt = lats[l, c, DOWN, rows, cols].astype(F32)
        product = qbuf[pl.ds(pl.multiple_of(c * buf.shape[2] + row, 16), 16), cols]
        return [
            product[h] + stencil(cur[h], prev[h], nxt[h]) for h in (slice(0, 8), slice(8, 16))
        ]

    def forward_finish(l, c):
        wait_halo(forward, l, c, (UP, DOWN))

        def one(fi):
            f = c * NFC + fi
            for cols in pieces:
                coefs = coef[l, :, cols]
                new = []
                for s in range(2):
                    q_re, q_im = lateral(hbuf, hlat, l, c, (fi * 2 + s) * 16, cols)
                    re = phased[l, f, s, 0, :, cols] - coefs * q_im
                    im = phased[l, f, s, 1, :, cols] + coefs * q_re
                    new.append((re, im))
                    if l + 1 < L:
                        store_phase(
                            l + 1,
                            c,
                            fi,
                            s,
                            cols,
                            re.astype(BF16).astype(F32),
                            im.astype(BF16).astype(F32),
                        )
                state[l, f, 0, :, cols] = new[0][0]
                state[l, f, 1, :, cols] = new[0][1]
                product = new[0][0] * new[1][0] + new[0][1] * new[1][1]
                if c == 0 and isinstance(fi, int) and fi == 0:
                    img[l, :, cols] = product
                else:
                    img[l, :, cols] += product

        if NFC > 2 and c == 0:
            img[l] = jnp.zeros(img.shape[1:], F32)
        loop(NFC, one)
        if c == C - 1:
            img[l] = img[l] * (1.0 / NF)

    results = ((img, image_ref), (grad, grad_ref))

    def own_copy(a, l):
        return pltpu.make_async_copy(
            results[a][0].at[l], results[a][1].at[l % layers, :, mine], own_sem.at[a, l % layers]
        )

    def out_copy(a, l):
        owner = l // layers
        return pltpu.make_async_remote_copy(
            src_ref=results[a][0].at[l],
            dst_ref=results[a][1].at[l % layers, :, mine],
            send_sem=osend.at[a, l],
            recv_sem=orecv.at[a, l % layers, lax.rem(owner - me + D, D)],
            device_id={"depth": owner},
            device_id_type=MESH,
        )

    def deliver(a, l):
        @pl.when(me == l // layers)
        def _():
            own_copy(a, l).start()

        @pl.when(me != l // layers)
        def _():
            out_copy(a, l).start()

    def begin_adjoint(l, c, fi, cols, mu):
        f = c * NFC + fi
        weight = mask[l, :, cols].astype(F32) * img[l, :, cols]
        coefs = coef[l, :, cols]
        scaled = []
        for part in range(2):
            value = weight * state[l, f, part, :, cols]
            if mu is not None:
                value = value + mu[part]
            adj[f, part, :, cols] = value
            scaled.append(coefs * value)
        rows = pl.ds(pl.multiple_of(fi * 16, 16), 16)
        gbuf[l, c, rows, cols.start + B : cols.stop + B] = jnp.concatenate(
            scaled, axis=0
        ).astype(BF16)

    def first_adjoint(c):
        def one(fi):
            for cols in pieces:
                begin_adjoint(L - 1, c, fi, cols, None)

        loop(NFC, one)

    def backward_finish(l, c):
        wait_halo(backward, l, c, (UP, DOWN))

        def one(fi):
            f = c * NFC + fi
            omega = omega_of(f)
            for cols in pieces:
                t_re, t_im = lateral(gbuf, glat, l, c, fi * 16, cols)
                back_re = adj[f, 0, :, cols] + t_im
                back_im = adj[f, 1, :, cols] - t_re
                term = omega * (
                    back_im * phased[l, f, 1, 0, :, cols] - back_re * phased[l, f, 1, 1, :, cols]
                )
                if c == 0 and isinstance(fi, int) and fi == 0:
                    grad[l, :, cols] = term
                else:
                    grad[l, :, cols] += term
                if l > 0:
                    cosine, sine = cosines[l, f, :, cols], sines[l, f, :, cols]
                    mu_re = back_re * cosine + back_im * sine
                    mu_im = back_im * cosine - back_re * sine
                    mu = [mu_re.astype(BF16).astype(F32), mu_im.astype(BF16).astype(F32)]
                    begin_adjoint(l - 1, c, fi, cols, mu)

        if NFC > 2 and c == 0:
            grad[l] = jnp.zeros(grad.shape[1:], F32)
        loop(NFC, one)
        if c == C - 1:
            grad[l] = grad[l] * (1.0 / NF)

    def arrive(a, l):
        if l % layers == 0:
            s = lax.rem(me - l // layers + D, D)

            @pl.when(s != 0)
            def _():
                table_wait(a, s)

    def transpose(j, k):
        i = j + k - 1
        if k != 1 and not 0 <= j < nb:
            value = band_edge[0 if j < 0 else 1]
        else:
            value = band[j // G, j % G + k, :, (j % G) * B : (j % G + 1) * B]
        band_t[i // G, i % G + 2 - k, :, (i % G) * B : (i % G + 1) * B] = (
            value.astype(F32).T.astype(BF16)
        )

    for copy in local[6:]:
        copy.wait()
    for j in range(nb):
        for k in range(3):
            if 0 <= j + k - 1 < nb:
                transpose(j, k)
    local[0].wait()
    local[5].wait()
    arrive(0, 0)
    angles(0)
    local[1].wait()
    local[2].wait()
    for c in range(C):
        first_phase(c)
        send_halo(forward, 0, c)
    late_sends()
    for l in range(1, L):
        arrive(0, l)
        angles(l)
    local[3].wait()
    arrive(1, 0)
    for l in range(L):
        if l > 0:
            arrive(1, l)
        band_products(forward, band, l, R)
        if l == L - 1:
            for way in (LEFT, RIGHT):

                @pl.when(exists[way])
                def _():
                    edge_copy(opposite[way]).wait_recv()

            transpose(-1, 2)
            transpose(nb, 0)
        for c in range(C):
            forward_finish(l, c)
            if l + 1 < L:
                send_halo(forward, l + 1, c)
        if l + 1 < L:
            deliver(0, l)
    local[4].wait()
    for l in range(L):
        arrive(2, l)
    for c in range(C):
        first_adjoint(c)
        send_halo(backward, L - 1, c)
    deliver(0, L - 1)
    for l in reversed(range(L)):
        band_products(backward, band_t, l, RB)
        for c in range(C):
            backward_finish(l, c)
            if l > 0:
                send_halo(backward, l - 1, c)
        deliver(1, l)

    for l in range(L):
        for c in range(C):
            for way in DIRS:

                @pl.when(exists[way])
                def _():
                    halo_copy(*forward, l, c, way).wait_send()
                    halo_copy(*backward, l, c, way).wait_send()

    for s in range(1, D):
        for a in range(3):
            table_copy(a, s).wait_send()
    for way in (LEFT, RIGHT):

        @pl.when(exists[way])
        def _():
            edge_copy(way).wait_send()

    for a in range(2):
        for l in range(L):

            @pl.when(me == l // layers)
            def _():
                own_copy(a, l).wait()

            @pl.when(me != l // layers)
            def _():
                out_copy(a, l).wait_send()

        for i in range(layers):
            for s in range(1, D):
                source = lax.rem(me - s + D, D)
                theirs = pl.ds(pl.multiple_of(source * W, B), W)
                pltpu.make_async_remote_copy(
                    src_ref=results[a][0].at[i],
                    dst_ref=results[a][1].at[i, :, theirs],
                    send_sem=osend.at[a, i],
                    recv_sem=orecv.at[a, i, s],
                    device_id={"depth": source},
                    device_id_type=MESH,
                ).wait_recv()


def publish(image_in, grad_in, image_out, grad_out, sems):
    copies = [
        pltpu.make_async_copy(image_in, image_out, sems.at[0]),
        pltpu.make_async_copy(grad_in, grad_out, sems.at[1]),
    ]
    for copy in copies:
        copy.start()
    for copy in copies:
        copy.wait()


def per_device(source_field, receiver_field, freq_index, slowness, ffd_coef, band, image_mask):
    D, LATS = lax.axis_size("depth"), lax.axis_size("lat")
    NF, _, height, width = source_field.shape
    layers = slowness.shape[0]
    L = layers * D
    nb, _, B, _ = band.shape
    W = width // D
    assert height == HALO and W == nb * B
    C = 2 if NF % 2 == 0 else 1
    NFC = NF // C
    G = 2 if nb % 2 == 0 else 1
    dims = (D, LATS, L, layers, NF, C, nb, G, B, W)
    R, RB = NFC * 32, NFC * 16
    dma = pltpu.SemaphoreType.DMA
    anywhere = pl.BlockSpec(memory_space=pl.ANY)
    in_hbm = pl.BlockSpec(memory_space=pltpu.HBM)
    tile = (height, W)
    scratch = [
        pltpu.SMEM((NF,), jnp.int32),
        pltpu.VMEM((2, NF, 2) + tile, BF16),
        pltpu.VMEM((L,) + tile, F32),
        pltpu.VMEM((L,) + tile, F32),
        pltpu.VMEM((L,) + tile, jnp.int32),
        pltpu.VMEM((nb // G, G + 2, B, G * B), BF16),
        pltpu.VMEM((nb // G, G + 2, B, G * B), BF16),
        pltpu.VMEM((2, B, B), BF16),
        pltpu.VMEM((L, NF) + tile, F32),
        pltpu.VMEM((L, NF) + tile, F32),
        pltpu.VMEM((L, NF, 2, 2) + tile, F32),
        pltpu.VMEM((L, NF, 2) + tile, F32),
        pltpu.VMEM((NF, 2) + tile, F32),
        pltpu.VMEM((L, C, R, W + 2 * B), BF16),
        pltpu.VMEM((L, C, 2, R, W), BF16),
        pltpu.VMEM((L, C, RB, W + 2 * B), BF16),
        pltpu.VMEM((L, C, 2, RB, W), BF16),
        pltpu.VMEM((C * R, W), F32),
        pltpu.VMEM((L,) + tile, F32),
        pltpu.VMEM((L,) + tile, F32),
        dma((L, C, 4)),
        dma((L, C, 4)),
        dma((L, C, 4)),
        dma((L, C, 4)),
        dma((3, D)),
        dma((3, D)),
        dma((2,)),
        dma((2,)),
        dma((2, L)),
        dma((2, layers, D)),
        dma((2, layers)),
        dma((6,)),
        dma((G,)),
    ]
    image, grad = pl.pallas_call(
        functools.partial(kernel, dims),
        out_shape=[pltpu.VMEM(slowness.shape, F32)] * 2,
        in_specs=[in_hbm] * 7,
        out_specs=[anywhere] * 2,
        scratch_shapes=scratch,
        compiler_params=pltpu.CompilerParams(
            collective_id=0, has_side_effects=True, vmem_limit_bytes=VMEM_BYTES
        ),
    )(freq_index, source_field, receiver_field, slowness, ffd_coef, image_mask, band.reshape(nb // G, G, 3, B, B))
    return pl.pallas_call(
        publish,
        out_shape=[jax.ShapeDtypeStruct(slowness.shape, F32)] * 2,
        in_specs=[anywhere] * 2,
        out_specs=[in_hbm] * 2,
        scratch_shapes=[dma((2,))],
        compiler_params=pltpu.CompilerParams(vmem_limit_bytes=1024 * 1024),
    )(image, grad)


def solution(mesh):
    return jax.shard_map(
        per_device,
        mesh=mesh,
        in_specs=(
            P(None, None, "lat", None),
            P(None, None, "lat", None),
            P(),
            P("depth", "lat", None),
            P("depth", "lat", None),
            P("depth", None, None, None),
            P("depth", "lat", None),
        ),
        out_specs=(P("depth", "lat", None), P("depth", "lat", None)),
        check_vma=False,
    )
```

```python
import functools

import jax
import jax.numpy as jnp
from jax import lax
from jax.experimental import pallas as pl
from jax.experimental.pallas import tpu as pltpu
from jax.sharding import PartitionSpec as P

HALO = 8
VMEM_BYTES = 64 * 1024 * 1024 - 208 * 1024
F32 = jnp.float32
BF16 = jnp.bfloat16
WEIGHTS = [0.0] + [0.25 / k for k in range(1, HALO + 1)]
UP, DOWN, LEFT, RIGHT = range(4)


def sincos(theta):
    turns = jnp.floor(theta * 0.6366197723675814 + 0.5)
    rest = theta - turns * 1.5703125
    rest = rest - turns * 4.837512969970703125e-4
    rest = rest - turns * 7.54978995489188216e-8
    square = rest * rest
    sine = rest + rest * square * (
        -1.6666654611e-1 + square * (8.3321608736e-3 + square * -1.9515295891e-4)
    )
    cosine = (
        1.0
        - 0.5 * square
        + square
        * square
        * (
            4.166664568298827e-2
            + square * (-1.388731625493765e-3 + square * 2.443315711809948e-5)
        )
    )
    quadrant = turns.astype(jnp.int32)
    odd = (quadrant & 1) == 1
    sin_out = jnp.where(odd, cosine, sine)
    cos_out = jnp.where(odd, sine, cosine)
    sin_out = jnp.where((quadrant & 2) == 2, -sin_out, sin_out)
    cos_out = jnp.where(((quadrant + 1) & 2) == 2, -cos_out, cos_out)
    return sin_out, cos_out


def stencil_matrix(rows):
    shape = (rows, 3 * rows)
    out = lax.broadcasted_iota(jnp.int32, shape, 0)
    source = lax.broadcasted_iota(jnp.int32, shape, 1)
    tile = (source >= rows).astype(jnp.int32) + (source >= 2 * rows).astype(jnp.int32) - 1
    source = source - (tile + 1) * rows
    same = (out >> 3) == (source >> 3)
    distance = jnp.abs(tile * HALO + (source & 7) - (out & 7))
    weight = jnp.where(distance == 0, -2.0 * sum(WEIGHTS), 0.0)
    for k in range(1, HALO + 1):
        weight = jnp.where(distance == k, WEIGHTS[k], weight)
    weight = jnp.where(same, weight, 0.0)
    high = weight.astype(BF16)
    return jnp.concatenate([high, (weight - high.astype(F32)).astype(BF16)], axis=0)


def loop(count, body):
    if count <= 2:
        for i in range(count):
            body(i)
    else:
        lax.fori_loop(0, count, lambda i, c: (body(i), c)[1], 0)


def kernel(
    dims,
    freq_hbm,
    src_ref,
    rcv_ref,
    slow_ref,
    coef_ref,
    mask_ref,
    band_ref,
    image_ref,
    grad_ref,
    freq_ref,
    fields,
    slow,
    coef,
    mask,
    band,
    band_t,
    band_edge,
    sines,
    cosines,
    phased,
    state,
    adj,
    hbuf,
    gbuf,
    hmat,
    gmat,
    qbuf,
    img,
    grad,
    fsend,
    frecv,
    bsend,
    brecv,
    rsend,
    rrecv,
    esend,
    erecv,
    osend,
    orecv,
    own_sem,
    loc_sem,
    band_sem,
):
    D, LATS, L, layers, NF, C, nb, G, B, W = dims
    NFC = NF // C
    R, RB = NFC * 32, NFC * 16
    me = lax.axis_index("depth")
    lat = lax.axis_index("lat")
    first = pl.multiple_of(me * W, B)
    mine = pl.ds(first, W)
    exists = {UP: lat > 0, DOWN: lat < LATS - 1, LEFT: me > 0, RIGHT: me < D - 1}
    target = {
        UP: {"lat": lat - 1},
        DOWN: {"lat": lat + 1},
        LEFT: {"depth": me - 1},
        RIGHT: {"depth": me + 1},
    }
    opposite = {UP: DOWN, DOWN: UP, LEFT: RIGHT, RIGHT: LEFT}
    DIRS = (LEFT, RIGHT, UP, DOWN)
    MESH = pl.DeviceIdType.MESH

    own_levels = pl.ds(me * layers, layers)
    local = [
        pltpu.make_async_copy(slow_ref.at[:, :, mine], slow.at[own_levels], loc_sem.at[0]),
        pltpu.make_async_copy(src_ref.at[:, :, :, mine], fields.at[0], loc_sem.at[1]),
        pltpu.make_async_copy(rcv_ref.at[:, :, :, mine], fields.at[1], loc_sem.at[2]),
        pltpu.make_async_copy(coef_ref.at[:, :, mine], coef.at[own_levels], loc_sem.at[3]),
        pltpu.make_async_copy(mask_ref.at[:, :, mine], mask.at[own_levels], loc_sem.at[4]),
        pltpu.make_async_copy(freq_hbm, freq_ref, loc_sem.at[5]),
    ] + [
        pltpu.make_async_copy(
            band_ref.at[:, e], band.at[:, e : e + 3, :, e * B : (e + 1) * B], band_sem.at[e]
        )
        for e in range(G)
    ]
    for copy in local:
        copy.start()

    barrier = pltpu.get_barrier_semaphore()
    for way in (UP, DOWN):

        @pl.when(exists[way])
        def _():
            pl.semaphore_signal(barrier, inc=1, device_id=target[way], device_id_type=MESH)

    for s in range(1, D):
        pl.semaphore_signal(
            barrier, inc=1, device_id={"depth": lax.rem(me + s, D)}, device_id_type=MESH
        )
    for way in (UP, DOWN):

        @pl.when(jnp.logical_not(exists[way]))
        def _():
            for buf, rows in ((hbuf, R), (gbuf, RB)):
                start = 0 if way == UP else 2 * rows
                buf[:, :, start : start + rows, B : B + W] = jnp.zeros((L, C, rows, W), BF16)

    for way, start, slot in ((LEFT, 0, 0), (RIGHT, W + B, 1)):

        @pl.when(jnp.logical_not(exists[way]))
        def _():
            for buf, rows in ((hbuf, R), (gbuf, RB)):
                buf[:, :, rows : 2 * rows, start : start + B] = jnp.zeros((L, C, rows, B), BF16)
            band_edge[slot] = jnp.zeros((B, B), BF16)

    hmat[...] = stencil_matrix(R)
    gmat[...] = stencil_matrix(RB)
    for matrix in (band, band_t):
        for e in range(G):
            for r in range(G + 2):
                if not e <= r < e + 3:
                    matrix[:, r, :, e * B : (e + 1) * B] = jnp.zeros((nb // G, B, B), BF16)

    pl.semaphore_wait(
        barrier, (D - 1) + exists[UP].astype(jnp.int32) + exists[DOWN].astype(jnp.int32)
    )

    tables = ((slow_ref, slow), (coef_ref, coef), (mask_ref, mask))

    def table_copy(a, s):
        peer = lax.rem(me + s, D)
        return pltpu.make_async_remote_copy(
            src_ref=tables[a][0].at[:, :, pl.ds(pl.multiple_of(peer * W, B), W)],
            dst_ref=tables[a][1].at[own_levels],
            send_sem=rsend.at[a, s],
            recv_sem=rrecv.at[a, s],
            device_id={"depth": peer},
            device_id_type=MESH,
        )

    def table_wait(a, s):
        source = lax.rem(me - s + D, D)
        pltpu.make_async_remote_copy(
            src_ref=tables[a][1].at[pl.ds(source * layers, layers)],
            dst_ref=tables[a][1].at[pl.ds(source * layers, layers)],
            send_sem=rsend.at[a, s],
            recv_sem=rrecv.at[a, s],
            device_id={"depth": source},
            device_id_type=MESH,
        ).wait_recv()

    def edge_copy(way):
        j, k, slot = (0, 0, 1) if way == LEFT else (nb - 1, 2, 0)
        return pltpu.make_async_remote_copy(
            src_ref=band_ref.at[j // G, j % G, k],
            dst_ref=band_edge.at[slot],
            send_sem=esend.at[slot],
            recv_sem=erecv.at[slot],
            device_id=target[way],
            device_id_type=MESH,
        )

    for a in (0, 1):
        for s in range(1, D):
            table_copy(a, s).start()

    def late_sends():
        for s in range(1, D):
            table_copy(2, s).start()
        for way in (LEFT, RIGHT):

            @pl.when(exists[way])
            def _():
                edge_copy(way).start()

    def halo_copy(buf, rows, ssem, rsem, l, c, way):
        own = pl.ds(rows, rows)
        if way in (UP, DOWN):
            src = buf.at[l, c, own, pl.ds(B, W)]
            dst = buf.at[l, c, pl.ds(2 * rows if way == UP else 0, rows), pl.ds(B, W)]
        else:
            src = buf.at[l, c, own, pl.ds(B if way == LEFT else W, B)]
            dst = buf.at[l, c, own, pl.ds(W + B if way == LEFT else 0, B)]
        return pltpu.make_async_remote_copy(
            src_ref=src,
            dst_ref=dst,
            send_sem=ssem.at[l, c, way],
            recv_sem=rsem.at[l, c, opposite[way]],
            device_id=target[way],
            device_id_type=MESH,
        )

    def send_halo(args, l, c):
        for way in DIRS:

            @pl.when(exists[way])
            def _():
                halo_copy(*args, l, c, way).start()

    def wait_halo(args, l, c, ways):
        for way in ways:

            @pl.when(exists[way])
            def _():
                halo_copy(*args, l, c, opposite[way]).wait_recv()

    forward = (hbuf, R, fsend, frecv)
    backward = (gbuf, RB, bsend, brecv)

    CW = min(W, 512)
    pieces = [slice(x, x + CW) for x in range(0, W, CW)]

    def omega_of(f):
        return 0.1 * (freq_ref[f].astype(F32) + 1.0)

    def angles(l):
        def one(f):
            omega = omega_of(f)
            for cols in pieces:
                sines[l, f, :, cols], cosines[l, f, :, cols] = sincos(omega * slow[l, :, cols])

        loop(NF, one)

    def store_phase(l, c, fi, s, cols, re, im):
        f = c * NFC + fi
        cosine, sine = cosines[l, f, :, cols], sines[l, f, :, cols]
        phase_re = re * cosine - im * sine
        phase_im = re * sine + im * cosine
        phased[l, f, s, 0, :, cols] = phase_re
        phased[l, f, s, 1, :, cols] = phase_im
        rows = pl.ds(pl.multiple_of(R + (fi * 2 + s) * 16, 16), 16)
        inner = slice(cols.start + B, cols.stop + B)
        hbuf[l, c, rows, inner] = jnp.concatenate([phase_re, phase_im], axis=0).astype(BF16)

    def first_phase(c):
        def one(fi):
            f = c * NFC + fi
            for s in range(2):
                for cols in pieces:
                    re = fields[s, f, 0, :, cols].astype(F32)
                    im = fields[s, f, 1, :, cols].astype(F32)
                    store_phase(0, c, fi, s, cols, re, im)

        loop(NFC, one)

    def band_groups(buf, matrix, l, groups, rows):
        for p in groups:
            left = p * G * B
            qbuf[: C * rows, left : left + G * B] = jnp.dot(
                buf[l, :, rows : 2 * rows, left : left + (G + 2) * B].reshape(C * rows, (G + 2) * B),
                matrix[p].reshape((G + 2) * B, G * B),
                preferred_element_type=F32,
            )

    inner_groups = range(1, nb // G - 1)
    outer_groups = sorted({0, nb // G - 1})

    def band_products(args, matrix, l, rows):
        band_groups(args[0], matrix, l, inner_groups, rows)
        for c in range(C):
            wait_halo(args, l, c, (LEFT, RIGHT))
        band_groups(args[0], matrix, l, outer_groups, rows)

    def add_stencil(buf, matrix, l, c, rows):
        own = slice(c * rows, (c + 1) * rows)
        for cols in pieces:
            both = jnp.dot(
                matrix[...],
                buf[l, c, :, cols.start + B : cols.stop + B],
                preferred_element_type=F32,
            )
            qbuf[own, cols] += both[:rows] + both[rows:]

    def lateral(rows, c, row, cols):
        product = qbuf[pl.ds(pl.multiple_of(c * rows + row, 16), 16), cols]
        return product[:8], product[8:]

    def forward_finish(l, c):
        wait_halo(forward, l, c, (UP, DOWN))
        add_stencil(hbuf, hmat, l, c, R)

        def one(fi):
            f = c * NFC + fi
            for cols in pieces:
                coefs = coef[l, :, cols]
                new = []
                for s in range(2):
                    q_re, q_im = lateral(R, c, (fi * 2 + s) * 16, cols)
                    re = phased[l, f, s, 0, :, cols] - coefs * q_im
                    im = phased[l, f, s, 1, :, cols] + coefs * q_re
                    new.append((re, im))
                    if l + 1 < L:
                        store_phase(
                            l + 1,
                            c,
                            fi,
                            s,
                            cols,
                            re.astype(BF16).astype(F32),
                            im.astype(BF16).astype(F32),
                        )
                state[l, f, 0, :, cols] = new[0][0]
                state[l, f, 1, :, cols] = new[0][1]
                product = new[0][0] * new[1][0] + new[0][1] * new[1][1]
                if c == 0 and isinstance(fi, int) and fi == 0:
                    img[l, :, cols] = product
                else:
                    img[l, :, cols] += product

        if NFC > 2 and c == 0:
            img[l] = jnp.zeros(img.shape[1:], F32)
        loop(NFC, one)
        if c == C - 1:
            img[l] = img[l] * (1.0 / NF)

    results = ((img, image_ref), (grad, grad_ref))

    def own_copy(a, l):
        return pltpu.make_async_copy(
            results[a][0].at[l], results[a][1].at[l % layers, :, mine], own_sem.at[a, l % layers]
        )

    def out_copy(a, l):
        owner = l // layers
        return pltpu.make_async_remote_copy(
            src_ref=results[a][0].at[l],
            dst_ref=results[a][1].at[l % layers, :, mine],
            send_sem=osend.at[a, l],
            recv_sem=orecv.at[a, l % layers, lax.rem(owner - me + D, D)],
            device_id={"depth": owner},
            device_id_type=MESH,
        )

    def deliver(a, l):
        @pl.when(me == l // layers)
        def _():
            own_copy(a, l).start()

        @pl.when(me != l // layers)
        def _():
            out_copy(a, l).start()

    def begin_adjoint(l, c, fi, cols, mu):
        f = c * NFC + fi
        weight = mask[l, :, cols].astype(F32) * img[l, :, cols]
        coefs = coef[l, :, cols]
        scaled = []
        for part in range(2):
            value = weight * state[l, f, part, :, cols]
            if mu is not None:
                value = value + mu[part]
            adj[f, part, :, cols] = value
            scaled.append(coefs * value)
        rows = pl.ds(pl.multiple_of(RB + fi * 16, 16), 16)
        gbuf[l, c, rows, cols.start + B : cols.stop + B] = jnp.concatenate(
            scaled, axis=0
        ).astype(BF16)

    def first_adjoint(c):
        def one(fi):
            for cols in pieces:
                begin_adjoint(L - 1, c, fi, cols, None)

        loop(NFC, one)

    def backward_finish(l, c):
        wait_halo(backward, l, c, (UP, DOWN))
        add_stencil(gbuf, gmat, l, c, RB)

        def one(fi):
            f = c * NFC + fi
            omega = omega_of(f)
            for cols in pieces:
                t_re, t_im = lateral(RB, c, fi * 16, cols)
                back_re = adj[f, 0, :, cols] + t_im
                back_im = adj[f, 1, :, cols] - t_re
                term = omega * (
                    back_im * phased[l, f, 1, 0, :, cols] - back_re * phased[l, f, 1, 1, :, cols]
                )
                if c == 0 and isinstance(fi, int) and fi == 0:
                    grad[l, :, cols] = term
                else:
                    grad[l, :, cols] += term
                if l > 0:
                    cosine, sine = cosines[l, f, :, cols], sines[l, f, :, cols]
                    mu_re = back_re * cosine + back_im * sine
                    mu_im = back_im * cosine - back_re * sine
                    mu = [mu_re.astype(BF16).astype(F32), mu_im.astype(BF16).astype(F32)]
                    begin_adjoint(l - 1, c, fi, cols, mu)

        if NFC > 2 and c == 0:
            grad[l] = jnp.zeros(grad.shape[1:], F32)
        loop(NFC, one)
        if c == C - 1:
            grad[l] = grad[l] * (1.0 / NF)

    def arrive(a, l):
        if l % layers == 0:
            s = lax.rem(me - l // layers + D, D)

            @pl.when(s != 0)
            def _():
                table_wait(a, s)

    def transpose(j, k):
        i = j + k - 1
        if k != 1 and not 0 <= j < nb:
            value = band_edge[0 if j < 0 else 1]
        else:
            value = band[j // G, j % G + k, :, (j % G) * B : (j % G + 1) * B]
        band_t[i // G, i % G + 2 - k, :, (i % G) * B : (i % G + 1) * B] = (
            value.astype(F32).T.astype(BF16)
        )

    for copy in local[6:]:
        copy.wait()
    for j in range(nb):
        for k in range(3):
            if 0 <= j + k - 1 < nb:
                transpose(j, k)
    local[0].wait()
    local[5].wait()
    arrive(0, 0)
    angles(0)
    local[1].wait()
    local[2].wait()
    for c in range(C):
        first_phase(c)
        send_halo(forward, 0, c)
    late_sends()
    for l in range(1, L):
        arrive(0, l)
        angles(l)
    local[3].wait()
    arrive(1, 0)
    for l in range(L):
        if l > 0:
            arrive(1, l)
        band_products(forward, band, l, R)
        if l == L - 1:
            for way in (LEFT, RIGHT):

                @pl.when(exists[way])
                def _():
                    edge_copy(opposite[way]).wait_recv()

            transpose(-1, 2)
            transpose(nb, 0)
        for c in range(C):
            forward_finish(l, c)
            if l + 1 < L:
                send_halo(forward, l + 1, c)
        if l + 1 < L:
            deliver(0, l)
    local[4].wait()
    for l in range(L):
        arrive(2, l)
    for c in range(C):
        first_adjoint(c)
        send_halo(backward, L - 1, c)
    deliver(0, L - 1)
    for l in reversed(range(L)):
        band_products(backward, band_t, l, RB)
        for c in range(C):
            backward_finish(l, c)
            if l > 0:
                send_halo(backward, l - 1, c)
        deliver(1, l)

    for l in range(L):
        for c in range(C):
            for way in DIRS:

                @pl.when(exists[way])
                def _():
                    halo_copy(*forward, l, c, way).wait_send()
                    halo_copy(*backward, l, c, way).wait_send()

    for s in range(1, D):
        for a in range(3):
            table_copy(a, s).wait_send()
    for way in (LEFT, RIGHT):

        @pl.when(exists[way])
        def _():
            edge_copy(way).wait_send()

    for a in range(2):
        for l in range(L):

            @pl.when(me == l // layers)
            def _():
                own_copy(a, l).wait()

            @pl.when(me != l // layers)
            def _():
                out_copy(a, l).wait_send()

        for i in range(layers):
            for s in range(1, D):
                source = lax.rem(me - s + D, D)
                theirs = pl.ds(pl.multiple_of(source * W, B), W)
                pltpu.make_async_remote_copy(
                    src_ref=results[a][0].at[i],
                    dst_ref=results[a][1].at[i, :, theirs],
                    send_sem=osend.at[a, i],
                    recv_sem=orecv.at[a, i, s],
                    device_id={"depth": source},
                    device_id_type=MESH,
                ).wait_recv()


def publish(image_in, grad_in, image_out, grad_out, sems):
    copies = [
        pltpu.make_async_copy(image_in, image_out, sems.at[0]),
        pltpu.make_async_copy(grad_in, grad_out, sems.at[1]),
    ]
    for copy in copies:
        copy.start()
    for copy in copies:
        copy.wait()


def per_device(source_field, receiver_field, freq_index, slowness, ffd_coef, band, image_mask):
    D, LATS = lax.axis_size("depth"), lax.axis_size("lat")
    NF, _, height, width = source_field.shape
    layers = slowness.shape[0]
    L = layers * D
    nb, _, B, _ = band.shape
    W = width // D
    assert height == HALO and W == nb * B
    C = 2 if NF % 2 == 0 else 1
    NFC = NF // C
    G = 2 if nb % 2 == 0 else 1
    dims = (D, LATS, L, layers, NF, C, nb, G, B, W)
    R, RB = NFC * 32, NFC * 16
    dma = pltpu.SemaphoreType.DMA
    anywhere = pl.BlockSpec(memory_space=pl.ANY)
    in_hbm = pl.BlockSpec(memory_space=pltpu.HBM)
    tile = (height, W)
    scratch = [
        pltpu.SMEM((NF,), jnp.int32),
        pltpu.VMEM((2, NF, 2) + tile, BF16),
        pltpu.VMEM((L,) + tile, F32),
        pltpu.VMEM((L,) + tile, F32),
        pltpu.VMEM((L,) + tile, jnp.int32),
        pltpu.VMEM((nb // G, G + 2, B, G * B), BF16),
        pltpu.VMEM((nb // G, G + 2, B, G * B), BF16),
        pltpu.VMEM((2, B, B), BF16),
        pltpu.VMEM((L, NF) + tile, F32),
        pltpu.VMEM((L, NF) + tile, F32),
        pltpu.VMEM((L, NF, 2, 2) + tile, F32),
        pltpu.VMEM((L, NF, 2) + tile, F32),
        pltpu.VMEM((NF, 2) + tile, F32),
        pltpu.VMEM((L, C, 3 * R, W + 2 * B), BF16),
        pltpu.VMEM((L, C, 3 * RB, W + 2 * B), BF16),
        pltpu.VMEM((2 * R, 3 * R), BF16),
        pltpu.VMEM((2 * RB, 3 * RB), BF16),
        pltpu.VMEM((C * R, W), F32),
        pltpu.VMEM((L,) + tile, F32),
        pltpu.VMEM((L,) + tile, F32),
        dma((L, C, 4)),
        dma((L, C, 4)),
        dma((L, C, 4)),
        dma((L, C, 4)),
        dma((3, D)),
        dma((3, D)),
        dma((2,)),
        dma((2,)),
        dma((2, L)),
        dma((2, layers, D)),
        dma((2, layers)),
        dma((6,)),
        dma((G,)),
    ]
    image, grad = pl.pallas_call(
        functools.partial(kernel, dims),
        out_shape=[pltpu.VMEM(slowness.shape, F32)] * 2,
        in_specs=[in_hbm] * 7,
        out_specs=[anywhere] * 2,
        scratch_shapes=scratch,
        compiler_params=pltpu.CompilerParams(
            collective_id=0, has_side_effects=True, vmem_limit_bytes=VMEM_BYTES
        ),
    )(freq_index, source_field, receiver_field, slowness, ffd_coef, image_mask, band.reshape(nb // G, G, 3, B, B))
    return pl.pallas_call(
        publish,
        out_shape=[jax.ShapeDtypeStruct(slowness.shape, F32)] * 2,
        in_specs=[anywhere] * 2,
        out_specs=[in_hbm] * 2,
        scratch_shapes=[dma((2,))],
        compiler_params=pltpu.CompilerParams(vmem_limit_bytes=1024 * 1024),
    )(image, grad)


def solution(mesh):
    return jax.shard_map(
        per_device,
        mesh=mesh,
        in_specs=(
            P(None, None, "lat", None),
            P(None, None, "lat", None),
            P(),
            P("depth", "lat", None),
            P("depth", "lat", None),
            P("depth", None, None, None),
            P("depth", "lat", None),
        ),
        out_specs=(P("depth", "lat", None), P("depth", "lat", None)),
        check_vma=False,
    )
```

```python
import functools

import jax
import jax.numpy as jnp
from jax import lax
from jax.experimental import pallas as pl
from jax.experimental.pallas import tpu as pltpu
from jax.sharding import PartitionSpec as P

HALO = 8
VMEM_BYTES = 64 * 1024 * 1024 - 208 * 1024
F32 = jnp.float32
BF16 = jnp.bfloat16
WEIGHTS = [0.0] + [0.25 / k for k in range(1, HALO + 1)]
UP, DOWN, LEFT, RIGHT = range(4)


def sincos(theta):
    turns = jnp.floor(theta * 0.6366197723675814 + 0.5)
    rest = theta - turns * 1.5703125
    rest = rest - turns * 4.837512969970703125e-4
    rest = rest - turns * 7.54978995489188216e-8
    square = rest * rest
    sine = rest + rest * square * (
        -1.6666654611e-1 + square * (8.3321608736e-3 + square * -1.9515295891e-4)
    )
    cosine = (
        1.0
        - 0.5 * square
        + square
        * square
        * (
            4.166664568298827e-2
            + square * (-1.388731625493765e-3 + square * 2.443315711809948e-5)
        )
    )
    quadrant = turns.astype(jnp.int32)
    odd = (quadrant & 1) == 1
    sin_out = jnp.where(odd, cosine, sine)
    cos_out = jnp.where(odd, sine, cosine)
    sin_out = jnp.where((quadrant & 2) == 2, -sin_out, sin_out)
    cos_out = jnp.where(((quadrant + 1) & 2) == 2, -cos_out, cos_out)
    return sin_out, cos_out


def stencil_matrix(rows):
    shape = (rows, 3 * rows)
    out = lax.broadcasted_iota(jnp.int32, shape, 0)
    source = lax.broadcasted_iota(jnp.int32, shape, 1)
    tile = (source >= rows).astype(jnp.int32) + (source >= 2 * rows).astype(jnp.int32) - 1
    source = source - (tile + 1) * rows
    same = (out >> 3) == (source >> 3)
    distance = jnp.abs(tile * HALO + (source & 7) - (out & 7))
    weight = jnp.where(distance == 0, -2.0 * sum(WEIGHTS), 0.0)
    for k in range(1, HALO + 1):
        weight = jnp.where(distance == k, WEIGHTS[k], weight)
    weight = jnp.where(same, weight, 0.0)
    high = weight.astype(BF16)
    return jnp.concatenate([high, (weight - high.astype(F32)).astype(BF16)], axis=0)


def loop(count, body):
    if count <= 2:
        for i in range(count):
            body(i)
    else:
        lax.fori_loop(0, count, lambda i, c: (body(i), c)[1], 0)


def kernel(
    dims,
    freq_hbm,
    src_ref,
    rcv_ref,
    slow_ref,
    coef_ref,
    mask_ref,
    band_ref,
    image_ref,
    grad_ref,
    freq_ref,
    fields,
    slow,
    coef,
    mask,
    band,
    band_t,
    band_edge,
    sines,
    cosines,
    phased,
    state,
    adj,
    hbuf,
    gbuf,
    hmat,
    gmat,
    qbuf,
    img,
    grad,
    fsend,
    frecv,
    bsend,
    brecv,
    rsend,
    rrecv,
    esend,
    erecv,
    osend,
    orecv,
    xsend,
    xrecv,
    own_sem,
    loc_sem,
    band_sem,
):
    D, LATS, L, layers, NF, C, nb, G, B, W = dims
    NFC = NF // C
    R, RB = NFC * 32, NFC * 16
    me = lax.axis_index("depth")
    lat = lax.axis_index("lat")
    first = pl.multiple_of(me * W, B)
    mine = pl.ds(first, W)
    snake = LATS == 16

    def partner_of(place):
        if not snake:
            return place
        return place + lax.rem(place // 4, 2) * (2 - 4 * lax.rem(place // 2, 2))

    partner = partner_of(lat)
    swapped = partner != lat
    stays = jnp.logical_not(swapped)
    exists = {UP: partner > 0, DOWN: partner < LATS - 1, LEFT: me > 0, RIGHT: me < D - 1}
    target = {
        UP: {"lat": partner_of(jnp.maximum(partner - 1, 0))},
        DOWN: {"lat": partner_of(jnp.minimum(partner + 1, LATS - 1))},
        LEFT: {"depth": me - 1},
        RIGHT: {"depth": me + 1},
    }
    opposite = {UP: DOWN, DOWN: UP, LEFT: RIGHT, RIGHT: LEFT}
    DIRS = (LEFT, RIGHT, UP, DOWN)
    MESH = pl.DeviceIdType.MESH

    own_levels = pl.ds(me * layers, layers)
    tables = ((slow_ref, slow), (coef_ref, coef), (mask_ref, mask))
    sources = (src_ref, rcv_ref)
    local_tables = [
        pltpu.make_async_copy(ref.at[:, :, mine], held.at[own_levels], loc_sem.at[a])
        for a, (ref, held) in enumerate(tables)
    ]
    local_fields = [
        pltpu.make_async_copy(sources[a].at[:, :, :, mine], fields.at[a], loc_sem.at[3 + a])
        for a in range(2)
    ]
    freq_copy = pltpu.make_async_copy(freq_hbm, freq_ref, loc_sem.at[5])
    band_copies = [
        pltpu.make_async_copy(
            band_ref.at[:, e], band.at[:, e : e + 3, :, e * B : (e + 1) * B], band_sem.at[e]
        )
        for e in range(G)
    ]

    @pl.when(stays)
    def _():
        for copy in local_tables + local_fields:
            copy.start()

    for copy in [freq_copy] + band_copies:
        copy.start()

    barrier = pltpu.get_barrier_semaphore()
    for way in (UP, DOWN):

        @pl.when(exists[way])
        def _():
            pl.semaphore_signal(barrier, inc=1, device_id=target[way], device_id_type=MESH)

    for s in range(1, D):
        pl.semaphore_signal(
            barrier, inc=1, device_id={"depth": lax.rem(me + s, D)}, device_id_type=MESH
        )

    @pl.when(swapped)
    def _():
        for s in range(D):
            pl.semaphore_signal(
                barrier,
                inc=1,
                device_id={"depth": lax.rem(me + s, D), "lat": partner},
                device_id_type=MESH,
            )

    for way in (UP, DOWN):

        @pl.when(jnp.logical_not(exists[way]))
        def _():
            for buf, rows in ((hbuf, R), (gbuf, RB)):
                start = 0 if way == UP else 2 * rows
                buf[:, :, start : start + rows, B : B + W] = jnp.zeros((L, C, rows, W), BF16)

    for way, start, slot in ((LEFT, 0, 0), (RIGHT, W + B, 1)):

        @pl.when(jnp.logical_not(exists[way]))
        def _():
            for buf, rows in ((hbuf, R), (gbuf, RB)):
                buf[:, :, rows : 2 * rows, start : start + B] = jnp.zeros((L, C, rows, B), BF16)
            band_edge[slot] = jnp.zeros((B, B), BF16)

    hmat[...] = stencil_matrix(R)
    gmat[...] = stencil_matrix(RB)
    for matrix in (band, band_t):
        for e in range(G):
            for r in range(G + 2):
                if not e <= r < e + 3:
                    matrix[:, r, :, e * B : (e + 1) * B] = jnp.zeros((nb // G, B, B), BF16)

    pl.semaphore_wait(
        barrier,
        (D - 1)
        + exists[UP].astype(jnp.int32)
        + exists[DOWN].astype(jnp.int32)
        + D * swapped.astype(jnp.int32),
    )

    def table_copy(a, s):
        peer = lax.rem(me + s, D)
        return pltpu.make_async_remote_copy(
            src_ref=tables[a][0].at[:, :, pl.ds(pl.multiple_of(peer * W, B), W)],
            dst_ref=tables[a][1].at[own_levels],
            send_sem=rsend.at[a, s],
            recv_sem=rrecv.at[a, s],
            device_id={"depth": peer, "lat": partner},
            device_id_type=MESH,
        )

    def table_wait(a, s):
        source = lax.rem(me - s + D, D)
        pltpu.make_async_remote_copy(
            src_ref=tables[a][1].at[pl.ds(source * layers, layers)],
            dst_ref=tables[a][1].at[pl.ds(source * layers, layers)],
            send_sem=rsend.at[a, s],
            recv_sem=rrecv.at[a, s],
            device_id={"depth": source, "lat": partner},
            device_id_type=MESH,
        ).wait_recv()

    def edge_copy(way):
        j, k, slot = (0, 0, 1) if way == LEFT else (nb - 1, 2, 0)
        return pltpu.make_async_remote_copy(
            src_ref=band_ref.at[j // G, j % G, k],
            dst_ref=band_edge.at[slot],
            send_sem=esend.at[slot],
            recv_sem=erecv.at[slot],
            device_id=target[way],
            device_id_type=MESH,
        )

    def field_copy(a, c):
        chunk = pl.ds(c * NFC, NFC)
        return pltpu.make_async_remote_copy(
            src_ref=sources[a].at[chunk, :, :, mine],
            dst_ref=fields.at[a, chunk],
            send_sem=xsend.at[a, c],
            recv_sem=xrecv.at[a, c],
            device_id={"lat": partner},
            device_id_type=MESH,
        )

    def send_table(a):
        for s in range(1, D):
            table_copy(a, s).start()
        if snake:

            @pl.when(swapped)
            def _():
                table_copy(a, 0).start()

    def send_fields(c):
        if snake:

            @pl.when(swapped)
            def _():
                for a in range(2):
                    field_copy(a, c).start()

    def wait_fields(c):
        if snake:

            @pl.when(swapped)
            def _():
                for a in range(2):
                    field_copy(a, c).wait_recv()

        if c == 0:

            @pl.when(stays)
            def _():
                for copy in local_fields:
                    copy.wait()

    send_table(0)
    send_fields(0)
    send_table(1)
    for c in range(1, C):
        send_fields(c)

    def late_sends():
        send_table(2)
        for way in (LEFT, RIGHT):

            @pl.when(exists[way])
            def _():
                edge_copy(way).start()

    def halo_copy(buf, rows, ssem, rsem, l, c, way):
        own = pl.ds(rows, rows)
        if way in (UP, DOWN):
            src = buf.at[l, c, own, pl.ds(B, W)]
            dst = buf.at[l, c, pl.ds(2 * rows if way == UP else 0, rows), pl.ds(B, W)]
        else:
            src = buf.at[l, c, own, pl.ds(B if way == LEFT else W, B)]
            dst = buf.at[l, c, own, pl.ds(W + B if way == LEFT else 0, B)]
        return pltpu.make_async_remote_copy(
            src_ref=src,
            dst_ref=dst,
            send_sem=ssem.at[l, c, way],
            recv_sem=rsem.at[l, c, opposite[way]],
            device_id=target[way],
            device_id_type=MESH,
        )

    def send_halo(args, l, c):
        for way in DIRS:

            @pl.when(exists[way])
            def _():
                halo_copy(*args, l, c, way).start()

    def wait_halo(args, l, c, ways):
        for way in ways:

            @pl.when(exists[way])
            def _():
                halo_copy(*args, l, c, opposite[way]).wait_recv()

    forward = (hbuf, R, fsend, frecv)
    backward = (gbuf, RB, bsend, brecv)

    CW = min(W, 512)
    pieces = [slice(x, x + CW) for x in range(0, W, CW)]

    def omega_of(f):
        return 0.1 * (freq_ref[f].astype(F32) + 1.0)

    def angles(l):
        def one(f):
            omega = omega_of(f)
            for cols in pieces:
                sines[l, f, :, cols], cosines[l, f, :, cols] = sincos(omega * slow[l, :, cols])

        loop(NF, one)

    def store_phase(l, c, fi, s, cols, re, im):
        f = c * NFC + fi
        cosine, sine = cosines[l, f, :, cols], sines[l, f, :, cols]
        phase_re = re * cosine - im * sine
        phase_im = re * sine + im * cosine
        phased[l, f, s, 0, :, cols] = phase_re
        phased[l, f, s, 1, :, cols] = phase_im
        rows = pl.ds(pl.multiple_of(R + (fi * 2 + s) * 16, 16), 16)
        inner = slice(cols.start + B, cols.stop + B)
        hbuf[l, c, rows, inner] = jnp.concatenate([phase_re, phase_im], axis=0).astype(BF16)

    def first_phase(c):
        def one(fi):
            f = c * NFC + fi
            for s in range(2):
                for cols in pieces:
                    re = fields[s, f, 0, :, cols].astype(F32)
                    im = fields[s, f, 1, :, cols].astype(F32)
                    store_phase(0, c, fi, s, cols, re, im)

        loop(NFC, one)

    def band_groups(buf, matrix, l, groups, rows):
        for p in groups:
            left = p * G * B
            qbuf[: C * rows, left : left + G * B] = jnp.dot(
                buf[l, :, rows : 2 * rows, left : left + (G + 2) * B].reshape(C * rows, (G + 2) * B),
                matrix[p].reshape((G + 2) * B, G * B),
                preferred_element_type=F32,
            )

    inner_groups = range(1, nb // G - 1)
    outer_groups = sorted({0, nb // G - 1})

    def band_products(args, matrix, l, rows):
        band_groups(args[0], matrix, l, inner_groups, rows)
        for c in range(C):
            wait_halo(args, l, c, (LEFT, RIGHT))
        band_groups(args[0], matrix, l, outer_groups, rows)

    def add_stencil(buf, matrix, l, c, rows):
        own = slice(c * rows, (c + 1) * rows)
        for cols in pieces:
            both = jnp.dot(
                matrix[...],
                buf[l, c, :, cols.start + B : cols.stop + B],
                preferred_element_type=F32,
            )
            qbuf[own, cols] += both[:rows] + both[rows:]

    def lateral(rows, c, row, cols):
        product = qbuf[pl.ds(pl.multiple_of(c * rows + row, 16), 16), cols]
        return product[:8], product[8:]

    def forward_finish(l, c):
        wait_halo(forward, l, c, (UP, DOWN))
        add_stencil(hbuf, hmat, l, c, R)

        def one(fi):
            f = c * NFC + fi
            for cols in pieces:
                coefs = coef[l, :, cols]
                new = []
                for s in range(2):
                    q_re, q_im = lateral(R, c, (fi * 2 + s) * 16, cols)
                    re = phased[l, f, s, 0, :, cols] - coefs * q_im
                    im = phased[l, f, s, 1, :, cols] + coefs * q_re
                    new.append((re, im))
                    if l + 1 < L:
                        store_phase(
                            l + 1,
                            c,
                            fi,
                            s,
                            cols,
                            re.astype(BF16).astype(F32),
                            im.astype(BF16).astype(F32),
                        )
                state[l, f, 0, :, cols] = new[0][0]
                state[l, f, 1, :, cols] = new[0][1]
                product = new[0][0] * new[1][0] + new[0][1] * new[1][1]
                if c == 0 and isinstance(fi, int) and fi == 0:
                    img[l, :, cols] = product
                else:
                    img[l, :, cols] += product

        if NFC > 2 and c == 0:
            img[l] = jnp.zeros(img.shape[1:], F32)
        loop(NFC, one)
        if c == C - 1:
            img[l] = img[l] * (1.0 / NF)

    results = ((img, image_ref), (grad, grad_ref))

    def own_copy(a, l):
        return pltpu.make_async_copy(
            results[a][0].at[l], results[a][1].at[l % layers, :, mine], own_sem.at[a, l % layers]
        )

    def out_copy(a, l):
        owner = l // layers
        return pltpu.make_async_remote_copy(
            src_ref=results[a][0].at[l],
            dst_ref=results[a][1].at[l % layers, :, mine],
            send_sem=osend.at[a, l],
            recv_sem=orecv.at[a, l % layers, lax.rem(owner - me + D, D)],
            device_id={"depth": owner, "lat": partner},
            device_id_type=MESH,
        )

    def deliver(a, l):
        keeps = jnp.logical_and(me == l // layers, stays)

        @pl.when(keeps)
        def _():
            own_copy(a, l).start()

        @pl.when(jnp.logical_not(keeps))
        def _():
            out_copy(a, l).start()

    def begin_adjoint(l, c, fi, cols, mu):
        f = c * NFC + fi
        weight = mask[l, :, cols].astype(F32) * img[l, :, cols]
        coefs = coef[l, :, cols]
        scaled = []
        for part in range(2):
            value = weight * state[l, f, part, :, cols]
            if mu is not None:
                value = value + mu[part]
            adj[f, part, :, cols] = value
            scaled.append(coefs * value)
        rows = pl.ds(pl.multiple_of(RB + fi * 16, 16), 16)
        gbuf[l, c, rows, cols.start + B : cols.stop + B] = jnp.concatenate(
            scaled, axis=0
        ).astype(BF16)

    def first_adjoint(c):
        def one(fi):
            for cols in pieces:
                begin_adjoint(L - 1, c, fi, cols, None)

        loop(NFC, one)

    def backward_finish(l, c):
        wait_halo(backward, l, c, (UP, DOWN))
        add_stencil(gbuf, gmat, l, c, RB)

        def one(fi):
            f = c * NFC + fi
            omega = omega_of(f)
            for cols in pieces:
                t_re, t_im = lateral(RB, c, fi * 16, cols)
                back_re = adj[f, 0, :, cols] + t_im
                back_im = adj[f, 1, :, cols] - t_re
                term = omega * (
                    back_im * phased[l, f, 1, 0, :, cols] - back_re * phased[l, f, 1, 1, :, cols]
                )
                if c == 0 and isinstance(fi, int) and fi == 0:
                    grad[l, :, cols] = term
                else:
                    grad[l, :, cols] += term
                if l > 0:
                    cosine, sine = cosines[l, f, :, cols], sines[l, f, :, cols]
                    mu_re = back_re * cosine + back_im * sine
                    mu_im = back_im * cosine - back_re * sine
                    mu = [mu_re.astype(BF16).astype(F32), mu_im.astype(BF16).astype(F32)]
                    begin_adjoint(l - 1, c, fi, cols, mu)

        if NFC > 2 and c == 0:
            grad[l] = jnp.zeros(grad.shape[1:], F32)
        loop(NFC, one)
        if c == C - 1:
            grad[l] = grad[l] * (1.0 / NF)

    def arrive(a, l):
        if l % layers == 0:
            s = lax.rem(me - l // layers + D, D)

            keeps = jnp.logical_and(s == 0, stays)

            @pl.when(keeps)
            def _():
                local_tables[a].wait()

            @pl.when(jnp.logical_not(keeps))
            def _():
                table_wait(a, s)

    def transpose(j, k):
        i = j + k - 1
        if k != 1 and not 0 <= j < nb:
            value = band_edge[0 if j < 0 else 1]
        else:
            value = band[j // G, j % G + k, :, (j % G) * B : (j % G + 1) * B]
        band_t[i // G, i % G + 2 - k, :, (i % G) * B : (i % G + 1) * B] = (
            value.astype(F32).T.astype(BF16)
        )

    for copy in band_copies:
        copy.wait()
    for j in range(nb):
        for k in range(3):
            if 0 <= j + k - 1 < nb:
                transpose(j, k)
    freq_copy.wait()
    arrive(0, 0)
    angles(0)
    for c in range(C):
        wait_fields(c)
        first_phase(c)
        send_halo(forward, 0, c)
    late_sends()
    for l in range(1, L):
        arrive(0, l)
        angles(l)
    arrive(1, 0)
    for l in range(L):
        if l > 0:
            arrive(1, l)
        band_products(forward, band, l, R)
        if l == L - 1:
            for way in (LEFT, RIGHT):

                @pl.when(exists[way])
                def _():
                    edge_copy(opposite[way]).wait_recv()

            transpose(-1, 2)
            transpose(nb, 0)
        for c in range(C):
            forward_finish(l, c)
            if l + 1 < L:
                send_halo(forward, l + 1, c)
        if l + 1 < L:
            deliver(0, l)
    for l in range(L):
        arrive(2, l)
    for c in range(C):
        first_adjoint(c)
        send_halo(backward, L - 1, c)
    deliver(0, L - 1)
    for l in reversed(range(L)):
        band_products(backward, band_t, l, RB)
        for c in range(C):
            backward_finish(l, c)
            if l > 0:
                send_halo(backward, l - 1, c)
        deliver(1, l)

    for l in range(L):
        for c in range(C):
            for way in DIRS:

                @pl.when(exists[way])
                def _():
                    halo_copy(*forward, l, c, way).wait_send()
                    halo_copy(*backward, l, c, way).wait_send()

    for s in range(1, D):
        for a in range(3):
            table_copy(a, s).wait_send()
    if snake:

        @pl.when(swapped)
        def _():
            for a in range(3):
                table_copy(a, 0).wait_send()
            for a in range(2):
                for c in range(C):
                    field_copy(a, c).wait_send()

    for way in (LEFT, RIGHT):

        @pl.when(exists[way])
        def _():
            edge_copy(way).wait_send()

    for a in range(2):
        for l in range(L):

            keeps = jnp.logical_and(me == l // layers, stays)

            @pl.when(keeps)
            def _():
                own_copy(a, l).wait()

            @pl.when(jnp.logical_not(keeps))
            def _():
                out_copy(a, l).wait_send()

        def result_wait(i, s):
            source = lax.rem(me - s + D, D)
            theirs = pl.ds(pl.multiple_of(source * W, B), W)
            pltpu.make_async_remote_copy(
                src_ref=results[a][0].at[i],
                dst_ref=results[a][1].at[i, :, theirs],
                send_sem=osend.at[a, i],
                recv_sem=orecv.at[a, i, s],
                device_id={"depth": source, "lat": partner},
                device_id_type=MESH,
            ).wait_recv()

        for i in range(layers):
            for s in range(1, D):
                result_wait(i, s)
            if snake:

                @pl.when(swapped)
                def _():
                    result_wait(i, 0)


def publish(image_in, grad_in, image_out, grad_out, sems):
    copies = [
        pltpu.make_async_copy(image_in, image_out, sems.at[0]),
        pltpu.make_async_copy(grad_in, grad_out, sems.at[1]),
    ]
    for copy in copies:
        copy.start()
    for copy in copies:
        copy.wait()


def per_device(source_field, receiver_field, freq_index, slowness, ffd_coef, band, image_mask):
    D, LATS = lax.axis_size("depth"), lax.axis_size("lat")
    NF, _, height, width = source_field.shape
    layers = slowness.shape[0]
    L = layers * D
    nb, _, B, _ = band.shape
    W = width // D
    assert height == HALO and W == nb * B
    C = 2 if NF % 2 == 0 else 1
    NFC = NF // C
    G = 2 if nb % 2 == 0 else 1
    dims = (D, LATS, L, layers, NF, C, nb, G, B, W)
    R, RB = NFC * 32, NFC * 16
    dma = pltpu.SemaphoreType.DMA
    anywhere = pl.BlockSpec(memory_space=pl.ANY)
    in_hbm = pl.BlockSpec(memory_space=pltpu.HBM)
    tile = (height, W)
    scratch = [
        pltpu.SMEM((NF,), jnp.int32),
        pltpu.VMEM((2, NF, 2) + tile, BF16),
        pltpu.VMEM((L,) + tile, F32),
        pltpu.VMEM((L,) + tile, F32),
        pltpu.VMEM((L,) + tile, jnp.int32),
        pltpu.VMEM((nb // G, G + 2, B, G * B), BF16),
        pltpu.VMEM((nb // G, G + 2, B, G * B), BF16),
        pltpu.VMEM((2, B, B), BF16),
        pltpu.VMEM((L, NF) + tile, F32),
        pltpu.VMEM((L, NF) + tile, F32),
        pltpu.VMEM((L, NF, 2, 2) + tile, F32),
        pltpu.VMEM((L, NF, 2) + tile, F32),
        pltpu.VMEM((NF, 2) + tile, F32),
        pltpu.VMEM((L, C, 3 * R, W + 2 * B), BF16),
        pltpu.VMEM((L, C, 3 * RB, W + 2 * B), BF16),
        pltpu.VMEM((2 * R, 3 * R), BF16),
        pltpu.VMEM((2 * RB, 3 * RB), BF16),
        pltpu.VMEM((C * R, W), F32),
        pltpu.VMEM((L,) + tile, F32),
        pltpu.VMEM((L,) + tile, F32),
        dma((L, C, 4)),
        dma((L, C, 4)),
        dma((L, C, 4)),
        dma((L, C, 4)),
        dma((3, D)),
        dma((3, D)),
        dma((2,)),
        dma((2,)),
        dma((2, L)),
        dma((2, layers, D)),
        dma((2, C)),
        dma((2, C)),
        dma((2, layers)),
        dma((6,)),
        dma((G,)),
    ]
    image, grad = pl.pallas_call(
        functools.partial(kernel, dims),
        out_shape=[pltpu.VMEM(slowness.shape, F32)] * 2,
        in_specs=[in_hbm] * 7,
        out_specs=[anywhere] * 2,
        scratch_shapes=scratch,
        compiler_params=pltpu.CompilerParams(
            collective_id=0, has_side_effects=True, vmem_limit_bytes=VMEM_BYTES
        ),
    )(freq_index, source_field, receiver_field, slowness, ffd_coef, image_mask, band.reshape(nb // G, G, 3, B, B))
    return pl.pallas_call(
        publish,
        out_shape=[jax.ShapeDtypeStruct(slowness.shape, F32)] * 2,
        in_specs=[anywhere] * 2,
        out_specs=[in_hbm] * 2,
        scratch_shapes=[dma((2,))],
        compiler_params=pltpu.CompilerParams(vmem_limit_bytes=1024 * 1024),
    )(image, grad)


def solution(mesh):
    return jax.shard_map(
        per_device,
        mesh=mesh,
        in_specs=(
            P(None, None, "lat", None),
            P(None, None, "lat", None),
            P(),
            P("depth", "lat", None),
            P("depth", "lat", None),
            P("depth", None, None, None),
            P("depth", "lat", None),
        ),
        out_specs=(P("depth", "lat", None), P("depth", "lat", None)),
        check_vma=False,
    )
```

```python
import functools

import jax
import jax.numpy as jnp
from jax import lax
from jax.experimental import pallas as pl
from jax.experimental.pallas import tpu as pltpu
from jax.sharding import PartitionSpec as P

HALO = 8
VMEM_BYTES = 64 * 1024 * 1024 - 208 * 1024
F32 = jnp.float32
BF16 = jnp.bfloat16
WEIGHTS = [0.0] + [0.25 / k for k in range(1, HALO + 1)]
UP, DOWN, LEFT, RIGHT = range(4)


def sincos(theta):
    turns = jnp.floor(theta * 0.6366197723675814 + 0.5)
    rest = theta - turns * 1.5703125
    rest = rest - turns * 4.837512969970703125e-4
    rest = rest - turns * 7.54978995489188216e-8
    square = rest * rest
    sine = rest + rest * square * (
        -1.6666654611e-1 + square * (8.3321608736e-3 + square * -1.9515295891e-4)
    )
    cosine = (
        1.0
        - 0.5 * square
        + square
        * square
        * (
            4.166664568298827e-2
            + square * (-1.388731625493765e-3 + square * 2.443315711809948e-5)
        )
    )
    quadrant = turns.astype(jnp.int32)
    odd = (quadrant & 1) == 1
    sin_out = jnp.where(odd, cosine, sine)
    cos_out = jnp.where(odd, sine, cosine)
    sin_out = jnp.where((quadrant & 2) == 2, -sin_out, sin_out)
    cos_out = jnp.where(((quadrant + 1) & 2) == 2, -cos_out, cos_out)
    return sin_out, cos_out


def stencil_matrix(rows):
    shape = (rows, 3 * rows)
    out = lax.broadcasted_iota(jnp.int32, shape, 0)
    source = lax.broadcasted_iota(jnp.int32, shape, 1)
    tile = (source >= rows).astype(jnp.int32) + (source >= 2 * rows).astype(jnp.int32) - 1
    source = source - (tile + 1) * rows
    same = (out >> 3) == (source >> 3)
    distance = jnp.abs(tile * HALO + (source & 7) - (out & 7))
    weight = jnp.where(distance == 0, -2.0 * sum(WEIGHTS), 0.0)
    for k in range(1, HALO + 1):
        weight = jnp.where(distance == k, WEIGHTS[k], weight)
    weight = jnp.where(same, weight, 0.0)
    high = weight.astype(BF16)
    return jnp.concatenate([high, (weight - high.astype(F32)).astype(BF16)], axis=0)


def loop(count, body):
    if count <= 2:
        for i in range(count):
            body(i)
    else:
        lax.fori_loop(0, count, lambda i, c: (body(i), c)[1], 0)


def kernel(
    dims,
    freq_hbm,
    src_ref,
    rcv_ref,
    slow_ref,
    coef_ref,
    mask_ref,
    band_ref,
    image_ref,
    grad_ref,
    freq_ref,
    fields,
    slow,
    coef,
    mask,
    band,
    band_t,
    band_edge,
    sines,
    cosines,
    phased,
    state,
    adj,
    hbuf,
    gbuf,
    hmat,
    gmat,
    qbuf,
    img,
    grad,
    fsend,
    frecv,
    bsend,
    brecv,
    rsend,
    rrecv,
    esend,
    erecv,
    osend,
    orecv,
    own_sem,
    loc_sem,
    band_sem,
):
    D, LATS, L, layers, NF, C, nb, G, B, W = dims
    NFC = NF // C
    R, RB = NFC * 32, NFC * 16
    me = lax.axis_index("depth")
    lat = lax.axis_index("lat")
    first = pl.multiple_of(me * W, B)
    mine = pl.ds(first, W)
    exists = {UP: lat > 0, DOWN: lat < LATS - 1, LEFT: me > 0, RIGHT: me < D - 1}
    target = {
        UP: {"lat": lat - 1},
        DOWN: {"lat": lat + 1},
        LEFT: {"depth": me - 1},
        RIGHT: {"depth": me + 1},
    }
    opposite = {UP: DOWN, DOWN: UP, LEFT: RIGHT, RIGHT: LEFT}
    DIRS = (LEFT, RIGHT, UP, DOWN)
    MESH = pl.DeviceIdType.MESH

    own_levels = pl.ds(me * layers, layers)
    local = [
        pltpu.make_async_copy(slow_ref.at[:, :, mine], slow.at[own_levels], loc_sem.at[0]),
        pltpu.make_async_copy(src_ref.at[:, :, :, mine], fields.at[0], loc_sem.at[1]),
        pltpu.make_async_copy(rcv_ref.at[:, :, :, mine], fields.at[1], loc_sem.at[2]),
        pltpu.make_async_copy(coef_ref.at[:, :, mine], coef.at[own_levels], loc_sem.at[3]),
        pltpu.make_async_copy(mask_ref.at[:, :, mine], mask.at[own_levels], loc_sem.at[4]),
        pltpu.make_async_copy(freq_hbm, freq_ref, loc_sem.at[5]),
    ] + [
        pltpu.make_async_copy(
            band_ref.at[:, e], band.at[:, e : e + 3, :, e * B : (e + 1) * B], band_sem.at[e]
        )
        for e in range(G)
    ]
    for copy in local:
        copy.start()

    barrier = pltpu.get_barrier_semaphore()
    for way in (UP, DOWN):

        @pl.when(exists[way])
        def _():
            pl.semaphore_signal(barrier, inc=1, device_id=target[way], device_id_type=MESH)

    for s in range(1, D):
        pl.semaphore_signal(
            barrier, inc=1, device_id={"depth": lax.rem(me + s, D)}, device_id_type=MESH
        )
    for way in (UP, DOWN):

        @pl.when(jnp.logical_not(exists[way]))
        def _():
            for buf, rows in ((hbuf, R), (gbuf, RB)):
                start = 0 if way == UP else 2 * rows
                buf[:, :, start : start + rows, B : B + W] = jnp.zeros((L, C, rows, W), BF16)

    for way, start, slot in ((LEFT, 0, 0), (RIGHT, W + B, 1)):

        @pl.when(jnp.logical_not(exists[way]))
        def _():
            for buf, rows in ((hbuf, R), (gbuf, RB)):
                buf[:, :, rows : 2 * rows, start : start + B] = jnp.zeros((L, C, rows, B), BF16)
            band_edge[slot] = jnp.zeros((B, B), BF16)

    pl.semaphore_wait(
        barrier, (D - 1) + exists[UP].astype(jnp.int32) + exists[DOWN].astype(jnp.int32)
    )

    tables = ((slow_ref, slow), (coef_ref, coef), (mask_ref, mask))

    def table_copy(a, s):
        peer = lax.rem(me + s, D)
        return pltpu.make_async_remote_copy(
            src_ref=tables[a][0].at[:, :, pl.ds(pl.multiple_of(peer * W, B), W)],
            dst_ref=tables[a][1].at[own_levels],
            send_sem=rsend.at[a, s],
            recv_sem=rrecv.at[a, s],
            device_id={"depth": peer},
            device_id_type=MESH,
        )

    def table_wait(a, s):
        source = lax.rem(me - s + D, D)
        pltpu.make_async_remote_copy(
            src_ref=tables[a][1].at[pl.ds(source * layers, layers)],
            dst_ref=tables[a][1].at[pl.ds(source * layers, layers)],
            send_sem=rsend.at[a, s],
            recv_sem=rrecv.at[a, s],
            device_id={"depth": source},
            device_id_type=MESH,
        ).wait_recv()

    def edge_copy(way):
        j, k, slot = (0, 0, 1) if way == LEFT else (nb - 1, 2, 0)
        return pltpu.make_async_remote_copy(
            src_ref=band_ref.at[j // G, j % G, k],
            dst_ref=band_edge.at[slot],
            send_sem=esend.at[slot],
            recv_sem=erecv.at[slot],
            device_id=target[way],
            device_id_type=MESH,
        )

    for a in (0, 1):
        for s in range(1, D):
            table_copy(a, s).start()

    def late_sends():
        for s in range(1, D):
            table_copy(2, s).start()
        for way in (LEFT, RIGHT):

            @pl.when(exists[way])
            def _():
                edge_copy(way).start()

    def halo_copy(buf, rows, ssem, rsem, l, c, way):
        own = pl.ds(rows, rows)
        if way in (UP, DOWN):
            src = buf.at[l, c, own, pl.ds(B, W)]
            dst = buf.at[l, c, pl.ds(2 * rows if way == UP else 0, rows), pl.ds(B, W)]
        else:
            src = buf.at[l, c, own, pl.ds(B if way == LEFT else W, B)]
            dst = buf.at[l, c, own, pl.ds(W + B if way == LEFT else 0, B)]
        return pltpu.make_async_remote_copy(
            src_ref=src,
            dst_ref=dst,
            send_sem=ssem.at[l, c, way],
            recv_sem=rsem.at[l, c, opposite[way]],
            device_id=target[way],
            device_id_type=MESH,
        )

    def send_halo(args, l, c):
        for way in DIRS:

            @pl.when(exists[way])
            def _():
                halo_copy(*args, l, c, way).start()

    def wait_halo(args, l, c, ways):
        for way in ways:

            @pl.when(exists[way])
            def _():
                halo_copy(*args, l, c, opposite[way]).wait_recv()

    forward = (hbuf, R, fsend, frecv)
    backward = (gbuf, RB, bsend, brecv)

    CW = min(W, 512)
    pieces = [slice(x, x + CW) for x in range(0, W, CW)]

    def omega_of(f):
        return 0.1 * (freq_ref[f].astype(F32) + 1.0)

    def angles(l):
        def one(f):
            omega = omega_of(f)
            for cols in pieces:
                sines[l, f, :, cols], cosines[l, f, :, cols] = sincos(omega * slow[l, :, cols])

        loop(NF, one)

    def store_phase(l, c, fi, s, cols, re, im):
        f = c * NFC + fi
        cosine, sine = cosines[l, f, :, cols], sines[l, f, :, cols]
        phase_re = re * cosine - im * sine
        phase_im = re * sine + im * cosine
        phased[l, f, s, 0, :, cols] = phase_re
        phased[l, f, s, 1, :, cols] = phase_im
        rows = pl.ds(pl.multiple_of(R + (fi * 2 + s) * 16, 16), 16)
        inner = slice(cols.start + B, cols.stop + B)
        hbuf[l, c, rows, inner] = jnp.concatenate([phase_re, phase_im], axis=0).astype(BF16)

    def first_phase(c):
        def one(fi):
            f = c * NFC + fi
            for s in range(2):
                for cols in pieces:
                    re = fields[s, f, 0, :, cols].astype(F32)
                    im = fields[s, f, 1, :, cols].astype(F32)
                    store_phase(0, c, fi, s, cols, re, im)

        loop(NFC, one)

    def band_groups(buf, matrix, l, groups, rows):
        for p in groups:
            left = p * G * B
            qbuf[: C * rows, left : left + G * B] = jnp.dot(
                buf[l, :, rows : 2 * rows, left : left + (G + 2) * B].reshape(C * rows, (G + 2) * B),
                matrix[p].reshape((G + 2) * B, G * B),
                preferred_element_type=F32,
            )

    inner_groups = range(1, nb // G - 1)
    outer_groups = sorted({0, nb // G - 1})

    def band_products(args, matrix, l, rows):
        band_groups(args[0], matrix, l, inner_groups, rows)
        for c in range(C):
            wait_halo(args, l, c, (LEFT, RIGHT))
        band_groups(args[0], matrix, l, outer_groups, rows)

    def add_stencil(buf, matrix, l, c, rows):
        own = slice(c * rows, (c + 1) * rows)
        for cols in pieces:
            both = jnp.dot(
                matrix[...],
                buf[l, c, :, cols.start + B : cols.stop + B],
                preferred_element_type=F32,
            )
            qbuf[own, cols] += both[:rows] + both[rows:]

    def lateral(rows, c, row, cols):
        product = qbuf[pl.ds(pl.multiple_of(c * rows + row, 16), 16), cols]
        return product[:8], product[8:]

    def forward_finish(l, c):
        wait_halo(forward, l, c, (UP, DOWN))
        add_stencil(hbuf, hmat, l, c, R)

        def one(fi):
            f = c * NFC + fi
            for cols in pieces:
                coefs = coef[l, :, cols]
                new = []
                for s in range(2):
                    q_re, q_im = lateral(R, c, (fi * 2 + s) * 16, cols)
                    re = phased[l, f, s, 0, :, cols] - coefs * q_im
                    im = phased[l, f, s, 1, :, cols] + coefs * q_re
                    new.append((re, im))
                    if l + 1 < L:
                        store_phase(
                            l + 1,
                            c,
                            fi,
                            s,
                            cols,
                            re.astype(BF16).astype(F32),
                            im.astype(BF16).astype(F32),
                        )
                state[l, f, 0, :, cols] = new[0][0]
                state[l, f, 1, :, cols] = new[0][1]
                product = new[0][0] * new[1][0] + new[0][1] * new[1][1]
                if c == 0 and isinstance(fi, int) and fi == 0:
                    img[l, :, cols] = product
                else:
                    img[l, :, cols] += product

        if NFC > 2 and c == 0:
            img[l] = jnp.zeros(img.shape[1:], F32)
        loop(NFC, one)
        if c == C - 1:
            img[l] = img[l] * (1.0 / NF)

    results = ((img, image_ref), (grad, grad_ref))

    def own_copy(a, l):
        return pltpu.make_async_copy(
            results[a][0].at[l], results[a][1].at[l % layers, :, mine], own_sem.at[a, l % layers]
        )

    def out_copy(a, l):
        owner = l // layers
        return pltpu.make_async_remote_copy(
            src_ref=results[a][0].at[l],
            dst_ref=results[a][1].at[l % layers, :, mine],
            send_sem=osend.at[a, l],
            recv_sem=orecv.at[a, l % layers, lax.rem(owner - me + D, D)],
            device_id={"depth": owner},
            device_id_type=MESH,
        )

    def deliver(a, l):
        @pl.when(me == l // layers)
        def _():
            own_copy(a, l).start()

        @pl.when(me != l // layers)
        def _():
            out_copy(a, l).start()

    def begin_adjoint(l, c, fi, cols, mu):
        f = c * NFC + fi
        weight = mask[l, :, cols].astype(F32) * img[l, :, cols]
        coefs = coef[l, :, cols]
        scaled = []
        for part in range(2):
            value = weight * state[l, f, part, :, cols]
            if mu is not None:
                value = value + mu[part]
            adj[f, part, :, cols] = value
            scaled.append(coefs * value)
        rows = pl.ds(pl.multiple_of(RB + fi * 16, 16), 16)
        gbuf[l, c, rows, cols.start + B : cols.stop + B] = jnp.concatenate(
            scaled, axis=0
        ).astype(BF16)

    def first_adjoint(c):
        def one(fi):
            for cols in pieces:
                begin_adjoint(L - 1, c, fi, cols, None)

        loop(NFC, one)

    def backward_finish(l, c):
        wait_halo(backward, l, c, (UP, DOWN))
        add_stencil(gbuf, gmat, l, c, RB)

        def one(fi):
            f = c * NFC + fi
            omega = omega_of(f)
            for cols in pieces:
                t_re, t_im = lateral(RB, c, fi * 16, cols)
                back_re = adj[f, 0, :, cols] + t_im
                back_im = adj[f, 1, :, cols] - t_re
                term = omega * (
                    back_im * phased[l, f, 1, 0, :, cols] - back_re * phased[l, f, 1, 1, :, cols]
                )
                if c == 0 and isinstance(fi, int) and fi == 0:
                    grad[l, :, cols] = term
                else:
                    grad[l, :, cols] += term
                if l > 0:
                    cosine, sine = cosines[l, f, :, cols], sines[l, f, :, cols]
                    mu_re = back_re * cosine + back_im * sine
                    mu_im = back_im * cosine - back_re * sine
                    mu = [mu_re.astype(BF16).astype(F32), mu_im.astype(BF16).astype(F32)]
                    begin_adjoint(l - 1, c, fi, cols, mu)

        if NFC > 2 and c == 0:
            grad[l] = jnp.zeros(grad.shape[1:], F32)
        loop(NFC, one)
        if c == C - 1:
            grad[l] = grad[l] * (1.0 / NF)

    def arrive(a, l):
        if l % layers == 0:
            s = lax.rem(me - l // layers + D, D)

            @pl.when(s != 0)
            def _():
                table_wait(a, s)

    def transpose(j, k):
        i = j + k - 1
        if k != 1 and not 0 <= j < nb:
            value = band_edge[0 if j < 0 else 1]
        else:
            value = band[j // G, j % G + k, :, (j % G) * B : (j % G + 1) * B]
        band_t[i // G, i % G + 2 - k, :, (i % G) * B : (i % G + 1) * B] = (
            value.astype(F32).T.astype(BF16)
        )

    hmat[...] = stencil_matrix(R)
    gmat[...] = stencil_matrix(RB)
    for matrix in (band, band_t):
        for e in range(G):
            for r in range(G + 2):
                if not e <= r < e + 3:
                    matrix[:, r, :, e * B : (e + 1) * B] = jnp.zeros((nb // G, B, B), BF16)
    inside = [(j, k) for j in range(nb) for k in range(3) if 0 <= j + k - 1 < nb]
    half = len(inside) // 2
    local[0].wait()
    local[5].wait()
    arrive(0, 0)
    angles(0)
    local[1].wait()
    local[2].wait()
    for c in range(C):
        first_phase(c)
        send_halo(forward, 0, c)
    late_sends()
    for l in range(1, L):
        arrive(0, l)
        angles(l)
    local[3].wait()
    arrive(1, 0)
    for copy in local[6:]:
        copy.wait()
    for l in range(L):
        if l > 0:
            arrive(1, l)
        band_products(forward, band, l, R)
        if l == 0:
            for j, k in inside[:half]:
                transpose(j, k)
        if l == L - 1:
            for way in (LEFT, RIGHT):

                @pl.when(exists[way])
                def _():
                    edge_copy(opposite[way]).wait_recv()

            for j, k in inside[half:]:
                transpose(j, k)
            transpose(-1, 2)
            transpose(nb, 0)
        for c in range(C):
            forward_finish(l, c)
            if l + 1 < L:
                send_halo(forward, l + 1, c)
        if l + 1 < L:
            deliver(0, l)
    local[4].wait()
    for l in range(L):
        arrive(2, l)
    for c in range(C):
        first_adjoint(c)
        send_halo(backward, L - 1, c)
    deliver(0, L - 1)
    for l in reversed(range(L)):
        band_products(backward, band_t, l, RB)
        for c in range(C):
            backward_finish(l, c)
            if l > 0:
                send_halo(backward, l - 1, c)
        deliver(1, l)

    for l in range(L):
        for c in range(C):
            for way in DIRS:

                @pl.when(exists[way])
                def _():
                    halo_copy(*forward, l, c, way).wait_send()
                    halo_copy(*backward, l, c, way).wait_send()

    for s in range(1, D):
        for a in range(3):
            table_copy(a, s).wait_send()
    for way in (LEFT, RIGHT):

        @pl.when(exists[way])
        def _():
            edge_copy(way).wait_send()

    for a in range(2):
        for l in range(L):

            @pl.when(me == l // layers)
            def _():
                own_copy(a, l).wait()

            @pl.when(me != l // layers)
            def _():
                out_copy(a, l).wait_send()

        for i in range(layers):
            for s in range(1, D):
                source = lax.rem(me - s + D, D)
                theirs = pl.ds(pl.multiple_of(source * W, B), W)
                pltpu.make_async_remote_copy(
                    src_ref=results[a][0].at[i],
                    dst_ref=results[a][1].at[i, :, theirs],
                    send_sem=osend.at[a, i],
                    recv_sem=orecv.at[a, i, s],
                    device_id={"depth": source},
                    device_id_type=MESH,
                ).wait_recv()


def publish(image_in, grad_in, image_out, grad_out, sems):
    copies = [
        pltpu.make_async_copy(image_in, image_out, sems.at[0]),
        pltpu.make_async_copy(grad_in, grad_out, sems.at[1]),
    ]
    for copy in copies:
        copy.start()
    for copy in copies:
        copy.wait()


def per_device(source_field, receiver_field, freq_index, slowness, ffd_coef, band, image_mask):
    D, LATS = lax.axis_size("depth"), lax.axis_size("lat")
    NF, _, height, width = source_field.shape
    layers = slowness.shape[0]
    L = layers * D
    nb, _, B, _ = band.shape
    W = width // D
    assert height == HALO and W == nb * B
    C = 2 if NF % 2 == 0 else 1
    NFC = NF // C
    G = 2 if nb % 2 == 0 else 1
    dims = (D, LATS, L, layers, NF, C, nb, G, B, W)
    R, RB = NFC * 32, NFC * 16
    dma = pltpu.SemaphoreType.DMA
    anywhere = pl.BlockSpec(memory_space=pl.ANY)
    in_hbm = pl.BlockSpec(memory_space=pltpu.HBM)
    tile = (height, W)
    scratch = [
        pltpu.SMEM((NF,), jnp.int32),
        pltpu.VMEM((2, NF, 2) + tile, BF16),
        pltpu.VMEM((L,) + tile, F32),
        pltpu.VMEM((L,) + tile, F32),
        pltpu.VMEM((L,) + tile, jnp.int32),
        pltpu.VMEM((nb // G, G + 2, B, G * B), BF16),
        pltpu.VMEM((nb // G, G + 2, B, G * B), BF16),
        pltpu.VMEM((2, B, B), BF16),
        pltpu.VMEM((L, NF) + tile, F32),
        pltpu.VMEM((L, NF) + tile, F32),
        pltpu.VMEM((L, NF, 2, 2) + tile, F32),
        pltpu.VMEM((L, NF, 2) + tile, F32),
        pltpu.VMEM((NF, 2) + tile, F32),
        pltpu.VMEM((L, C, 3 * R, W + 2 * B), BF16),
        pltpu.VMEM((L, C, 3 * RB, W + 2 * B), BF16),
        pltpu.VMEM((2 * R, 3 * R), BF16),
        pltpu.VMEM((2 * RB, 3 * RB), BF16),
        pltpu.VMEM((C * R, W), F32),
        pltpu.VMEM((L,) + tile, F32),
        pltpu.VMEM((L,) + tile, F32),
        dma((L, C, 4)),
        dma((L, C, 4)),
        dma((L, C, 4)),
        dma((L, C, 4)),
        dma((3, D)),
        dma((3, D)),
        dma((2,)),
        dma((2,)),
        dma((2, L)),
        dma((2, layers, D)),
        dma((2, layers)),
        dma((6,)),
        dma((G,)),
    ]
    image, grad = pl.pallas_call(
        functools.partial(kernel, dims),
        out_shape=[pltpu.VMEM(slowness.shape, F32)] * 2,
        in_specs=[in_hbm] * 7,
        out_specs=[anywhere] * 2,
        scratch_shapes=scratch,
        compiler_params=pltpu.CompilerParams(
            collective_id=0, has_side_effects=True, vmem_limit_bytes=VMEM_BYTES
        ),
    )(freq_index, source_field, receiver_field, slowness, ffd_coef, image_mask, band.reshape(nb // G, G, 3, B, B))
    return pl.pallas_call(
        publish,
        out_shape=[jax.ShapeDtypeStruct(slowness.shape, F32)] * 2,
        in_specs=[anywhere] * 2,
        out_specs=[in_hbm] * 2,
        scratch_shapes=[dma((2,))],
        compiler_params=pltpu.CompilerParams(vmem_limit_bytes=1024 * 1024),
    )(image, grad)


def solution(mesh):
    return jax.shard_map(
        per_device,
        mesh=mesh,
        in_specs=(
            P(None, None, "lat", None),
            P(None, None, "lat", None),
            P(),
            P("depth", "lat", None),
            P("depth", "lat", None),
            P("depth", None, None, None),
            P("depth", "lat", None),
        ),
        out_specs=(P("depth", "lat", None), P("depth", "lat", None)),
        check_vma=False,
    )
```

```python
import functools

import jax
import jax.numpy as jnp
from jax import lax
from jax.experimental import pallas as pl
from jax.experimental.pallas import tpu as pltpu
from jax.sharding import PartitionSpec as P

HALO = 8
VMEM_BYTES = 64 * 1024 * 1024 - 208 * 1024
F32 = jnp.float32
BF16 = jnp.bfloat16
WEIGHTS = [0.0] + [0.25 / k for k in range(1, HALO + 1)]
UP, DOWN, LEFT, RIGHT = range(4)


def sincos(theta):
    turns = jnp.floor(theta * 0.6366197723675814 + 0.5)
    rest = theta - turns * 1.5703125
    rest = rest - turns * 4.837512969970703125e-4
    rest = rest - turns * 7.54978995489188216e-8
    square = rest * rest
    sine = rest + rest * square * (
        -1.6666654611e-1 + square * (8.3321608736e-3 + square * -1.9515295891e-4)
    )
    cosine = (
        1.0
        - 0.5 * square
        + square
        * square
        * (
            4.166664568298827e-2
            + square * (-1.388731625493765e-3 + square * 2.443315711809948e-5)
        )
    )
    quadrant = turns.astype(jnp.int32)
    odd = (quadrant & 1) == 1
    sin_out = jnp.where(odd, cosine, sine)
    cos_out = jnp.where(odd, sine, cosine)
    sin_out = jnp.where((quadrant & 2) == 2, -sin_out, sin_out)
    cos_out = jnp.where(((quadrant + 1) & 2) == 2, -cos_out, cos_out)
    return sin_out, cos_out


def stencil_matrix(rows):
    shape = (rows, 3 * rows)
    out = lax.broadcasted_iota(jnp.int32, shape, 0)
    source = lax.broadcasted_iota(jnp.int32, shape, 1)
    tile = (source >= rows).astype(jnp.int32) + (source >= 2 * rows).astype(jnp.int32) - 1
    source = source - (tile + 1) * rows
    same = (out >> 3) == (source >> 3)
    distance = jnp.abs(tile * HALO + (source & 7) - (out & 7))
    weight = jnp.where(distance == 0, -2.0 * sum(WEIGHTS), 0.0)
    for k in range(1, HALO + 1):
        weight = jnp.where(distance == k, WEIGHTS[k], weight)
    weight = jnp.where(same, weight, 0.0)
    high = weight.astype(BF16)
    return jnp.concatenate([high, (weight - high.astype(F32)).astype(BF16)], axis=0)


def loop(count, body):
    if count <= 2:
        for i in range(count):
            body(i)
    else:
        lax.fori_loop(0, count, lambda i, c: (body(i), c)[1], 0)


def kernel(
    dims,
    freq_hbm,
    src_ref,
    rcv_ref,
    slow_ref,
    coef_ref,
    mask_ref,
    band_ref,
    image_ref,
    grad_ref,
    freq_ref,
    fields,
    slow,
    coef,
    mask,
    band,
    band_t,
    band_edge,
    sines,
    cosines,
    phased,
    state,
    adj,
    hbuf,
    gbuf,
    hmat,
    gmat,
    qbuf,
    img,
    grad,
    fsend,
    frecv,
    bsend,
    brecv,
    rsend,
    rrecv,
    esend,
    erecv,
    osend,
    orecv,
    own_sem,
    loc_sem,
    band_sem,
):
    D, LATS, L, layers, NF, C, nb, G, B, W = dims
    NFC = NF // C
    R, RB = NFC * 32, NFC * 16
    me = lax.axis_index("depth")
    lat = lax.axis_index("lat")
    first = pl.multiple_of(me * W, B)
    mine = pl.ds(first, W)
    exists = {UP: lat > 0, DOWN: lat < LATS - 1, LEFT: me > 0, RIGHT: me < D - 1}
    target = {
        UP: {"lat": lat - 1},
        DOWN: {"lat": lat + 1},
        LEFT: {"depth": me - 1},
        RIGHT: {"depth": me + 1},
    }
    opposite = {UP: DOWN, DOWN: UP, LEFT: RIGHT, RIGHT: LEFT}
    DIRS = (LEFT, RIGHT, UP, DOWN)
    MESH = pl.DeviceIdType.MESH

    own_levels = pl.ds(me * layers, layers)
    local = [
        pltpu.make_async_copy(slow_ref.at[:, :, mine], slow.at[own_levels], loc_sem.at[0]),
        pltpu.make_async_copy(src_ref.at[:, :, :, mine], fields.at[0], loc_sem.at[1]),
        pltpu.make_async_copy(rcv_ref.at[:, :, :, mine], fields.at[1], loc_sem.at[2]),
        pltpu.make_async_copy(coef_ref.at[:, :, mine], coef.at[own_levels], loc_sem.at[3]),
        pltpu.make_async_copy(mask_ref.at[:, :, mine], mask.at[own_levels], loc_sem.at[4]),
        pltpu.make_async_copy(freq_hbm, freq_ref, loc_sem.at[5]),
    ] + [
        pltpu.make_async_copy(
            band_ref.at[:, e], band.at[:, e : e + 3, :, e * B : (e + 1) * B], band_sem.at[e]
        )
        for e in range(G)
    ]
    for copy in local:
        copy.start()

    barrier = pltpu.get_barrier_semaphore()
    for way in (UP, DOWN):

        @pl.when(exists[way])
        def _():
            pl.semaphore_signal(barrier, inc=1, device_id=target[way], device_id_type=MESH)

    for s in range(1, D):
        pl.semaphore_signal(
            barrier, inc=1, device_id={"depth": lax.rem(me + s, D)}, device_id_type=MESH
        )
    for way in (UP, DOWN):

        @pl.when(jnp.logical_not(exists[way]))
        def _():
            for buf, rows in ((hbuf, R), (gbuf, RB)):
                start = 0 if way == UP else 2 * rows
                buf[:, :, start : start + rows, B : B + W] = jnp.zeros((L, C, rows, W), BF16)

    for way, start, slot in ((LEFT, 0, 0), (RIGHT, W + B, 1)):

        @pl.when(jnp.logical_not(exists[way]))
        def _():
            for buf, rows in ((hbuf, R), (gbuf, RB)):
                buf[:, :, rows : 2 * rows, start : start + B] = jnp.zeros((L, C, rows, B), BF16)
            band_edge[slot] = jnp.zeros((B, B), BF16)

    hmat[...] = stencil_matrix(R)
    gmat[...] = stencil_matrix(RB)
    for matrix in (band, band_t):
        for e in range(G):
            for r in range(G + 2):
                if not e <= r < e + 3:
                    matrix[:, r, :, e * B : (e + 1) * B] = jnp.zeros((nb // G, B, B), BF16)

    pl.semaphore_wait(
        barrier, (D - 1) + exists[UP].astype(jnp.int32) + exists[DOWN].astype(jnp.int32)
    )

    tables = ((slow_ref, slow), (coef_ref, coef), (mask_ref, mask))

    def table_copy(a, s):
        peer = lax.rem(me + s, D)
        return pltpu.make_async_remote_copy(
            src_ref=tables[a][0].at[:, :, pl.ds(pl.multiple_of(peer * W, B), W)],
            dst_ref=tables[a][1].at[own_levels],
            send_sem=rsend.at[a, s],
            recv_sem=rrecv.at[a, s],
            device_id={"depth": peer},
            device_id_type=MESH,
        )

    def table_wait(a, s):
        source = lax.rem(me - s + D, D)
        pltpu.make_async_remote_copy(
            src_ref=tables[a][1].at[pl.ds(source * layers, layers)],
            dst_ref=tables[a][1].at[pl.ds(source * layers, layers)],
            send_sem=rsend.at[a, s],
            recv_sem=rrecv.at[a, s],
            device_id={"depth": source},
            device_id_type=MESH,
        ).wait_recv()

    def edge_copy(way):
        j, k, slot = (0, 0, 1) if way == LEFT else (nb - 1, 2, 0)
        return pltpu.make_async_remote_copy(
            src_ref=band_ref.at[j // G, j % G, k],
            dst_ref=band_edge.at[slot],
            send_sem=esend.at[slot],
            recv_sem=erecv.at[slot],
            device_id=target[way],
            device_id_type=MESH,
        )

    for a in (0, 1):
        for s in range(1, D):
            table_copy(a, s).start()

    def late_sends():
        for s in range(1, D):
            table_copy(2, s).start()
        for way in (LEFT, RIGHT):

            @pl.when(exists[way])
            def _():
                edge_copy(way).start()

    def halo_copy(buf, rows, ssem, rsem, l, c, way):
        own = pl.ds(rows, rows)
        if way in (UP, DOWN):
            src = buf.at[l, c, own, pl.ds(B, W)]
            dst = buf.at[l, c, pl.ds(2 * rows if way == UP else 0, rows), pl.ds(B, W)]
        else:
            src = buf.at[l, c, own, pl.ds(B if way == LEFT else W, B)]
            dst = buf.at[l, c, own, pl.ds(W + B if way == LEFT else 0, B)]
        return pltpu.make_async_remote_copy(
            src_ref=src,
            dst_ref=dst,
            send_sem=ssem.at[l, c, way],
            recv_sem=rsem.at[l, c, opposite[way]],
            device_id=target[way],
            device_id_type=MESH,
        )

    def send_halo(args, l, c):
        for way in DIRS:

            @pl.when(exists[way])
            def _():
                halo_copy(*args, l, c, way).start()

    def wait_halo(args, l, c, ways):
        for way in ways:

            @pl.when(exists[way])
            def _():
                halo_copy(*args, l, c, opposite[way]).wait_recv()

    forward = (hbuf, R, fsend, frecv)
    backward = (gbuf, RB, bsend, brecv)

    CW = min(W, 512)
    pieces = [slice(x, x + CW) for x in range(0, W, CW)]

    def omega_of(f):
        return 0.1 * (freq_ref[f].astype(F32) + 1.0)

    def angles(l):
        def one(f):
            omega = omega_of(f)
            for cols in pieces:
                sines[l, f, :, cols], cosines[l, f, :, cols] = sincos(omega * slow[l, :, cols])

        loop(NF, one)

    def store_phase(l, c, fi, s, cols, re, im):
        f = c * NFC + fi
        cosine, sine = cosines[l, f, :, cols], sines[l, f, :, cols]
        phase_re = re * cosine - im * sine
        phase_im = re * sine + im * cosine
        phased[l, f, s, 0, :, cols] = phase_re
        phased[l, f, s, 1, :, cols] = phase_im
        rows = pl.ds(pl.multiple_of(R + (fi * 2 + s) * 16, 16), 16)
        inner = slice(cols.start + B, cols.stop + B)
        hbuf[l, c, rows, inner] = jnp.concatenate([phase_re, phase_im], axis=0).astype(BF16)

    def first_phase(c):
        def one(fi):
            f = c * NFC + fi
            for s in range(2):
                for cols in pieces:
                    re = fields[s, f, 0, :, cols].astype(F32)
                    im = fields[s, f, 1, :, cols].astype(F32)
                    store_phase(0, c, fi, s, cols, re, im)

        loop(NFC, one)

    def band_groups(buf, matrix, l, groups, rows):
        for p in groups:
            left = p * G * B
            qbuf[: C * rows, left : left + G * B] = jnp.dot(
                buf[l, :, rows : 2 * rows, left : left + (G + 2) * B].reshape(C * rows, (G + 2) * B),
                matrix[p].reshape((G + 2) * B, G * B),
                preferred_element_type=F32,
            )

    inner_groups = range(1, nb // G - 1)
    outer_groups = sorted({0, nb // G - 1})

    def band_products(args, matrix, l, rows):
        band_groups(args[0], matrix, l, inner_groups, rows)
        for c in range(C):
            wait_halo(args, l, c, (LEFT, RIGHT))
        band_groups(args[0], matrix, l, outer_groups, rows)

    def add_stencil(buf, matrix, l, c, rows):
        own = slice(c * rows, (c + 1) * rows)
        for cols in pieces:
            both = jnp.dot(
                matrix[...],
                buf[l, c, :, cols.start + B : cols.stop + B],
                preferred_element_type=F32,
            )
            qbuf[own, cols] += both[:rows] + both[rows:]

    def lateral(rows, c, row, cols):
        product = qbuf[pl.ds(pl.multiple_of(c * rows + row, 16), 16), cols]
        return product[:8], product[8:]

    def forward_finish(l, c):
        wait_halo(forward, l, c, (UP, DOWN))
        add_stencil(hbuf, hmat, l, c, R)

        def one(fi):
            f = c * NFC + fi
            for cols in pieces:
                coefs = coef[l, :, cols]
                new = []
                for s in range(2):
                    q_re, q_im = lateral(R, c, (fi * 2 + s) * 16, cols)
                    re = phased[l, f, s, 0, :, cols] - coefs * q_im
                    im = phased[l, f, s, 1, :, cols] + coefs * q_re
                    new.append((re, im))
                    if l + 1 < L:
                        store_phase(
                            l + 1,
                            c,
                            fi,
                            s,
                            cols,
                            re.astype(BF16).astype(F32),
                            im.astype(BF16).astype(F32),
                        )
                state[l, f, 0, :, cols] = new[0][0]
                state[l, f, 1, :, cols] = new[0][1]
                product = new[0][0] * new[1][0] + new[0][1] * new[1][1]
                if c == 0 and isinstance(fi, int) and fi == 0:
                    img[l, :, cols] = product
                else:
                    img[l, :, cols] += product

        if NFC > 2 and c == 0:
            img[l] = jnp.zeros(img.shape[1:], F32)
        loop(NFC, one)
        if c == C - 1:
            img[l] = img[l] * (1.0 / NF)

    results = ((img, image_ref), (grad, grad_ref))

    def own_copy(a, l):
        return pltpu.make_async_copy(
            results[a][0].at[l], results[a][1].at[l % layers, :, mine], own_sem.at[a, l % layers]
        )

    def out_copy(a, l):
        owner = l // layers
        return pltpu.make_async_remote_copy(
            src_ref=results[a][0].at[l],
            dst_ref=results[a][1].at[l % layers, :, mine],
            send_sem=osend.at[a, l],
            recv_sem=orecv.at[a, l % layers, lax.rem(owner - me + D, D)],
            device_id={"depth": owner},
            device_id_type=MESH,
        )

    def deliver(a, l):
        @pl.when(me == l // layers)
        def _():
            own_copy(a, l).start()

        @pl.when(me != l // layers)
        def _():
            out_copy(a, l).start()

    def begin_adjoint(l, c, fi, cols, mu):
        f = c * NFC + fi
        weight = mask[l, :, cols].astype(F32) * img[l, :, cols]
        coefs = coef[l, :, cols]
        scaled = []
        for part in range(2):
            value = weight * state[l, f, part, :, cols]
            if mu is not None:
                value = value + mu[part]
            adj[f, part, :, cols] = value
            scaled.append(coefs * value)
        rows = pl.ds(pl.multiple_of(RB + fi * 16, 16), 16)
        gbuf[l, c, rows, cols.start + B : cols.stop + B] = jnp.concatenate(
            scaled, axis=0
        ).astype(BF16)

    def first_adjoint(c):
        def one(fi):
            for cols in pieces:
                begin_adjoint(L - 1, c, fi, cols, None)

        loop(NFC, one)

    def backward_finish(l, c):
        wait_halo(backward, l, c, (UP, DOWN))
        add_stencil(gbuf, gmat, l, c, RB)

        def one(fi):
            f = c * NFC + fi
            omega = omega_of(f)
            for cols in pieces:
                t_re, t_im = lateral(RB, c, fi * 16, cols)
                back_re = adj[f, 0, :, cols] + t_im
                back_im = adj[f, 1, :, cols] - t_re
                term = omega * (
                    back_im * phased[l, f, 1, 0, :, cols] - back_re * phased[l, f, 1, 1, :, cols]
                )
                if c == 0 and isinstance(fi, int) and fi == 0:
                    grad[l, :, cols] = term
                else:
                    grad[l, :, cols] += term
                if l > 0:
                    cosine, sine = cosines[l, f, :, cols], sines[l, f, :, cols]
                    mu_re = back_re * cosine + back_im * sine
                    mu_im = back_im * cosine - back_re * sine
                    mu = [mu_re.astype(BF16).astype(F32), mu_im.astype(BF16).astype(F32)]
                    begin_adjoint(l - 1, c, fi, cols, mu)

        if NFC > 2 and c == 0:
            grad[l] = jnp.zeros(grad.shape[1:], F32)
        loop(NFC, one)
        if c == C - 1:
            grad[l] = grad[l] * (1.0 / NF)

    def arrive(a, l):
        if l % layers == 0:
            s = lax.rem(me - l // layers + D, D)

            @pl.when(s != 0)
            def _():
                table_wait(a, s)

    def transpose(j, k):
        i = j + k - 1
        if k != 1 and not 0 <= j < nb:
            value = band_edge[0 if j < 0 else 1]
        else:
            value = band[j // G, j % G + k, :, (j % G) * B : (j % G + 1) * B]
        band_t[i // G, i % G + 2 - k, :, (i % G) * B : (i % G + 1) * B] = (
            value.astype(F32).T.astype(BF16)
        )

    for copy in local[6:]:
        copy.wait()
    for j in range(nb):
        for k in range(3):
            if 0 <= j + k - 1 < nb:
                transpose(j, k)
    local[0].wait()
    local[5].wait()
    arrive(0, 0)
    angles(0)
    local[1].wait()
    local[2].wait()
    for c in range(C):
        first_phase(c)
        send_halo(forward, 0, c)
    late_sends()
    for l in range(1, L):
        arrive(0, l)
        angles(l)
    local[3].wait()
    arrive(1, 0)
    for l in range(L):
        if l > 0:
            arrive(1, l)
        band_products(forward, band, l, R)
        if l == L - 1:
            for way in (LEFT, RIGHT):

                @pl.when(exists[way])
                def _():
                    edge_copy(opposite[way]).wait_recv()

            transpose(-1, 2)
            transpose(nb, 0)
        for c in range(C):
            forward_finish(l, c)
            if l + 1 < L:
                send_halo(forward, l + 1, c)
        if l + 1 < L:
            deliver(0, l)
    local[4].wait()
    for l in range(L):
        arrive(2, l)
    for c in range(C):
        first_adjoint(c)
        send_halo(backward, L - 1, c)
    deliver(0, L - 1)
    for l in reversed(range(L)):
        band_products(backward, band_t, l, RB)
        for c in range(C):
            backward_finish(l, c)
            if l > 0:
                send_halo(backward, l - 1, c)
        deliver(1, l)

    for l in range(L):
        for c in range(C):
            for way in DIRS:

                @pl.when(exists[way])
                def _():
                    halo_copy(*forward, l, c, way).wait_send()
                    halo_copy(*backward, l, c, way).wait_send()

    for s in range(1, D):
        for a in range(3):
            table_copy(a, s).wait_send()
    for way in (LEFT, RIGHT):

        @pl.when(exists[way])
        def _():
            edge_copy(way).wait_send()

    for a in range(2):
        for l in range(L):

            @pl.when(me == l // layers)
            def _():
                own_copy(a, l).wait()

            @pl.when(me != l // layers)
            def _():
                out_copy(a, l).wait_send()

        for i in range(layers):
            for s in range(1, D):
                source = lax.rem(me - s + D, D)
                theirs = pl.ds(pl.multiple_of(source * W, B), W)
                pltpu.make_async_remote_copy(
                    src_ref=results[a][0].at[i],
                    dst_ref=results[a][1].at[i, :, theirs],
                    send_sem=osend.at[a, i],
                    recv_sem=orecv.at[a, i, s],
                    device_id={"depth": source},
                    device_id_type=MESH,
                ).wait_recv()


def publish(image_in, grad_in, image_out, grad_out, sems):
    copies = [
        pltpu.make_async_copy(image_in, image_out, sems.at[0]),
        pltpu.make_async_copy(grad_in, grad_out, sems.at[1]),
    ]
    for copy in copies:
        copy.start()
    for copy in copies:
        copy.wait()


def per_device(source_field, receiver_field, freq_index, slowness, ffd_coef, band, image_mask):
    D, LATS = lax.axis_size("depth"), lax.axis_size("lat")
    NF, _, height, width = source_field.shape
    layers = slowness.shape[0]
    L = layers * D
    nb, _, B, _ = band.shape
    W = width // D
    assert height == HALO and W == nb * B
    C = 1
    NFC = NF // C
    G = 2 if nb % 2 == 0 else 1
    dims = (D, LATS, L, layers, NF, C, nb, G, B, W)
    R, RB = NFC * 32, NFC * 16
    dma = pltpu.SemaphoreType.DMA
    anywhere = pl.BlockSpec(memory_space=pl.ANY)
    in_hbm = pl.BlockSpec(memory_space=pltpu.HBM)
    tile = (height, W)
    scratch = [
        pltpu.SMEM((NF,), jnp.int32),
        pltpu.VMEM((2, NF, 2) + tile, BF16),
        pltpu.VMEM((L,) + tile, F32),
        pltpu.VMEM((L,) + tile, F32),
        pltpu.VMEM((L,) + tile, jnp.int32),
        pltpu.VMEM((nb // G, G + 2, B, G * B), BF16),
        pltpu.VMEM((nb // G, G + 2, B, G * B), BF16),
        pltpu.VMEM((2, B, B), BF16),
        pltpu.VMEM((L, NF) + tile, F32),
        pltpu.VMEM((L, NF) + tile, F32),
        pltpu.VMEM((L, NF, 2, 2) + tile, F32),
        pltpu.VMEM((L, NF, 2) + tile, F32),
        pltpu.VMEM((NF, 2) + tile, F32),
        pltpu.VMEM((L, C, 3 * R, W + 2 * B), BF16),
        pltpu.VMEM((L, C, 3 * RB, W + 2 * B), BF16),
        pltpu.VMEM((2 * R, 3 * R), BF16),
        pltpu.VMEM((2 * RB, 3 * RB), BF16),
        pltpu.VMEM((C * R, W), F32),
        pltpu.VMEM((L,) + tile, F32),
        pltpu.VMEM((L,) + tile, F32),
        dma((L, C, 4)),
        dma((L, C, 4)),
        dma((L, C, 4)),
        dma((L, C, 4)),
        dma((3, D)),
        dma((3, D)),
        dma((2,)),
        dma((2,)),
        dma((2, L)),
        dma((2, layers, D)),
        dma((2, layers)),
        dma((6,)),
        dma((G,)),
    ]
    image, grad = pl.pallas_call(
        functools.partial(kernel, dims),
        out_shape=[pltpu.VMEM(slowness.shape, F32)] * 2,
        in_specs=[in_hbm] * 7,
        out_specs=[anywhere] * 2,
        scratch_shapes=scratch,
        compiler_params=pltpu.CompilerParams(
            collective_id=0, has_side_effects=True, vmem_limit_bytes=VMEM_BYTES
        ),
    )(freq_index, source_field, receiver_field, slowness, ffd_coef, image_mask, band.reshape(nb // G, G, 3, B, B))
    return pl.pallas_call(
        publish,
        out_shape=[jax.ShapeDtypeStruct(slowness.shape, F32)] * 2,
        in_specs=[anywhere] * 2,
        out_specs=[in_hbm] * 2,
        scratch_shapes=[dma((2,))],
        compiler_params=pltpu.CompilerParams(vmem_limit_bytes=1024 * 1024),
    )(image, grad)


def solution(mesh):
    return jax.shard_map(
        per_device,
        mesh=mesh,
        in_specs=(
            P(None, None, "lat", None),
            P(None, None, "lat", None),
            P(),
            P("depth", "lat", None),
            P("depth", "lat", None),
            P("depth", None, None, None),
            P("depth", "lat", None),
        ),
        out_specs=(P("depth", "lat", None), P("depth", "lat", None)),
        check_vma=False,
    )
```

```python
import functools

import jax
import jax.numpy as jnp
from jax import lax
from jax.experimental import pallas as pl
from jax.experimental.pallas import tpu as pltpu
from jax.sharding import PartitionSpec as P

HALO = 8
VMEM_BYTES = 64 * 1024 * 1024 - 208 * 1024
F32 = jnp.float32
BF16 = jnp.bfloat16
WEIGHTS = [0.0] + [0.25 / k for k in range(1, HALO + 1)]
UP, DOWN, LEFT, RIGHT = range(4)


def sincos(theta):
    turns = jnp.floor(theta * 0.6366197723675814 + 0.5)
    rest = theta - turns * 1.5703125
    rest = rest - turns * 4.837512969970703125e-4
    rest = rest - turns * 7.54978995489188216e-8
    square = rest * rest
    sine = rest + rest * square * (
        -1.6666654611e-1 + square * (8.3321608736e-3 + square * -1.9515295891e-4)
    )
    cosine = (
        1.0
        - 0.5 * square
        + square
        * square
        * (
            4.166664568298827e-2
            + square * (-1.388731625493765e-3 + square * 2.443315711809948e-5)
        )
    )
    quadrant = turns.astype(jnp.int32)
    odd = (quadrant & 1) == 1
    sin_out = jnp.where(odd, cosine, sine)
    cos_out = jnp.where(odd, sine, cosine)
    sin_out = jnp.where((quadrant & 2) == 2, -sin_out, sin_out)
    cos_out = jnp.where(((quadrant + 1) & 2) == 2, -cos_out, cos_out)
    return sin_out, cos_out


def stencil_matrix(rows):
    shape = (rows, 3 * rows)
    out = lax.broadcasted_iota(jnp.int32, shape, 0)
    source = lax.broadcasted_iota(jnp.int32, shape, 1)
    tile = (source >= rows).astype(jnp.int32) + (source >= 2 * rows).astype(jnp.int32) - 1
    source = source - (tile + 1) * rows
    same = (out >> 3) == (source >> 3)
    distance = jnp.abs(tile * HALO + (source & 7) - (out & 7))
    weight = jnp.where(distance == 0, -2.0 * sum(WEIGHTS), 0.0)
    for k in range(1, HALO + 1):
        weight = jnp.where(distance == k, WEIGHTS[k], weight)
    weight = jnp.where(same, weight, 0.0)
    high = weight.astype(BF16)
    return jnp.concatenate([high, (weight - high.astype(F32)).astype(BF16)], axis=0)


def loop(count, body):
    if count <= 2:
        for i in range(count):
            body(i)
    else:
        lax.fori_loop(0, count, lambda i, c: (body(i), c)[1], 0)


def kernel(
    dims,
    freq_hbm,
    src_ref,
    rcv_ref,
    slow_ref,
    coef_ref,
    mask_ref,
    band_ref,
    image_ref,
    grad_ref,
    freq_ref,
    fields,
    slow,
    coef,
    mask,
    band,
    band_t,
    band_edge,
    sines,
    cosines,
    phased,
    state,
    adj,
    hbuf,
    gbuf,
    hmat,
    gmat,
    qbuf,
    img,
    grad,
    fsend,
    frecv,
    bsend,
    brecv,
    rsend,
    rrecv,
    esend,
    erecv,
    osend,
    orecv,
    own_sem,
    loc_sem,
    band_sem,
):
    D, LATS, L, layers, NF, C, nb, G, B, W = dims
    NFC = NF // C
    R, RB = NFC * 32, NFC * 16
    me = lax.axis_index("depth")
    lat = lax.axis_index("lat")
    first = pl.multiple_of(me * W, B)
    mine = pl.ds(first, W)
    exists = {UP: lat > 0, DOWN: lat < LATS - 1, LEFT: me > 0, RIGHT: me < D - 1}
    target = {
        UP: {"lat": lat - 1},
        DOWN: {"lat": lat + 1},
        LEFT: {"depth": me - 1},
        RIGHT: {"depth": me + 1},
    }
    opposite = {UP: DOWN, DOWN: UP, LEFT: RIGHT, RIGHT: LEFT}
    DIRS = (UP, DOWN, LEFT, RIGHT)
    MESH = pl.DeviceIdType.MESH

    own_levels = pl.ds(me * layers, layers)
    local = [
        pltpu.make_async_copy(slow_ref.at[:, :, mine], slow.at[own_levels], loc_sem.at[0]),
        pltpu.make_async_copy(src_ref.at[:, :, :, mine], fields.at[0], loc_sem.at[1]),
        pltpu.make_async_copy(rcv_ref.at[:, :, :, mine], fields.at[1], loc_sem.at[2]),
        pltpu.make_async_copy(coef_ref.at[:, :, mine], coef.at[own_levels], loc_sem.at[3]),
        pltpu.make_async_copy(mask_ref.at[:, :, mine], mask.at[own_levels], loc_sem.at[4]),
        pltpu.make_async_copy(freq_hbm, freq_ref, loc_sem.at[5]),
    ] + [
        pltpu.make_async_copy(
            band_ref.at[:, e], band.at[:, e : e + 3, :, e * B : (e + 1) * B], band_sem.at[e]
        )
        for e in range(G)
    ]
    for copy in local:
        copy.start()

    barrier = pltpu.get_barrier_semaphore()
    for way in (UP, DOWN):

        @pl.when(exists[way])
        def _():
            pl.semaphore_signal(barrier, inc=1, device_id=target[way], device_id_type=MESH)

    for s in range(1, D):
        pl.semaphore_signal(
            barrier, inc=1, device_id={"depth": lax.rem(me + s, D)}, device_id_type=MESH
        )
    for way in (UP, DOWN):

        @pl.when(jnp.logical_not(exists[way]))
        def _():
            for buf, rows in ((hbuf, R), (gbuf, RB)):
                start = 0 if way == UP else 2 * rows
                buf[:, :, start : start + rows, B : B + W] = jnp.zeros((L, C, rows, W), BF16)

    for way, start, slot in ((LEFT, 0, 0), (RIGHT, W + B, 1)):

        @pl.when(jnp.logical_not(exists[way]))
        def _():
            for buf, rows in ((hbuf, R), (gbuf, RB)):
                buf[:, :, rows : 2 * rows, start : start + B] = jnp.zeros((L, C, rows, B), BF16)
            band_edge[slot] = jnp.zeros((B, B), BF16)

    hmat[...] = stencil_matrix(R)
    gmat[...] = stencil_matrix(RB)
    for matrix in (band, band_t):
        for e in range(G):
            for r in range(G + 2):
                if not e <= r < e + 3:
                    matrix[:, r, :, e * B : (e + 1) * B] = jnp.zeros((nb // G, B, B), BF16)

    pl.semaphore_wait(
        barrier, (D - 1) + exists[UP].astype(jnp.int32) + exists[DOWN].astype(jnp.int32)
    )

    tables = ((slow_ref, slow), (coef_ref, coef), (mask_ref, mask))

    def table_copy(a, s):
        peer = lax.rem(me + s, D)
        return pltpu.make_async_remote_copy(
            src_ref=tables[a][0].at[:, :, pl.ds(pl.multiple_of(peer * W, B), W)],
            dst_ref=tables[a][1].at[own_levels],
            send_sem=rsend.at[a, s],
            recv_sem=rrecv.at[a, s],
            device_id={"depth": peer},
            device_id_type=MESH,
        )

    def table_wait(a, s):
        source = lax.rem(me - s + D, D)
        pltpu.make_async_remote_copy(
            src_ref=tables[a][1].at[pl.ds(source * layers, layers)],
            dst_ref=tables[a][1].at[pl.ds(source * layers, layers)],
            send_sem=rsend.at[a, s],
            recv_sem=rrecv.at[a, s],
            device_id={"depth": source},
            device_id_type=MESH,
        ).wait_recv()

    def edge_copy(way):
        j, k, slot = (0, 0, 1) if way == LEFT else (nb - 1, 2, 0)
        return pltpu.make_async_remote_copy(
            src_ref=band_ref.at[j // G, j % G, k],
            dst_ref=band_edge.at[slot],
            send_sem=esend.at[slot],
            recv_sem=erecv.at[slot],
            device_id=target[way],
            device_id_type=MESH,
        )

    for s in range(1, D):
        table_copy(0, s).start()

    def late_sends():
        for a in (1, 2):
            for s in range(1, D):
                table_copy(a, s).start()
        for way in (LEFT, RIGHT):

            @pl.when(exists[way])
            def _():
                edge_copy(way).start()

    def halo_copy(buf, rows, ssem, rsem, l, c, way):
        own = pl.ds(rows, rows)
        if way in (UP, DOWN):
            src = buf.at[l, c, own, pl.ds(B, W)]
            dst = buf.at[l, c, pl.ds(2 * rows if way == UP else 0, rows), pl.ds(B, W)]
        else:
            src = buf.at[l, c, own, pl.ds(B if way == LEFT else W, B)]
            dst = buf.at[l, c, own, pl.ds(W + B if way == LEFT else 0, B)]
        return pltpu.make_async_remote_copy(
            src_ref=src,
            dst_ref=dst,
            send_sem=ssem.at[l, c, way],
            recv_sem=rsem.at[l, c, opposite[way]],
            device_id=target[way],
            device_id_type=MESH,
        )

    def send_halo(args, l, c):
        for way in DIRS:

            @pl.when(exists[way])
            def _():
                halo_copy(*args, l, c, way).start()

    def wait_halo(args, l, c, ways):
        for way in ways:

            @pl.when(exists[way])
            def _():
                halo_copy(*args, l, c, opposite[way]).wait_recv()

    forward = (hbuf, R, fsend, frecv)
    backward = (gbuf, RB, bsend, brecv)

    CW = min(W, 512)
    pieces = [slice(x, x + CW) for x in range(0, W, CW)]

    def omega_of(f):
        return 0.1 * (freq_ref[f].astype(F32) + 1.0)

    def angles(l):
        def one(f):
            omega = omega_of(f)
            for cols in pieces:
                sines[l, f, :, cols], cosines[l, f, :, cols] = sincos(omega * slow[l, :, cols])

        loop(NF, one)

    def store_phase(l, c, fi, s, cols, re, im):
        f = c * NFC + fi
        cosine, sine = cosines[l, f, :, cols], sines[l, f, :, cols]
        phase_re = re * cosine - im * sine
        phase_im = re * sine + im * cosine
        phased[l, f, s, 0, :, cols] = phase_re
        phased[l, f, s, 1, :, cols] = phase_im
        rows = pl.ds(pl.multiple_of(R + (fi * 2 + s) * 16, 16), 16)
        inner = slice(cols.start + B, cols.stop + B)
        hbuf[l, c, rows, inner] = jnp.concatenate([phase_re, phase_im], axis=0).astype(BF16)

    def first_phase(c):
        def one(fi):
            f = c * NFC + fi
            for s in range(2):
                for cols in pieces:
                    re = fields[s, f, 0, :, cols].astype(F32)
                    im = fields[s, f, 1, :, cols].astype(F32)
                    store_phase(0, c, fi, s, cols, re, im)

        loop(NFC, one)

    def band_groups(buf, matrix, l, groups, rows):
        for p in groups:
            left = p * G * B
            qbuf[: C * rows, left : left + G * B] = jnp.dot(
                buf[l, :, rows : 2 * rows, left : left + (G + 2) * B].reshape(C * rows, (G + 2) * B),
                matrix[p].reshape((G + 2) * B, G * B),
                preferred_element_type=F32,
            )

    inner_groups = range(1, nb // G - 1)
    outer_groups = sorted({0, nb // G - 1})

    def band_products(args, matrix, l, rows):
        band_groups(args[0], matrix, l, inner_groups, rows)
        for c in range(C):
            wait_halo(args, l, c, (LEFT, RIGHT))
        band_groups(args[0], matrix, l, outer_groups, rows)

    def add_stencil(buf, matrix, l, c, rows):
        own = slice(c * rows, (c + 1) * rows)
        for cols in pieces:
            both = jnp.dot(
                matrix[...],
                buf[l, c, :, cols.start + B : cols.stop + B],
                preferred_element_type=F32,
            )
            qbuf[own, cols] += both[:rows] + both[rows:]

    def lateral(rows, c, row, cols):
        product = qbuf[pl.ds(pl.multiple_of(c * rows + row, 16), 16), cols]
        return product[:8], product[8:]

    def forward_finish(l, c):
        wait_halo(forward, l, c, (UP, DOWN))
        add_stencil(hbuf, hmat, l, c, R)

        def one(fi):
            f = c * NFC + fi
            for cols in pieces:
                coefs = coef[l, :, cols]
                new = []
                for s in range(2):
                    q_re, q_im = lateral(R, c, (fi * 2 + s) * 16, cols)
                    re = phased[l, f, s, 0, :, cols] - coefs * q_im
                    im = phased[l, f, s, 1, :, cols] + coefs * q_re
                    new.append((re, im))
                    if l + 1 < L:
                        store_phase(
                            l + 1,
                            c,
                            fi,
                            s,
                            cols,
                            re.astype(BF16).astype(F32),
                            im.astype(BF16).astype(F32),
                        )
                state[l, f, 0, :, cols] = new[0][0]
                state[l, f, 1, :, cols] = new[0][1]
                product = new[0][0] * new[1][0] + new[0][1] * new[1][1]
                if c == 0 and isinstance(fi, int) and fi == 0:
                    img[l, :, cols] = product
                else:
                    img[l, :, cols] += product

        if NFC > 2 and c == 0:
            img[l] = jnp.zeros(img.shape[1:], F32)
        loop(NFC, one)
        if c == C - 1:
            img[l] = img[l] * (1.0 / NF)

    results = ((img, image_ref), (grad, grad_ref))

    def own_copy(a, l):
        return pltpu.make_async_copy(
            results[a][0].at[l], results[a][1].at[l % layers, :, mine], own_sem.at[a, l % layers]
        )

    def out_copy(a, l):
        owner = l // layers
        return pltpu.make_async_remote_copy(
            src_ref=results[a][0].at[l],
            dst_ref=results[a][1].at[l % layers, :, mine],
            send_sem=osend.at[a, l],
            recv_sem=orecv.at[a, l % layers, lax.rem(owner - me + D, D)],
            device_id={"depth": owner},
            device_id_type=MESH,
        )

    def deliver(a, l):
        @pl.when(me == l // layers)
        def _():
            own_copy(a, l).start()

        @pl.when(me != l // layers)
        def _():
            out_copy(a, l).start()

    def begin_adjoint(l, c, fi, cols, mu):
        f = c * NFC + fi
        weight = mask[l, :, cols].astype(F32) * img[l, :, cols]
        coefs = coef[l, :, cols]
        scaled = []
        for part in range(2):
            value = weight * state[l, f, part, :, cols]
            if mu is not None:
                value = value + mu[part]
            adj[f, part, :, cols] = value
            scaled.append(coefs * value)
        rows = pl.ds(pl.multiple_of(RB + fi * 16, 16), 16)
        gbuf[l, c, rows, cols.start + B : cols.stop + B] = jnp.concatenate(
            scaled, axis=0
        ).astype(BF16)

    def first_adjoint(c):
        def one(fi):
            for cols in pieces:
                begin_adjoint(L - 1, c, fi, cols, None)

        loop(NFC, one)

    def backward_finish(l, c):
        wait_halo(backward, l, c, (UP, DOWN))
        add_stencil(gbuf, gmat, l, c, RB)

        def one(fi):
            f = c * NFC + fi
            omega = omega_of(f)
            for cols in pieces:
                t_re, t_im = lateral(RB, c, fi * 16, cols)
                back_re = adj[f, 0, :, cols] + t_im
                back_im = adj[f, 1, :, cols] - t_re
                term = omega * (
                    back_im * phased[l, f, 1, 0, :, cols] - back_re * phased[l, f, 1, 1, :, cols]
                )
                if c == 0 and isinstance(fi, int) and fi == 0:
                    grad[l, :, cols] = term
                else:
                    grad[l, :, cols] += term
                if l > 0:
                    cosine, sine = cosines[l, f, :, cols], sines[l, f, :, cols]
                    mu_re = back_re * cosine + back_im * sine
                    mu_im = back_im * cosine - back_re * sine
                    mu = [mu_re.astype(BF16).astype(F32), mu_im.astype(BF16).astype(F32)]
                    begin_adjoint(l - 1, c, fi, cols, mu)

        if NFC > 2 and c == 0:
            grad[l] = jnp.zeros(grad.shape[1:], F32)
        loop(NFC, one)
        if c == C - 1:
            grad[l] = grad[l] * (1.0 / NF)

    def arrive(a, l):
        if l % layers == 0:
            s = lax.rem(me - l // layers + D, D)

            @pl.when(s != 0)
            def _():
                table_wait(a, s)

    def transpose(j, k):
        i = j + k - 1
        if k != 1 and not 0 <= j < nb:
            value = band_edge[0 if j < 0 else 1]
        else:
            value = band[j // G, j % G + k, :, (j % G) * B : (j % G + 1) * B]
        band_t[i // G, i % G + 2 - k, :, (i % G) * B : (i % G + 1) * B] = (
            value.astype(F32).T.astype(BF16)
        )

    for copy in local[6:]:
        copy.wait()
    for j in range(nb):
        for k in range(3):
            if 0 <= j + k - 1 < nb:
                transpose(j, k)
    local[0].wait()
    local[5].wait()
    arrive(0, 0)
    angles(0)
    local[1].wait()
    local[2].wait()
    for c in range(C):
        first_phase(c)
        send_halo(forward, 0, c)
    late_sends()
    for l in range(1, L):
        arrive(0, l)
        angles(l)
    local[3].wait()
    arrive(1, 0)
    for l in range(L):
        if l > 0:
            arrive(1, l)
        band_products(forward, band, l, R)
        if l == L - 1:
            for way in (LEFT, RIGHT):

                @pl.when(exists[way])
                def _():
                    edge_copy(opposite[way]).wait_recv()

            transpose(-1, 2)
            transpose(nb, 0)
        for c in range(C):
            forward_finish(l, c)
            if l + 1 < L:
                send_halo(forward, l + 1, c)
        if l + 1 < L:
            deliver(0, l)
    local[4].wait()
    for l in range(L):
        arrive(2, l)
    for c in range(C):
        first_adjoint(c)
        send_halo(backward, L - 1, c)
    deliver(0, L - 1)
    for l in reversed(range(L)):
        band_products(backward, band_t, l, RB)
        for c in range(C):
            backward_finish(l, c)
            if l > 0:
                send_halo(backward, l - 1, c)
        deliver(1, l)

    for l in range(L):
        for c in range(C):
            for way in DIRS:

                @pl.when(exists[way])
                def _():
                    halo_copy(*forward, l, c, way).wait_send()
                    halo_copy(*backward, l, c, way).wait_send()

    for s in range(1, D):
        for a in range(3):
            table_copy(a, s).wait_send()
    for way in (LEFT, RIGHT):

        @pl.when(exists[way])
        def _():
            edge_copy(way).wait_send()

    for a in range(2):
        for l in range(L):

            @pl.when(me == l // layers)
            def _():
                own_copy(a, l).wait()

            @pl.when(me != l // layers)
            def _():
                out_copy(a, l).wait_send()

        for i in range(layers):
            for s in range(1, D):
                source = lax.rem(me - s + D, D)
                theirs = pl.ds(pl.multiple_of(source * W, B), W)
                pltpu.make_async_remote_copy(
                    src_ref=results[a][0].at[i],
                    dst_ref=results[a][1].at[i, :, theirs],
                    send_sem=osend.at[a, i],
                    recv_sem=orecv.at[a, i, s],
                    device_id={"depth": source},
                    device_id_type=MESH,
                ).wait_recv()


def publish(image_in, grad_in, image_out, grad_out, sems):
    copies = [
        pltpu.make_async_copy(image_in, image_out, sems.at[0]),
        pltpu.make_async_copy(grad_in, grad_out, sems.at[1]),
    ]
    for copy in copies:
        copy.start()
    for copy in copies:
        copy.wait()


def per_device(source_field, receiver_field, freq_index, slowness, ffd_coef, band, image_mask):
    D, LATS = lax.axis_size("depth"), lax.axis_size("lat")
    NF, _, height, width = source_field.shape
    layers = slowness.shape[0]
    L = layers * D
    nb, _, B, _ = band.shape
    W = width // D
    assert height == HALO and W == nb * B
    C = 2 if NF % 2 == 0 else 1
    NFC = NF // C
    G = 2 if nb % 2 == 0 else 1
    dims = (D, LATS, L, layers, NF, C, nb, G, B, W)
    R, RB = NFC * 32, NFC * 16
    dma = pltpu.SemaphoreType.DMA
    anywhere = pl.BlockSpec(memory_space=pl.ANY)
    in_hbm = pl.BlockSpec(memory_space=pltpu.HBM)
    tile = (height, W)
    scratch = [
        pltpu.SMEM((NF,), jnp.int32),
        pltpu.VMEM((2, NF, 2) + tile, BF16),
        pltpu.VMEM((L,) + tile, F32),
        pltpu.VMEM((L,) + tile, F32),
        pltpu.VMEM((L,) + tile, jnp.int32),
        pltpu.VMEM((nb // G, G + 2, B, G * B), BF16),
        pltpu.VMEM((nb // G, G + 2, B, G * B), BF16),
        pltpu.VMEM((2, B, B), BF16),
        pltpu.VMEM((L, NF) + tile, F32),
        pltpu.VMEM((L, NF) + tile, F32),
        pltpu.VMEM((L, NF, 2, 2) + tile, F32),
        pltpu.VMEM((L, NF, 2) + tile, F32),
        pltpu.VMEM((NF, 2) + tile, F32),
        pltpu.VMEM((L, C, 3 * R, W + 2 * B), BF16),
        pltpu.VMEM((L, C, 3 * RB, W + 2 * B), BF16),
        pltpu.VMEM((2 * R, 3 * R), BF16),
        pltpu.VMEM((2 * RB, 3 * RB), BF16),
        pltpu.VMEM((C * R, W), F32),
        pltpu.VMEM((L,) + tile, F32),
        pltpu.VMEM((L,) + tile, F32),
        dma((L, C, 4)),
        dma((L, C, 4)),
        dma((L, C, 4)),
        dma((L, C, 4)),
        dma((3, D)),
        dma((3, D)),
        dma((2,)),
        dma((2,)),
        dma((2, L)),
        dma((2, layers, D)),
        dma((2, layers)),
        dma((6,)),
        dma((G,)),
    ]
    image, grad = pl.pallas_call(
        functools.partial(kernel, dims),
        out_shape=[pltpu.VMEM(slowness.shape, F32)] * 2,
        in_specs=[in_hbm] * 7,
        out_specs=[anywhere] * 2,
        scratch_shapes=scratch,
        compiler_params=pltpu.CompilerParams(
            collective_id=0, has_side_effects=True, vmem_limit_bytes=VMEM_BYTES
        ),
    )(freq_index, source_field, receiver_field, slowness, ffd_coef, image_mask, band.reshape(nb // G, G, 3, B, B))
    return pl.pallas_call(
        publish,
        out_shape=[jax.ShapeDtypeStruct(slowness.shape, F32)] * 2,
        in_specs=[anywhere] * 2,
        out_specs=[in_hbm] * 2,
        scratch_shapes=[dma((2,))],
        compiler_params=pltpu.CompilerParams(vmem_limit_bytes=1024 * 1024),
    )(image, grad)


def solution(mesh):
    return jax.shard_map(
        per_device,
        mesh=mesh,
        in_specs=(
            P(None, None, "lat", None),
            P(None, None, "lat", None),
            P(),
            P("depth", "lat", None),
            P("depth", "lat", None),
            P("depth", None, None, None),
            P("depth", "lat", None),
        ),
        out_specs=(P("depth", "lat", None), P("depth", "lat", None)),
        check_vma=False,
    )
```
